128 devices in a mesh: row: 16 (over z, x_hi, core), col: 8 (over x_lo, y).
Axes of the slice: x: 4 (x_hi: 2, x_lo: 2; x = x_hi * 2 + x_lo), y: 4, z: 4, core: 2. Of those that a mesh axis runs over, the one named last changes fastest.
Arguments:
- codes: int32 [512, 512], P('row', 'col'), may hold values from 0 to 511
- starts: int32 [512], replicated, may hold values from 0 to 511, as said below
- embed: bfloat16 [512, 512], replicated, may hold values from -6 to 6
- gain_one: float32 [512], replicated, may hold values from 0.1 to 1.9
- row_qkv: bfloat16 [512, 1536], replicated, may hold values from -2 to 2
- row_out: bfloat16 [512, 512], replicated, may hold values from -0.25 to 0.25
- gain_two: float32 [512], replicated, may hold values from 0.1 to 1.9
- col_qkv: bfloat16 [512, 640], replicated, may hold values from -2 to 2
- col_out: bfloat16 [512, 512], replicated, may hold values from -0.25 to 0.25
- gain_three: float32 [512], replicated, may hold values from 0.1 to 1.9
- mlp_in: bfloat16 [512, 1024], replicated, may hold values from -0.25 to 0.25
- mlp_out: bfloat16 [1024, 512], replicated, may hold values from -0.1875 to 0.1875
- project: bfloat16 [512, 128], replicated, may hold values from -0.25 to 0.25
- conv_one: bfloat16 [3, 3, 128, 128], replicated, may hold values from -0.1875 to 0.1875
- conv_two: bfloat16 [3, 3, 128, 128], replicated, may hold values from -0.1875 to 0.1875
Outputs:
- block_out: float32 [512, 512, 512], P('row', 'col')
- image: float32 [1024, 1024, 128], P('row', 'col')
The draws below stay inside these ranges and needn't reach their ends.
Inputs may be any that keep to these rules, and one draw needn't show every extreme that they name: starts[i] is at most i.
All inputs are finite; a program needn't handle non-finite values.
Results may differ from the reference program's by a relative error of at most 0.013.
The reference program's roundings to bfloat16 on the way count: a program that leaves them out, or rounds other values in their place, can miss the bound.
Values may be sent and summed in bfloat16 or wider, within the bound.
A program may use at most 192 MiB of HBM per device.

```python
import math
import jax
import jax.numpy as jnp
import numpy as np
from jax import lax

D = 512
HEADS = 8
FF = 1024
VOCAB = 512
CW = 128
COL_DEV = 64
HD = 64
NR = 512
NC = 512


def draw_starts(key, part):
    limits = jnp.arange(NR, dtype=jnp.int32) + 1
    return jax.random.randint(key, (NR,), 0, limits, dtype=jnp.int32)


def draw_row_qkv(key, part):
    key_q, key_k, key_v = jax.random.split(key, 3)
    scale = D ** (-0.5)
    base_q = jax.random.normal(key_q, (D, D), jnp.float32) * scale
    base_k = jax.random.normal(key_k, (D, D), jnp.float32) * scale
    base_v = jax.random.normal(key_v, (D, D), jnp.float32) * scale
    queries = base_q
    keys = base_k
    return jnp.clip(jnp.concatenate([queries, keys, base_v], axis=1), -2.0, 2.0).astype(jnp.bfloat16)


def draw_col_qkv(key, part):
    key_q, key_k, key_v = jax.random.split(jax.random.fold_in(key, 7), 3)
    scale = D ** (-0.5)
    base_q = jax.random.normal(key_q, (D, D), jnp.float32) * scale
    base_k = jax.random.normal(key_k, (D, HD), jnp.float32) * scale
    base_v = jax.random.normal(key_v, (D, HD), jnp.float32) * scale
    queries = base_q
    keys = base_k
    return jnp.clip(jnp.concatenate([queries, keys, base_v], axis=1), -2.0, 2.0).astype(jnp.bfloat16)


def with_ends(values, own_key, least, top_value):
    longest = values.shape.index(max(values.shape))
    spots = []
    for shift in (0, 1):
        where = [jax.random.randint(jax.random.fold_in(own_key, axis), (), 0, length) for axis, length in enumerate(values.shape)]
        where[longest] = (where[longest] + shift) % values.shape[longest]
        spots.append(tuple(where))
    return values.at[spots[0]].set(least).at[spots[1]].set(top_value)


def cumulative_ranks(number_of, skew):
    loads = [(1 << 20) // math.isqrt(rank ** skew) + 1 for rank in range(1, number_of + 1)]
    spread = 1 + sum(loads) // (1 << 30)
    return np.cumsum(np.array([max(1, weight // spread) for weight in loads]))


def skewed_ids(stream_key, extent, count, lean):
    table = cumulative_ranks(count, lean)
    pick = jax.random.randint(jax.random.fold_in(stream_key, 1), extent, 0, int(table[count - 1]))
    rank = jnp.searchsorted(jnp.asarray(table, jnp.int32), pick, side="right")
    return jax.random.permutation(jax.random.fold_in(stream_key, 2), count)[rank].astype(jnp.int32)


def normal_values(rng, extent, spread, reach, kind=jnp.bfloat16):
    values = spread * jax.random.normal(rng, extent, jnp.float32)
    return jnp.clip(values, min=-reach, max=reach).astype(kind)


def setup_inputs(seed: int = 0) -> dict:
    seeds = jax.random.split(jax.random.key(seed), 16)
    return {
        "codes": with_ends(skewed_ids(seeds[0], (NR, NC), VOCAB, 1), jax.random.fold_in(seeds[0], 3), 0, VOCAB - 1).astype(jnp.int32),
        "starts": draw_starts(jax.random.fold_in(seeds[15], 71), 0),
        "embed": normal_values(seeds[2], (VOCAB, D), 1.0, 6.0),
        "gain_one": jnp.clip(1.0 + 0.18 * jax.random.normal(seeds[3], (D,), jnp.float32), 0.1, 1.9),
        "row_qkv": draw_row_qkv(jax.random.fold_in(seeds[15], 71), 0),
        "row_out": normal_values(seeds[5], (D, D), D ** -0.5, 0.25),
        "gain_two": jnp.clip(1.0 + 0.18 * jax.random.normal(seeds[6], (D,), jnp.float32), 0.1, 1.9),
        "col_qkv": draw_col_qkv(jax.random.fold_in(seeds[15], 71), 0),
        "col_out": normal_values(seeds[8], (D, D), D ** -0.5, 0.25),
        "gain_three": jnp.clip(1.0 + 0.18 * jax.random.normal(seeds[9], (D,), jnp.float32), 0.1, 1.9),
        "mlp_in": normal_values(seeds[10], (D, FF), D ** -0.5, 0.25),
        "mlp_out": normal_values(seeds[11], (FF, D), FF ** -0.5, 0.1875),
        "project": normal_values(seeds[12], (D, CW), D ** -0.5, 0.25),
        "conv_one": normal_values(seeds[13], (3, 3, CW, CW), (9 * CW) ** -0.5, 0.1875),
        "conv_two": normal_values(seeds[14], (3, 3, CW, CW), (9 * CW) ** -0.5, 0.1875),
    }


EPS = 1e-06
NEGATIVE = -1e+30

def norm_round(values, norm_gain):
    scale = lax.rsqrt(lax.optimization_barrier(jnp.mean(values * values, axis=-1, keepdims=True)) + EPS)
    return (values * scale * norm_gain).astype(jnp.bfloat16)

def matmul(left, right):
    return jnp.einsum('...i,ij->...j', left.astype(jnp.float32), right.astype(jnp.float32))

def softmax_round(scores, visible):
    scores = jnp.where(visible, scores, NEGATIVE)
    top = lax.optimization_barrier(jnp.max(scores, axis=-1, keepdims=True))
    raised = jnp.exp(scores - top)
    return (raised / lax.optimization_barrier(jnp.sum(raised, axis=-1, keepdims=True))).astype(jnp.bfloat16)

def row_attend(queries, keys, values, head_count, first_column):
    depth = queries.shape[0]
    query_len = queries.shape[1]
    key_len = keys.shape[1]
    head_size = queries.shape[2] // head_count
    query_cols = first_column + jnp.arange(query_len, dtype=jnp.int32)
    key_cols = jnp.arange(key_len, dtype=jnp.int32)
    visible = query_cols[:, None] >= key_cols[None, :]

    def split_heads(block, length):
        return jnp.moveaxis(block.reshape(depth, length, head_count, head_size), 2, 0)

    def one_head(parts):
        head_q, head_k, head_v = parts
        scores = jnp.einsum('rqd,rkd->rqk', head_q.astype(jnp.float32), head_k.astype(jnp.float32)) * head_size ** (-0.5)
        soft_weights = softmax_round(scores, visible)
        return jnp.einsum('rqk,rkd->rqd', soft_weights.astype(jnp.float32), head_v.astype(jnp.float32)).astype(jnp.bfloat16)
    mixed = lax.map(one_head, (split_heads(queries, query_len), split_heads(keys, key_len), split_heads(values, key_len)))
    return jnp.moveaxis(mixed, 0, 2).reshape(depth, query_len, head_count * head_size)

def col_attend(queries, key_value, query_rows, query_starts):
    row_len, column_count, feature_width = queries.shape
    key_len = key_value.shape[0]
    head_size = key_value.shape[2] // 2
    head_count = feature_width // head_size
    split = queries.reshape(row_len, column_count, head_count, head_size)
    keys = key_value[..., :head_size]
    values = key_value[..., head_size:]
    scores = jnp.einsum('qchd,kcd->chqk', split.astype(jnp.float32), keys.astype(jnp.float32)) * head_size ** (-0.5)
    key_rows = jnp.arange(key_len, dtype=jnp.int32)
    visible = (key_rows[None, :] <= query_rows[:, None]) & (key_rows[None, :] >= query_starts[:, None])
    soft_weights = softmax_round(scores, visible)
    mixed = jnp.einsum('chqk,kcd->qchd', soft_weights.astype(jnp.float32), values.astype(jnp.float32)).astype(jnp.bfloat16)
    return mixed.reshape(row_len, column_count, feature_width)

def upsample(grid):
    return jnp.repeat(jnp.repeat(grid, 2, axis=0), 2, axis=1)

def conv_three(padded, kernel):
    height = padded.shape[0] - 2
    breadth = padded.shape[1] - 2
    total = jnp.zeros((height, breadth, kernel.shape[3]), jnp.float32)
    for shift_down in range(3):
        for shift_right in range(3):
            window = padded[shift_down:shift_down + height, shift_right:shift_right + breadth]
            total = total + matmul(window, kernel[shift_down, shift_right])
    return total

def pad_grid(grid):
    return jnp.pad(grid, ((1, 1), (1, 1), (0, 0)))

def reference(codes, starts, embed, gain_one, row_qkv, row_out, gain_two, col_qkv, col_out, gain_three, mlp_in, mlp_out, project, conv_one, conv_two):
    vocab_ids = jnp.arange(VOCAB, dtype=jnp.int32)
    one_hot = (codes[..., None] == vocab_ids).astype(jnp.bfloat16)
    hidden = matmul(one_hot, embed)
    normed = norm_round(hidden, gain_one)
    projected = matmul(normed, row_qkv).astype(jnp.bfloat16)
    queries = projected[..., :D]
    keys = projected[..., D:2 * D]
    values = projected[..., 2 * D:]

    def one_row(parts):
        return row_attend(parts[0][None], parts[1][None], parts[2][None], HEADS, 0)[0]
    row_mixed = lax.map(one_row, (queries, keys, values))
    hidden = hidden + matmul(row_mixed, row_out)
    normed = norm_round(hidden, gain_two)
    projected = matmul(normed, col_qkv).astype(jnp.bfloat16)
    col_queries = projected[..., :D]
    key_value = projected[..., D:]
    block_count = NC // COL_DEV

    def to_blocks(grid):
        return jnp.moveaxis(grid.reshape(NR, block_count, COL_DEV, grid.shape[2]), 1, 0)
    all_rows = jnp.arange(NR, dtype=jnp.int32)

    def one_block(parts):
        return col_attend(parts[0], parts[1], all_rows, starts)
    col_mixed = lax.map(one_block, (to_blocks(col_queries), to_blocks(key_value)))
    col_mixed = jnp.moveaxis(col_mixed, 0, 1).reshape(NR, NC, D)
    hidden = hidden + matmul(col_mixed, col_out)
    normed = norm_round(hidden, gain_three)
    inner = jax.nn.silu(matmul(normed, mlp_in)).astype(jnp.bfloat16)
    block_out = hidden + matmul(inner, mlp_out)
    coarse = matmul(block_out.astype(jnp.bfloat16), project).astype(jnp.bfloat16)
    upsampled = upsample(coarse)
    first = jax.nn.silu(conv_three(pad_grid(upsampled), conv_one)).astype(jnp.bfloat16)
    image = upsampled.astype(jnp.float32) + conv_three(pad_grid(first), conv_two)
    return (block_out, image)
```

```python
import math
import jax
import jax.numpy as jnp
from jax import lax
from jax.experimental import pallas as pl
from jax.experimental.pallas import tpu as pltpu
from jax.sharding import PartitionSpec as P

HEADS = 8
HD = 64
EPS = 1e-06
NEGATIVE = -1e30
LOG2E = math.log2(math.e)
F32 = jnp.float32
BF16 = jnp.bfloat16
VMEM_LIMIT = 56 * 1024 * 1024


def dot(left, right):
    return jnp.dot(left, right, preferred_element_type=F32)


def dot_t(left, right):
    return lax.dot_general(left, right, (((1,), (1,)), ((), ())), preferred_element_type=F32)


def norm_round(values, norm_gain):
    scale = lax.rsqrt(jnp.mean(values * values, axis=-1, keepdims=True) + EPS)
    return (values * scale * norm_gain).astype(BF16)


def silu(v):
    return v / (1.0 + jnp.exp(-v))


def lane_low(rows):
    return lax.broadcasted_iota(jnp.int32, (rows, 128), 1) < HD


def row_kernel(
    codes_ref, base_ref, embed_ref, g1_ref, wqkv_ref, wro_ref, g2_ref, wcol_ref,
    ar_ref, q2_ref, kv_ref,
    qtab, kz, vz, seen, tri, wq2,
):
    k = pl.program_id(0)
    vocab, width = embed_ref.shape
    rows = codes_ref.shape[0]
    tile = ar_ref.shape[0]
    per = tile // rows
    scale = (HD ** -0.5) * LOG2E

    @pl.when(k == 0)
    def _():
        normed = norm_round(embed_ref[...].astype(F32), g1_ref[...])
        low = lane_low(vocab)
        qtab[...] = (dot(normed, wqkv_ref[:, :width]) * scale).astype(BF16)
        keys = dot(normed, wqkv_ref[:, width : 2 * width])
        values = dot(normed, wqkv_ref[:, 2 * width :])
        for h in range(HEADS):
            p = h // 2
            mine = low if h % 2 == 0 else jnp.logical_not(low)
            sl = slice(p * 128, p * 128 + 128)
            kz[h] = jnp.where(mine, keys[:, sl], 0.0).astype(BF16)
            vz[h] = jnp.where(mine, values[:, sl], 1.0).astype(BF16)
        seen[...] = base_ref[...]
        out_t = lax.broadcasted_iota(jnp.int32, (tile, tile), 0)
        in_t = lax.broadcasted_iota(jnp.int32, (tile, tile), 1)
        tri[...] = jnp.where(
            (out_t % rows == in_t % rows) & (in_t // rows <= out_t // rows), 1.0, 0.0
        ).astype(BF16)
        lowd = lane_low(width)
        for p in range(HEADS // 2):
            w = wcol_ref[:, p * 128 : p * 128 + 128].astype(F32)
            wq2[:, (2 * p) * 128 : (2 * p + 1) * 128] = jnp.where(lowd, w, 0.0).astype(BF16)
            wq2[:, (2 * p + 1) * 128 : (2 * p + 2) * 128] = jnp.where(
                lowd, pltpu.roll(w, HD, 1), 0.0
            ).astype(BF16)

    rolled = pltpu.roll(codes_ref[...], 128 - per * k, 1)
    ids = lax.broadcasted_iota(jnp.int32, (rows, vocab), 1)
    one_hot = jnp.concatenate(
        [jnp.where(rolled[:, c : c + 1] == ids, 1.0, 0.0) for c in range(per)], axis=0
    ).astype(BF16)
    counts = dot(tri[...], one_hot) + jnp.concatenate([seen[...]] * per, axis=0)
    seen[...] = counts[tile - rows :]
    logn = jnp.where(counts > 0.5, jnp.log2(jnp.maximum(counts, 1.0)), NEGATIVE)
    emb = dot(one_hot, embed_ref[...])
    q = dot(one_hot, qtab[...]).astype(BF16)
    low = lane_low(tile)
    mixed = []
    for p in range(HEADS // 2):
        outs = []
        qp = q[:, p * 128 : p * 128 + 128]
        for h in (2 * p, 2 * p + 1):
            s = dot_t(qp, kz[h]) + logn
            top = jnp.max(s, axis=-1, keepdims=True)
            e = jnp.exp2(s - top).astype(BF16)
            outs.append(dot(e, vz[h]))
        num = jnp.where(low, outs[0], outs[1])
        den = pltpu.roll(jnp.where(low, outs[1], outs[0]), HD, 1)
        mixed.append((num / den).astype(BF16))
    after = emb + dot(jnp.concatenate(mixed, axis=1), wro_ref[...])
    ar_ref[...] = after
    normed = norm_round(after, g2_ref[...])
    q2 = dot(normed, wq2[...]) * scale
    lane = lax.broadcasted_iota(jnp.int32, (tile, 128), 1)
    row = lax.broadcasted_iota(jnp.int32, (tile, 128), 0) % rows
    mark = jnp.where(lane == HD + row, 1.0, 0.0)
    for h in range(HEADS):
        q2_ref[:, h * 128 : h * 128 + 128] = (q2[:, h * 128 : h * 128 + 128] + mark).astype(BF16)
    kv_ref[...] = dot(normed, wcol_ref[:, width:]).astype(BF16)


def full(shape):
    return pl.BlockSpec(shape, lambda *_: (0,) * len(shape))


def row_call(codes, base, embed, g1, wqkv, wro, g2, wcol, tokens):
    vocab, width = embed.shape
    rows = codes.shape[0]
    tile = rows * 8
    return pl.pallas_call(
        row_kernel,
        grid=(tokens // tile,),
        in_specs=[full(x.shape) for x in (codes, base, embed, g1, wqkv, wro, g2, wcol)],
        out_specs=[
            pl.BlockSpec((tile, width), lambda i: (i, 0)),
            pl.BlockSpec((tile, 2 * width), lambda i: (i, 0)),
            pl.BlockSpec((tile, 2 * HD), lambda i: (i, 0)),
        ],
        out_shape=[
            jax.ShapeDtypeStruct((tokens, width), F32),
            jax.ShapeDtypeStruct((tokens, 2 * width), BF16),
            jax.ShapeDtypeStruct((tokens, 2 * HD), BF16),
        ],
        scratch_shapes=[
            pltpu.VMEM((vocab, width), BF16),
            pltpu.VMEM((HEADS, vocab, 128), BF16),
            pltpu.VMEM((HEADS, vocab, 128), BF16),
            pltpu.VMEM((rows, vocab), F32),
            pltpu.VMEM((tile, tile), BF16),
            pltpu.VMEM((width, 2 * width), BF16),
        ],
        compiler_params=pltpu.CompilerParams(vmem_limit_bytes=VMEM_LIMIT),
        name="row_part",
    )(codes, base, embed, g1, wqkv, wro, g2, wcol)


def col_kernel(
    starts_ref, q2_ref, kv_ref, ar_ref, wco_ref, g3_ref, w1_ref, w2_ref, wp_ref,
    bo_ref, co_ref,
    bias, mixed,
):
    k = pl.program_id(0)
    rows = q2_ref.shape[1]
    per = q2_ref.shape[0]
    slots = kv_ref.shape[0]
    keys = slots * rows
    tile = per * rows

    @pl.when(k == 0)
    def _():
        first = lax.axis_index("row") * rows
        lane = lax.broadcasted_iota(jnp.int32, (keys, 128), 1)
        key_row = lax.broadcasted_iota(jnp.int32, (keys, 128), 0)
        query_row = first + lane - HD
        seen = (key_row <= query_row) & (key_row >= starts_ref[0:1, :])
        bias[...] = jnp.where((lane < HD) | seen, 0.0, NEGATIVE).astype(BF16)

    low_f = jnp.where(lane_low(keys), 1.0, 0.0)
    low_k = low_f.astype(BF16)
    high_k = (1.0 - low_f).astype(BF16)
    low = lane_low(rows)
    for c in range(per):
        kv = kv_ref[:, c].reshape(keys, 2 * HD)
        ka = kv * low_k + bias[...]
        va = kv * high_k + low_k
        q = q2_ref[c]
        q = jnp.concatenate([q[:, h * 128 : h * 128 + 128] for h in range(HEADS)], axis=0)
        s = dot_t(q, ka)
        top = jnp.max(s, axis=-1, keepdims=True)
        e = jnp.exp2(s - top).astype(BF16)
        o = dot(e, va)
        for p in range(HEADS // 2):
            even = o[(2 * p) * rows : (2 * p + 1) * rows]
            odd = o[(2 * p + 1) * rows : (2 * p + 2) * rows]
            keep = jnp.where(low, even, odd)
            other = pltpu.roll(jnp.where(low, odd, even), HD, 1)
            num = jnp.where(low, other, keep)
            den = jnp.where(low, keep, other)
            mixed[c * rows : (c + 1) * rows, p * 128 : p * 128 + 128] = (num / den).astype(BF16)
    after = ar_ref[...] + dot(mixed[...], wco_ref[...])
    normed = norm_round(after, g3_ref[...])
    inner = silu(dot(normed, w1_ref[...])).astype(BF16)
    out = after + dot(inner, w2_ref[...])
    coarse = dot(out.astype(BF16), wp_ref[...]).astype(BF16)
    bo_ref[...] = jnp.swapaxes(out.reshape(per, rows, out.shape[1]), 0, 1)
    co_ref[...] = coarse.reshape(per, rows, coarse.shape[1])


def col_call(starts, q2, kv, ar, wco, g3, w1, w2, wp):
    cols, rows, _ = q2.shape
    slots = kv.shape[0]
    width = ar.shape[1]
    channels = wp.shape[1]
    per = 8
    return pl.pallas_call(
        col_kernel,
        grid=(cols // per,),
        in_specs=[
            full(starts.shape),
            pl.BlockSpec((per, rows, 2 * width), lambda i: (i, 0, 0)),
            pl.BlockSpec((slots, per, rows, 2 * HD), lambda i: (0, i, 0, 0)),
            pl.BlockSpec((per * rows, width), lambda i: (i, 0)),
        ]
        + [full(x.shape) for x in (wco, g3, w1, w2, wp)],
        out_specs=[
            pl.BlockSpec((rows, per, width), lambda i: (0, i, 0)),
            pl.BlockSpec((per, rows, channels), lambda i: (i, 0, 0)),
        ],
        out_shape=[
            jax.ShapeDtypeStruct((rows, cols, width), F32),
            jax.ShapeDtypeStruct((cols, rows, channels), BF16),
        ],
        scratch_shapes=[
            pltpu.VMEM((slots * rows, 128), BF16),
            pltpu.VMEM((per * rows, width), BF16),
        ],
        compiler_params=pltpu.CompilerParams(vmem_limit_bytes=VMEM_LIMIT),
        name="col_part",
    )(starts, q2, kv, ar, wco, g3, w1, w2, wp)


def conv_kernel(ext_ref, k1_ref, k2_ref, out_ref, w1, w2, cat, fine):
    k = pl.program_id(0)
    erows, ring, ch = ext_ref.shape
    pairs = erows - 1
    cols = out_ref.shape[1] // 2
    step_rows = out_ref.shape[0]

    @pl.when(k == 0)
    def _():
        taps = [[k1_ref[y, x].astype(F32) for x in range(3)] for y in range(3)]
        none = jnp.zeros((ch, ch), F32)
        by_half = (
            ([taps[0][x] + taps[1][x] for x in range(3)], taps[2]),
            (taps[0], [taps[1][x] + taps[2][x] for x in range(3)]),
        )
        for half in range(2):
            for dy in range(2):
                t = by_half[half][dy]
                for b in range(2):
                    three = (t[0], t[1] + t[2], none) if b == 0 else (none, t[0] + t[1], t[2])
                    for dx in range(3):
                        w1[
                            (dy * 3 + dx) * ch : (dy * 3 + dx + 1) * ch,
                            (half * 2 + b) * ch : (half * 2 + b + 1) * ch,
                        ] = three[dx].astype(BF16)
        for dy in range(3):
            for s in range(4):
                for b in range(2):
                    w2[(dy * 4 + s) * ch : (dy * 4 + s + 1) * ch, b * ch : (b + 1) * ch] = (
                        k2_ref[dy, s - b] if 0 <= s - b <= 2 else none.astype(BF16)
                    )

        def widen(e, carry):
            x = ext_ref[e].astype(F32)
            cat[e] = jnp.concatenate(
                [pltpu.roll(x, 1, 0), x, pltpu.roll(x, ring - 1, 0)], axis=1
            ).astype(BF16)
            return carry

        lax.fori_loop(0, erows, widen, 0)
        place = lax.broadcasted_iota(jnp.int32, (ring, 128), 0)
        at_left = lax.axis_index("col") == 0
        at_right = lax.axis_index("col") == lax.axis_size("col") - 1
        col_keep = jnp.where(
            ((place == ring - 1) & at_left) | ((place == cols) & at_right), 0.0, 1.0
        )
        at_top = lax.axis_index("row") == 0
        at_bottom = lax.axis_index("row") == lax.axis_size("row") - 1
        group = 3

        def first_conv(g, carry):
            e0 = g * group
            left = jnp.concatenate(
                [
                    jnp.concatenate([cat[e0 + i], cat[e0 + i + 1]], axis=1)
                    for i in range(group)
                ],
                axis=0,
            )
            y = silu(dot(left, w1[...]))
            for i in range(group):
                for half in range(2):
                    f = 2 * (e0 + i) + half
                    outside = ((f == 0) & at_top) | ((f == 2 * pairs - 1) & at_bottom)
                    keep = jnp.where(outside, 0.0, 1.0) * col_keep
                    f0 = y[i * ring : (i + 1) * ring, (2 * half) * ch : (2 * half + 1) * ch] * keep
                    f1 = y[i * ring : (i + 1) * ring, (2 * half + 1) * ch : (2 * half + 2) * ch] * keep
                    fine[f] = jnp.concatenate(
                        [pltpu.roll(f1, 1, 0), f0, f1, pltpu.roll(f0, ring - 1, 0)], axis=1
                    ).astype(BF16)
            return carry

        lax.fori_loop(0, pairs // group, first_conv, 0)

    y0 = k * step_rows
    left = jnp.concatenate(
        [
            jnp.concatenate([fine[y0 + i + dy, 0:cols] for dy in range(3)], axis=1)
            for i in range(step_rows)
        ],
        axis=0,
    )
    second = dot(left, w2[...])
    for i in range(step_rows):
        up = ext_ref[k * (step_rows // 2) + i // 2 + 1, 0:cols].astype(F32)
        for b in range(2):
            out_ref[i, pl.ds(b, cols, stride=2), :] = (
                second[i * cols : (i + 1) * cols, b * ch : (b + 1) * ch] + up
            )


def conv_call(ext, k1, k2):
    erows, ring, ch = ext.shape
    fine_rows = 2 * (erows - 2)
    cols = ring - 16
    step_rows = 8
    return pl.pallas_call(
        conv_kernel,
        grid=(fine_rows // step_rows,),
        in_specs=[full(ext.shape), full(k1.shape), full(k2.shape)],
        out_specs=pl.BlockSpec((step_rows, 2 * cols, ch), lambda i: (i, 0, 0)),
        out_shape=jax.ShapeDtypeStruct((fine_rows, 2 * cols, ch), F32),
        scratch_shapes=[
            pltpu.VMEM((6 * ch, 4 * ch), BF16),
            pltpu.VMEM((12 * ch, 2 * ch), BF16),
            pltpu.VMEM((erows, ring, 3 * ch), BF16),
            pltpu.VMEM((fine_rows + 2, ring, 4 * ch), BF16),
        ],
        compiler_params=pltpu.CompilerParams(vmem_limit_bytes=VMEM_LIMIT),
        name="conv_part",
    )(ext, k1, k2)


def padded_2(block, sides, width):
    for axis, dim in sides:
        count = lax.axis_size(axis)
        forward = [(i, i + 1) for i in range(count - 1)]
        backward = [(target, source) for source, target in forward]
        low = lax.ppermute(
            lax.slice_in_dim(block, block.shape[dim] - width, None, axis=dim), axis, forward
        )
        high = lax.ppermute(lax.slice_in_dim(block, 0, width, axis=dim), axis, backward)
        block = jnp.concatenate([low, block, high], axis=dim)
    return block


def per_device(
    codes, starts, embed, gain_one, row_qkv, row_out, gain_two, col_qkv, col_out,
    gain_three, mlp_in, mlp_out, project, conv_one, conv_two,
):
    rows, cols = codes.shape
    vocab, width = embed.shape
    ids = jnp.arange(vocab, dtype=jnp.int32)
    mine = jnp.sum((codes[..., None] == ids).astype(F32), axis=1)
    every = lax.all_gather(mine, "col", axis=0)
    earlier = jnp.arange(every.shape[0]) < lax.axis_index("col")
    base = jnp.sum(jnp.where(earlier[:, None, None], every, 0.0), axis=0)
    wide = jnp.pad(codes, ((0, 0), (0, 128 - cols)))
    after_row, q2, kv = row_call(
        wide, base, embed, gain_one[None], row_qkv, row_out, gain_two[None], col_qkv, rows * cols
    )
    kv = kv.reshape(cols, rows, 2 * HD)
    kvs = lax.all_gather(kv, "row", axis=0)
    my_starts = lax.dynamic_slice_in_dim(starts, lax.axis_index("row") * rows, rows)
    my_starts = jnp.pad(my_starts, (HD, 128 - HD - rows))[None]
    block_out, coarse = col_call(
        my_starts, q2.reshape(cols, rows, 2 * width), kvs, after_row,
        col_out, gain_three[None], mlp_in, mlp_out, project,
    )
    coarse = jnp.swapaxes(coarse, 0, 1)
    ext = padded_2(coarse, (("row", 0), ("col", 1)), 1)
    ext = jnp.concatenate(
        [ext[:, 1:], jnp.zeros((rows + 2, 14, ext.shape[2]), BF16), ext[:, :1]], axis=1
    )
    image = conv_call(ext, conv_one, conv_two)
    return (block_out, image)


def solution(mesh):
    in_specs = (P("row", "col"),) + (P(),) * 14
    out_specs = (P("row", "col", None), P("row", "col", None))
    return jax.shard_map(
        per_device, mesh=mesh, in_specs=in_specs, out_specs=out_specs, check_vma=False
    )
```

```python
import functools
import math
import jax
import jax.numpy as jnp
from jax import lax
from jax.experimental import pallas as pl
from jax.experimental.pallas import tpu as pltpu
from jax.sharding import PartitionSpec as P

HEADS = 8
HD = 64
EPS = 1e-06
NEGATIVE = -1e30
LOG2E = math.log2(math.e)
F32 = jnp.float32
BF16 = jnp.bfloat16
MESH = pl.DeviceIdType.MESH
VMEM_LIMIT = 56 * 1024 * 1024


def dot(left, right):
    return jnp.dot(left, right, preferred_element_type=F32)


def dot_t(left, right):
    return lax.dot_general(left, right, (((1,), (1,)), ((), ())), preferred_element_type=F32)


def norm_round(values, norm_gain):
    scale = lax.rsqrt(jnp.mean(values * values, axis=-1, keepdims=True) + EPS)
    return (values * scale * norm_gain).astype(BF16)


def silu(v):
    return v / (1.0 + jnp.exp(-v))


def lane_low(rows):
    return lax.broadcasted_iota(jnp.int32, (rows, 128), 1) < HD


PER = 8


def row_setup(embed_ref, g1_ref, wqkv_ref, wcol_ref, qtab, kz, vz, tri, wq2, rows):
    vocab, width = embed_ref.shape
    tile = tri.shape[0]
    scale = (HD ** -0.5) * LOG2E
    normed = norm_round(embed_ref[...].astype(F32), g1_ref[...])
    low = lane_low(vocab)
    qtab[...] = (dot(normed, wqkv_ref[:, :width]) * scale).astype(BF16)
    keys = dot(normed, wqkv_ref[:, width : 2 * width])
    values = dot(normed, wqkv_ref[:, 2 * width :])
    for h in range(HEADS):
        p = h // 2
        mine = low if h % 2 == 0 else jnp.logical_not(low)
        sl = slice(p * 128, p * 128 + 128)
        kz[h] = jnp.where(mine, keys[:, sl], 0.0).astype(BF16)
        vz[h] = jnp.where(mine, values[:, sl], 1.0).astype(BF16)
    out_t = lax.broadcasted_iota(jnp.int32, (tile, tile), 0)
    in_t = lax.broadcasted_iota(jnp.int32, (tile, tile), 1)
    tri[...] = jnp.where(
        (out_t % rows == in_t % rows) & (in_t // rows <= out_t // rows), 1.0, 0.0
    ).astype(BF16)
    lowd = lane_low(width)
    for p in range(HEADS // 2):
        w = wcol_ref[:, p * 128 : p * 128 + 128].astype(F32)
        wq2[:, (2 * p) * 128 : (2 * p + 1) * 128] = jnp.where(lowd, w, 0.0).astype(BF16)
        wq2[:, (2 * p + 1) * 128 : (2 * p + 2) * 128] = jnp.where(
            lowd, pltpu.roll(w, HD, 1), 0.0
        ).astype(BF16)


def row_tile(k, codes_ref, embed_ref, wro_ref, g2_ref, wcol_ref, qtab, kz, vz, seen, tri, wq2):
    vocab, width = embed_ref.shape
    rows = codes_ref.shape[0]
    tile = tri.shape[0]
    scale = (HD ** -0.5) * LOG2E
    rolled = pltpu.roll(codes_ref[...], 128 - PER * k, 1)
    ids = lax.broadcasted_iota(jnp.int32, (rows, vocab), 1)
    one_hot = jnp.concatenate(
        [jnp.where(rolled[:, c : c + 1] == ids, 1.0, 0.0) for c in range(PER)], axis=0
    ).astype(BF16)
    counts = dot(tri[...], one_hot) + jnp.concatenate([seen[...]] * PER, axis=0)
    seen[...] = counts[tile - rows :]
    logn = jnp.where(counts > 0.5, jnp.log2(jnp.maximum(counts, 1.0)), NEGATIVE)
    emb = dot(one_hot, embed_ref[...])
    q = dot(one_hot, qtab[...]).astype(BF16)
    low = lane_low(tile)
    mixed = []
    for p in range(HEADS // 2):
        outs = []
        qp = q[:, p * 128 : p * 128 + 128]
        for h in (2 * p, 2 * p + 1):
            s = dot_t(qp, kz[h]) + logn
            top = jnp.max(s, axis=-1, keepdims=True)
            e = jnp.exp2(s - top).astype(BF16)
            outs.append(dot(e, vz[h]))
        num = jnp.where(low, outs[0], outs[1])
        den = pltpu.roll(jnp.where(low, outs[1], outs[0]), HD, 1)
        mixed.append((num / den).astype(BF16))
    after = emb + dot(jnp.concatenate(mixed, axis=1), wro_ref[...])
    normed = norm_round(after, g2_ref[...])
    q2 = dot(normed, wq2[...]) * scale
    lane = lax.broadcasted_iota(jnp.int32, (tile, 128), 1)
    row = lax.broadcasted_iota(jnp.int32, (tile, 128), 0) % rows
    mark = jnp.where(lane == HD + row, 1.0, 0.0)
    q2 = jnp.concatenate(
        [(q2[:, h * 128 : h * 128 + 128] + mark).astype(BF16) for h in range(HEADS)], axis=1
    )
    return after, q2, dot(normed, wcol_ref[:, width:]).astype(BF16)


def set_bias(bias, starts_ref, first):
    lane = lax.broadcasted_iota(jnp.int32, bias.shape, 1)
    key_row = lax.broadcasted_iota(jnp.int32, bias.shape, 0)
    query_row = first + lane - HD
    seen = (key_row <= query_row) & (key_row >= starts_ref[0:1, :])
    bias[...] = jnp.where((lane < HD) | seen, 0.0, NEGATIVE).astype(BF16)


def col_tile(q_of, kv_of, bias, mixed, rows, keys):
    low_f = jnp.where(lane_low(keys), 1.0, 0.0)
    low_k = low_f.astype(BF16)
    high_k = (1.0 - low_f).astype(BF16)
    low = lane_low(rows)
    for c in range(PER):
        kv = kv_of(c)
        ka = kv * low_k + bias[...]
        va = kv * high_k + low_k
        q = q_of(c)
        q = jnp.concatenate([q[:, h * 128 : h * 128 + 128] for h in range(HEADS)], axis=0)
        s = dot_t(q, ka)
        top = jnp.max(s, axis=-1, keepdims=True)
        e = jnp.exp2(s - top).astype(BF16)
        o = dot(e, va)
        for p in range(HEADS // 2):
            even = o[(2 * p) * rows : (2 * p + 1) * rows]
            odd = o[(2 * p + 1) * rows : (2 * p + 2) * rows]
            keep = jnp.where(low, even, odd)
            other = pltpu.roll(jnp.where(low, odd, even), HD, 1)
            num = jnp.where(low, other, keep)
            den = jnp.where(low, keep, other)
            mixed[c * rows : (c + 1) * rows, p * 128 : p * 128 + 128] = (num / den).astype(BF16)


CORNERS = ((-1, -1), (-1, 1), (1, -1), (1, 1))


def front_kernel(
    row_count, col_count,
    codes_ref, starts_ref, embed_ref, g1_ref, wqkv_ref, wro_ref, g2_ref, wcol_ref, wco_ref,
    after_ref, halo_ref,
    qtab, kz, vz, seen, tri, wq2, bias, mixed, kv_all, q2_all, held, hist, edge,
    kv_send, kv_recv, hist_send, hist_recv, halo_send, halo_recv, out_sem,
):
    rows = codes_ref.shape[0]
    vocab, width = embed_ref.shape
    slots, cols = kv_all.shape[0], kv_all.shape[1]
    keys = slots * rows
    tile = PER * rows
    chunks = cols // PER
    my_row, my_col = lax.axis_index("row"), lax.axis_index("col")

    half = row_count // 4

    def sibling(r):
        return r + 1 - 2 * lax.rem(r, 2)

    def across(r):
        return r + 2 - 4 * lax.rem(lax.div(r, 2), 2)

    def turned(r, steps):
        return lax.rem(r + 4 * steps, row_count)

    sib, beyond = sibling(my_row), across(my_row)
    down, up = turned(my_row, 1), turned(my_row, half - 1)
    far = turned(my_row, 2)

    halo_ref[...] = jnp.zeros_like(halo_ref)
    def row_by(dr):
        return lax.rem(my_row + dr + row_count, row_count)

    barrier = pltpu.get_barrier_semaphore()
    other = row_by(2 * lax.rem(my_row, 2) - 1)
    peers = [{"row": r, "col": my_col} for r in (sib, beyond, down, up, other)]
    for d in range(1, col_count):
        peers.append({"row": my_row, "col": lax.rem(my_col + d, col_count)})
    for dr, dc in CORNERS:
        peers.append({"row": row_by(dr), "col": lax.rem(my_col + dc + col_count, col_count)})
    for peer in peers:
        pl.semaphore_signal(barrier, 1, device_id=peer, device_id_type=MESH)

    def there(dr, dc):
        ok = None
        for at, step, count in ((my_row, dr, row_count), (my_col, dc, col_count)):
            if step:
                t = at + step >= 0 if step < 0 else at + step < count
                ok = t if ok is None else ok & t
        return ok

    ids = lax.broadcasted_iota(jnp.int32, (rows, vocab), 1)
    codes = codes_ref[...]
    own = jnp.zeros((rows, vocab), F32)
    for c in range(cols):
        own = own + jnp.where(codes[:, c : c + 1] == ids, 1.0, 0.0)
    hist[my_col] = own.astype(BF16)

    pl.semaphore_wait(barrier, len(peers))

    def hist_copy(d, slot):
        return pltpu.make_async_remote_copy(
            src_ref=hist.at[slot], dst_ref=hist.at[slot],
            send_sem=hist_send.at[d], recv_sem=hist_recv.at[slot],
            device_id={"col": lax.rem(my_col + d, col_count)}, device_id_type=MESH,
        )

    for d in range(1, col_count):
        hist_copy(d, my_col).start()

    row_setup(embed_ref, g1_ref, wqkv_ref, wcol_ref, qtab, kz, vz, tri, wq2, rows)
    set_bias(bias, starts_ref, my_row * rows)

    for d in range(1, col_count):
        hist_copy(d, lax.rem(my_col + d, col_count)).wait_recv()
    base = jnp.zeros((rows, vocab), F32)
    for c in range(col_count):
        base = base + jnp.where(c < my_col, 1.0, 0.0) * hist[c].astype(F32)
    seen[...] = base

    def kv_copy(n, k, slot, dest):
        part = kv_all.at[slot, pl.ds(k * PER, PER)]
        return pltpu.make_async_remote_copy(
            src_ref=part, dst_ref=part,
            send_sem=kv_send.at[n, k], recv_sem=kv_recv.at[slot, k],
            device_id={"row": dest}, device_id_type=MESH,
        )

    def arrived(k, slot):
        kv_copy(0, k, slot, sib).wait_recv()

    def relay(s):
        k1 = s - 1

        @pl.when((k1 >= 0) & (k1 < chunks))
        def _():
            arrived(k1, beyond)
            kv_copy(4, k1, beyond, down).start()
            kv_copy(5, k1, beyond, up).start()
            kv_copy(6, k1, beyond, sib).start()

        k2 = s - 2

        @pl.when((k2 >= 0) & (k2 < chunks))
        def _():
            from_up = (up, turned(beyond, half - 1))
            from_down = (down, turned(beyond, 1))
            for i, slot in enumerate(from_up + from_down):
                arrived(k2, slot)
            even = lax.rem(k2, 2) == 0
            for i in range(2):
                @pl.when(even)
                def _():
                    kv_copy(7 + i, k2, from_up[i], down).start()

                @pl.when(jnp.logical_not(even))
                def _():
                    kv_copy(7 + i, k2, from_down[i], up).start()
            for i, slot in enumerate(from_up + from_down):
                kv_copy(9 + i, k2, slot, sib).start()

        k3 = s - 3

        @pl.when((k3 >= 0) & (k3 < chunks))
        def _():
            for i, slot in enumerate((far, turned(beyond, 2))):
                arrived(k3, slot)
                kv_copy(13 + i, k3, slot, sib).start()

    def row_step(k, carry):
        relay(k)
        after, q2, kv = row_tile(
            k, codes_ref, embed_ref, wro_ref, g2_ref, wcol_ref, qtab, kz, vz, seen, tri, wq2
        )
        kv_all[my_row, pl.ds(k * PER, PER)] = kv.reshape(PER, rows, 2 * HD)
        kv_copy(0, k, my_row, beyond).start()
        kv_copy(1, k, my_row, down).start()
        kv_copy(2, k, my_row, up).start()
        kv_copy(3, k, my_row, sib).start()
        held[pl.ds(k * tile, tile)] = after
        q2_all[pl.ds(k * PER, PER)] = q2.reshape(PER, rows, 2 * width)
        return carry

    lax.fori_loop(0, chunks, row_step, 0)

    def halo_copy(sem, src, at, size, dr, dc):
        return pltpu.make_async_remote_copy(
            src_ref=src, dst_ref=halo_ref.at[pl.ds(at, size)],
            send_sem=halo_send.at[sem], recv_sem=halo_recv.at[sem],
            device_id={"row": my_row + dr, "col": my_col + dc}, device_id_type=MESH,
        )

    left_at, corner_at = 2 * cols, 2 * cols + 2 * rows
    side_sem = 2 * chunks

    def edge_copy(which, k, dr):
        at = cols if which == 0 else 0
        return halo_copy(
            which * chunks + k, edge.at[which, pl.ds(k * PER, PER)], at + k * PER, PER, dr, 0
        )

    def side_copy(which, dc):
        c = 0 if which == 0 else cols - 1
        at = left_at + rows if which == 0 else left_at
        return halo_copy(side_sem + which, held.at[pl.ds(c * rows, rows)], at, rows, 0, dc)

    def corner_copy(i, dr, dc):
        k = 0 if dc < 0 else chunks - 1
        at = corner_at + (len(CORNERS) - 1 - i) * PER
        return halo_copy(
            side_sem + 2 + i, edge.at[0 if dr < 0 else 1, pl.ds(k * PER, PER)], at, PER, dr, dc
        )

    def out_copy(k):
        return pltpu.make_async_copy(
            held.at[pl.ds(k * tile, tile)], after_ref.at[pl.ds(k * tile, tile)], out_sem.at[k]
        )

    def col_step(j, carry):
        relay(chunks + j)
        mid = chunks // 2
        k = jnp.where(j < mid, j, jnp.where(j == mid, chunks - 1, j - 1))
        for slot in (
            my_row, beyond, down, turned(beyond, 1), up, turned(beyond, half - 1),
            far, turned(beyond, 2),
        ):
            arrived(k, sibling(slot))
        col_tile(
            lambda c: q2_all[k * PER + c],
            lambda c: kv_all[:, k * PER + c].reshape(keys, 2 * HD),
            bias, mixed, rows, keys,
        )
        after = held[pl.ds(k * tile, tile)] + dot(mixed[...], wco_ref[...])
        held[pl.ds(k * tile, tile)] = after
        out_copy(k).start()
        grid = after.reshape(PER, rows, width)
        edge[0, pl.ds(k * PER, PER)] = grid[:, 0]
        edge[1, pl.ds(k * PER, PER)] = grid[:, rows - 1]

        @pl.when(there(-1, 0))
        def _():
            edge_copy(0, k, -1).start()

        @pl.when(there(1, 0))
        def _():
            edge_copy(1, k, 1).start()

        for which, dc in ((0, -1), (1, 1)):
            last = 0 if which == 0 else chunks - 1

            @pl.when(there(0, dc) & (k == last))
            def _():
                side_copy(which, dc).start()

        for i, (dr, dc) in enumerate(CORNERS):
            last = 0 if dc < 0 else chunks - 1

            @pl.when(there(dr, dc) & (k == last))
            def _():
                corner_copy(i, dr, dc).start()

        return carry

    lax.fori_loop(0, chunks, col_step, 0)

    for d in range(1, col_count):
        hist_copy(d, my_col).wait_send()

    def finish(k, carry):
        for n in range(kv_send.shape[0]):
            kv_copy(n, k, my_row, sib).wait_send()
        out_copy(k).wait()

        @pl.when(there(-1, 0))
        def _():
            edge_copy(0, k, -1).wait_send()
            edge_copy(1, k, -1).wait_recv()

        @pl.when(there(1, 0))
        def _():
            edge_copy(1, k, 1).wait_send()
            edge_copy(0, k, 1).wait_recv()

        return carry

    lax.fori_loop(0, chunks, finish, 0)
    for which, dc in ((0, -1), (1, 1)):
        @pl.when(there(0, dc))
        def _():
            side_copy(which, dc).wait_send()
            side_copy(1 - which, dc).wait_recv()
    for i, (dr, dc) in enumerate(CORNERS):
        @pl.when(there(dr, dc))
        def _():
            corner_copy(i, dr, dc).wait_send()
            corner_copy(len(CORNERS) - 1 - i, dr, dc).wait_recv()


def full(shape):
    return pl.BlockSpec(shape, lambda *_: (0,) * len(shape))


def front_call(codes, starts, embed, g1, wqkv, wro, g2, wcol, wco, cols):
    vocab, width = embed.shape
    rows = codes.shape[0]
    row_count, col_count = lax.axis_size("row"), lax.axis_size("col")
    tokens = rows * cols
    tile = rows * PER
    chunks = cols // PER
    halo = -(-(2 * cols + 2 * rows + 4 * PER) // tile) * tile
    dma = pltpu.SemaphoreType.DMA
    args = (codes, starts, embed, g1, wqkv, wro, g2, wcol, wco)
    return pl.pallas_call(
        functools.partial(front_kernel, row_count, col_count),
        in_specs=[pl.BlockSpec(memory_space=pltpu.VMEM)] * len(args),
        out_specs=[
            pl.BlockSpec(memory_space=pl.ANY),
            pl.BlockSpec(memory_space=pltpu.VMEM),
        ],
        out_shape=[
            jax.ShapeDtypeStruct((tokens, width), F32),
            jax.ShapeDtypeStruct((halo, width), F32),
        ],
        scratch_shapes=[
            pltpu.VMEM((vocab, width), BF16),
            pltpu.VMEM((HEADS, vocab, 128), BF16),
            pltpu.VMEM((HEADS, vocab, 128), BF16),
            pltpu.VMEM((rows, vocab), F32),
            pltpu.VMEM((tile, tile), BF16),
            pltpu.VMEM((width, 2 * width), BF16),
            pltpu.VMEM((row_count * rows, 128), BF16),
            pltpu.VMEM((tile, width), BF16),
            pltpu.VMEM((row_count, cols, rows, 2 * HD), BF16),
            pltpu.VMEM((cols, rows, 2 * width), BF16),
            pltpu.VMEM((tokens, width), F32),
            pltpu.VMEM((col_count, rows, vocab), BF16),
            pltpu.VMEM((2, cols, width), F32),
            dma((15, chunks)),
            dma((row_count, chunks)),
            dma((col_count,)),
            dma((col_count,)),
            dma((2 * chunks + 6,)),
            dma((2 * chunks + 6,)),
            dma((chunks,)),
        ],
        compiler_params=pltpu.CompilerParams(
            vmem_limit_bytes=VMEM_LIMIT, collective_id=0, has_side_effects=True
        ),
        name="front",
    )(*args)


def back_kernel(
    col_steps,
    after_ref, halo_ref, g3_ref, win_ref, wout_ref, wp_ref, k1_ref, k2_ref,
    bo_ref, img_ref,
    ext, w1, w2, cat, fine,
):
    k = pl.program_id(0)
    erows, ring, ch = ext.shape
    rows = erows - 2
    pairs = erows - 1
    cols = img_ref.shape[1] // 2
    fine_step = img_ref.shape[0]
    my_row, my_col = lax.axis_index("row"), lax.axis_index("col")
    at_top, at_bottom = my_row == 0, my_row == lax.axis_size("row") - 1
    at_left, at_right = my_col == 0, my_col == lax.axis_size("col") - 1

    def cells(after):
        normed = norm_round(after, g3_ref[...])
        inner = silu(dot(normed, win_ref[...])).astype(BF16)
        out = after + dot(inner, wout_ref[...])
        coarse = dot(out.astype(BF16), wp_ref[...]).astype(BF16).astype(F32)
        return out, coarse

    @pl.when(k == 0)
    def _():
        ext[...] = jnp.zeros_like(ext)

    @pl.when(k < col_steps)
    def _():
        out, coarse = cells(after_ref[...])
        bo_ref[...] = jnp.swapaxes(out.reshape(PER, rows, out.shape[1]), 0, 1)
        at = pl.multiple_of(k * PER, PER)
        ext[1 : rows + 1, pl.ds(at, PER), :] = jnp.swapaxes(coarse.reshape(PER, rows, ch), 0, 1)

    @pl.when(k == col_steps)
    def _():
        _, coarse = cells(halo_ref[...])
        zero = jnp.float32(0.0)
        ext[0, 0:cols] = jnp.where(at_top, zero, coarse[0:cols])
        ext[rows + 1, 0:cols] = jnp.where(at_bottom, zero, coarse[cols : 2 * cols])
        left = coarse[2 * cols : 2 * cols + rows]
        right = coarse[2 * cols + rows : 2 * cols + 2 * rows]
        ext[1 : rows + 1, ring - 1 : ring, :] = jnp.where(at_left, zero, left).reshape(rows, 1, ch)
        ext[1 : rows + 1, cols : cols + 1, :] = jnp.where(at_right, zero, right).reshape(rows, 1, ch)
        for i, (dr, dc) in enumerate(CORNERS):
            at = 2 * cols + 2 * rows + i * PER + (PER - 1 if dc < 0 else 0)
            outside = (at_top if dr < 0 else at_bottom) | (at_left if dc < 0 else at_right)
            to_row = 0 if dr < 0 else rows + 1
            to_col = ring - 1 if dc < 0 else cols
            ext[to_row, to_col : to_col + 1, :] = jnp.where(outside, zero, coarse[at : at + 1])
        taps = [[k1_ref[y, x].astype(F32) for x in range(3)] for y in range(3)]
        none = jnp.zeros((ch, ch), F32)
        by_half = (
            ([taps[0][x] + taps[1][x] for x in range(3)], taps[2]),
            (taps[0], [taps[1][x] + taps[2][x] for x in range(3)]),
        )
        for half in range(2):
            for dy in range(2):
                t = by_half[half][dy]
                for b in range(2):
                    three = (t[0], t[1] + t[2], none) if b == 0 else (none, t[0] + t[1], t[2])
                    for dx in range(3):
                        w1[
                            (dy * 3 + dx) * ch : (dy * 3 + dx + 1) * ch,
                            (half * 2 + b) * ch : (half * 2 + b + 1) * ch,
                        ] = three[dx].astype(BF16)
        for dy in range(3):
            for s in range(4):
                for b in range(2):
                    w2[(dy * 4 + s) * ch : (dy * 4 + s + 1) * ch, b * ch : (b + 1) * ch] = (
                        k2_ref[dy, s - b] if 0 <= s - b <= 2 else none.astype(BF16)
                    )

        def widen(e, carry):
            x = ext[e]
            cat[e] = jnp.concatenate(
                [pltpu.roll(x, 1, 0), x, pltpu.roll(x, ring - 1, 0)], axis=1
            ).astype(BF16)
            return carry

        lax.fori_loop(0, erows, widen, 0)
        place = lax.broadcasted_iota(jnp.int32, (ring, 128), 0)
        col_keep = jnp.where(
            ((place == ring - 1) & at_left) | ((place == cols) & at_right), 0.0, 1.0
        )
        group = 3

        def first_conv(g, carry):
            e0 = g * group
            left = jnp.concatenate(
                [
                    jnp.concatenate([cat[e0 + i], cat[e0 + i + 1]], axis=1)
                    for i in range(group)
                ],
                axis=0,
            )
            y = silu(dot(left, w1[...]))
            for i in range(group):
                for half in range(2):
                    f = 2 * (e0 + i) + half
                    outside = ((f == 0) & at_top) | ((f == 2 * pairs - 1) & at_bottom)
                    keep = jnp.where(outside, 0.0, 1.0) * col_keep
                    f0 = y[i * ring : (i + 1) * ring, (2 * half) * ch : (2 * half + 1) * ch] * keep
                    f1 = y[i * ring : (i + 1) * ring, (2 * half + 1) * ch : (2 * half + 2) * ch] * keep
                    fine[f] = jnp.concatenate(
                        [pltpu.roll(f1, 1, 0), f0, f1, pltpu.roll(f0, ring - 1, 0)], axis=1
                    ).astype(BF16)
            return carry

        lax.fori_loop(0, pairs // group, first_conv, 0)

    @pl.when(k > col_steps)
    def _():
        m = k - col_steps - 1
        y0 = m * fine_step
        left = jnp.concatenate(
            [
                jnp.concatenate([fine[y0 + i + dy, 0:cols] for dy in range(3)], axis=1)
                for i in range(fine_step)
            ],
            axis=0,
        )
        second = dot(left, w2[...])
        for i in range(fine_step):
            up = ext[m * (fine_step // 2) + i // 2 + 1, 0:cols]
            for b in range(2):
                img_ref[i, pl.ds(b, cols, stride=2), :] = (
                    second[i * cols : (i + 1) * cols, b * ch : (b + 1) * ch] + up
                )


def back_call(after, halo, g3, win, wout, wp, k1, k2, rows, cols):
    width = after.shape[1]
    ch = wp.shape[1]
    tile = rows * PER
    col_steps = cols // PER
    ring = cols + 16
    fine_step = 8
    return pl.pallas_call(
        functools.partial(back_kernel, col_steps),
        grid=(col_steps + 1 + 2 * rows // fine_step,),
        in_specs=[pl.BlockSpec((tile, width), lambda i: (jnp.minimum(i, col_steps - 1), 0))]
        + [full(x.shape) for x in (halo, g3, win, wout, wp, k1, k2)],
        out_specs=[
            pl.BlockSpec((rows, PER, width), lambda i: (0, jnp.minimum(i, col_steps - 1), 0)),
            pl.BlockSpec(
                (fine_step, 2 * cols, ch), lambda i: (jnp.maximum(i - col_steps - 1, 0), 0, 0)
            ),
        ],
        out_shape=[
            jax.ShapeDtypeStruct((rows, cols, width), F32),
            jax.ShapeDtypeStruct((2 * rows, 2 * cols, ch), F32),
        ],
        scratch_shapes=[
            pltpu.VMEM((rows + 2, ring, ch), F32),
            pltpu.VMEM((6 * ch, 4 * ch), BF16),
            pltpu.VMEM((12 * ch, 2 * ch), BF16),
            pltpu.VMEM((rows + 2, ring, 3 * ch), BF16),
            pltpu.VMEM((2 * rows + 2, ring, 4 * ch), BF16),
        ],
        compiler_params=pltpu.CompilerParams(vmem_limit_bytes=VMEM_LIMIT),
        name="back",
    )(after, halo, g3, win, wout, wp, k1, k2)


def per_device(
    codes, starts, embed, gain_one, row_qkv, row_out, gain_two, col_qkv, col_out,
    gain_three, mlp_in, mlp_out, project, conv_one, conv_two,
):
    rows, cols = codes.shape
    wide = jnp.pad(codes, ((0, 0), (0, 128 - cols)))
    my_starts = lax.dynamic_slice_in_dim(starts, lax.axis_index("row") * rows, rows)
    my_starts = jnp.pad(my_starts, (HD, 128 - HD - rows))[None]
    after_col, halo = front_call(
        wide, my_starts, embed, gain_one[None], row_qkv, row_out, gain_two[None],
        col_qkv, col_out, cols,
    )
    return tuple(
        back_call(
            after_col, halo, gain_three[None], mlp_in, mlp_out, project, conv_one, conv_two,
            rows, cols,
        )
    )


def solution(mesh):
    in_specs = (P("row", "col"),) + (P(),) * 14
    out_specs = (P("row", "col", None), P("row", "col", None))
    return jax.shard_map(
        per_device, mesh=mesh, in_specs=in_specs, out_specs=out_specs, check_vma=False
    )
```

```python
import functools
import math
import jax
import jax.numpy as jnp
from jax import lax
from jax.experimental import pallas as pl
from jax.experimental.pallas import tpu as pltpu
from jax.sharding import PartitionSpec as P

HEADS = 8
HD = 64
EPS = 1e-06
NEGATIVE = -1e30
LOG2E = math.log2(math.e)
F32 = jnp.float32
BF16 = jnp.bfloat16
MESH = pl.DeviceIdType.MESH
VMEM_LIMIT = 56 * 1024 * 1024


def dot(left, right):
    return jnp.dot(left, right, preferred_element_type=F32)


def dot_t(left, right):
    return lax.dot_general(left, right, (((1,), (1,)), ((), ())), preferred_element_type=F32)


def norm_round(values, norm_gain):
    scale = lax.rsqrt(jnp.mean(values * values, axis=-1, keepdims=True) + EPS)
    return (values * scale * norm_gain).astype(BF16)


def silu(v):
    return v / (1.0 + jnp.exp(-v))


def lane_low(rows):
    return lax.broadcasted_iota(jnp.int32, (rows, 128), 1) < HD


PER = 8
AHEAD = 2


def row_setup(embed_ref, g1_ref, wqkv_ref, wcol_ref, qtab, kz, vz, tri, wq2, rows):
    vocab, width = embed_ref.shape
    tile = tri.shape[0]
    scale = (HD ** -0.5) * LOG2E
    normed = norm_round(embed_ref[...].astype(F32), g1_ref[...])
    low = lane_low(vocab)
    qtab[...] = (dot(normed, wqkv_ref[:, :width]) * scale).astype(BF16)
    keys = dot(normed, wqkv_ref[:, width : 2 * width])
    values = dot(normed, wqkv_ref[:, 2 * width :])
    for h in range(HEADS):
        p = h // 2
        mine = low if h % 2 == 0 else jnp.logical_not(low)
        sl = slice(p * 128, p * 128 + 128)
        kz[h] = jnp.where(mine, keys[:, sl], 0.0).astype(BF16)
        vz[h] = jnp.where(mine, values[:, sl], 1.0).astype(BF16)
    out_t = lax.broadcasted_iota(jnp.int32, (tile, tile), 0)
    in_t = lax.broadcasted_iota(jnp.int32, (tile, tile), 1)
    tri[...] = jnp.where(
        (out_t % rows == in_t % rows) & (in_t // rows <= out_t // rows), 1.0, 0.0
    ).astype(BF16)
    lowd = lane_low(width)
    for p in range(HEADS // 2):
        w = wcol_ref[:, p * 128 : p * 128 + 128].astype(F32)
        wq2[:, (2 * p) * 128 : (2 * p + 1) * 128] = jnp.where(lowd, w, 0.0).astype(BF16)
        wq2[:, (2 * p + 1) * 128 : (2 * p + 2) * 128] = jnp.where(
            lowd, pltpu.roll(w, HD, 1), 0.0
        ).astype(BF16)


def row_tile(k, codes_ref, embed_ref, wro_ref, g2_ref, wcol_ref, qtab, kz, vz, seen, tri, wq2):
    vocab, width = embed_ref.shape
    rows = codes_ref.shape[0]
    tile = tri.shape[0]
    scale = (HD ** -0.5) * LOG2E
    rolled = pltpu.roll(codes_ref[...], 128 - PER * k, 1)
    ids = lax.broadcasted_iota(jnp.int32, (rows, vocab), 1)
    one_hot = jnp.concatenate(
        [jnp.where(rolled[:, c : c + 1] == ids, 1.0, 0.0) for c in range(PER)], axis=0
    ).astype(BF16)
    counts = dot(tri[...], one_hot) + jnp.concatenate([seen[...]] * PER, axis=0)
    seen[...] = counts[tile - rows :]
    logn = jnp.where(counts > 0.5, jnp.log2(jnp.maximum(counts, 1.0)), NEGATIVE)
    emb = dot(one_hot, embed_ref[...])
    q = dot(one_hot, qtab[...]).astype(BF16)
    low = lane_low(tile)

    def scores(h):
        return dot_t(q[:, h // 2 * 128 : h // 2 * 128 + 128], kz[h]) + logn

    line = [scores(h) for h in range(AHEAD)]
    mixed, outs = [], []
    for h in range(HEADS):
        s = line.pop(0)
        if h + AHEAD < HEADS:
            line.append(scores(h + AHEAD))
        top = jnp.max(s, axis=-1, keepdims=True)
        e = jnp.exp2(s - top).astype(BF16)
        outs.append(dot(e, vz[h]))
        if h % 2:
            num = jnp.where(low, outs[0], outs[1])
            den = pltpu.roll(jnp.where(low, outs[1], outs[0]), HD, 1)
            mixed.append((num / den).astype(BF16))
            outs = []
    after = emb + dot(jnp.concatenate(mixed, axis=1), wro_ref[...])
    normed = norm_round(after, g2_ref[...])
    q2 = dot(normed, wq2[...]) * scale
    lane = lax.broadcasted_iota(jnp.int32, (tile, 128), 1)
    row = lax.broadcasted_iota(jnp.int32, (tile, 128), 0) % rows
    mark = jnp.where(lane == HD + row, 1.0, 0.0)
    q2 = jnp.concatenate(
        [(q2[:, h * 128 : h * 128 + 128] + mark).astype(BF16) for h in range(HEADS)], axis=1
    )
    return after, q2, dot(normed, wcol_ref[:, width:]).astype(BF16)


def set_bias(bias, starts_ref, first, rows):
    lane = lax.broadcasted_iota(jnp.int32, bias.shape, 1)
    place = lax.broadcasted_iota(jnp.int32, bias.shape, 0)
    slot, line = place // rows, bias.shape[0] // rows // 2
    key_row = ((slot % line) * 2 + slot // line) * rows + place % rows
    query_row = first + lane - HD
    seen = (key_row <= query_row) & (key_row >= starts_ref[0:1, :])
    bias[...] = jnp.where((lane < HD) | seen, 0.0, NEGATIVE).astype(BF16)


def col_tile(q_of, kv_of, bias, mixed, rows, keys):
    low_f = jnp.where(lane_low(keys), 1.0, 0.0)
    low_k = low_f.astype(BF16)
    high_k = (1.0 - low_f).astype(BF16)
    low = lane_low(rows)

    def scores(c):
        kv = kv_of(c)
        q = q_of(c)
        q = jnp.concatenate([q[:, h * 128 : h * 128 + 128] for h in range(HEADS)], axis=0)
        return dot_t(q, kv * low_k + bias[...]), kv * high_k + low_k

    line = [scores(c) for c in range(AHEAD)]
    for c in range(PER):
        s, va = line.pop(0)
        if c + AHEAD < PER:
            line.append(scores(c + AHEAD))
        top = jnp.max(s, axis=-1, keepdims=True)
        e = jnp.exp2(s - top).astype(BF16)
        o = dot(e, va)
        for p in range(HEADS // 2):
            even = o[(2 * p) * rows : (2 * p + 1) * rows]
            odd = o[(2 * p + 1) * rows : (2 * p + 2) * rows]
            keep = jnp.where(low, even, odd)
            other = pltpu.roll(jnp.where(low, odd, even), HD, 1)
            num = jnp.where(low, other, keep)
            den = jnp.where(low, keep, other)
            mixed[c * rows : (c + 1) * rows, p * 128 : p * 128 + 128] = (num / den).astype(BF16)


PAIRED = (5, 8, 9, 10)
CORNERS = ((-1, -1), (-1, 1), (1, -1), (1, 1))


def front_kernel(
    row_count, col_count,
    codes_ref, starts_ref, embed_ref, g1_ref, wqkv_ref, wro_ref, g2_ref, wcol_ref, wco_ref,
    after_ref, halo_ref,
    qtab, kz, vz, seen, tri, wq2, bias, mixed, kv_all, q2_all, held, hist, edge,
    kv_send, kv_recv, hist_send, hist_recv, halo_send, halo_recv, out_sem,
):
    rows = codes_ref.shape[0]
    vocab, width = embed_ref.shape
    slots, cols = kv_all.shape[0], kv_all.shape[1]
    keys = slots * rows
    tile = PER * rows
    chunks = cols // PER
    my_row, my_col = lax.axis_index("row"), lax.axis_index("col")

    half = row_count // 4

    def sibling(r):
        return r + 1 - 2 * lax.rem(r, 2)

    def across(r):
        return r + 2 - 4 * lax.rem(lax.div(r, 2), 2)

    def turned(r, steps):
        return lax.rem(r + 4 * steps, row_count)

    sib, beyond = sibling(my_row), across(my_row)
    down, up = turned(my_row, 1), turned(my_row, half - 1)
    far = turned(my_row, 2)

    halo_ref[...] = jnp.zeros_like(halo_ref)
    def row_by(dr):
        return lax.rem(my_row + dr + row_count, row_count)

    barrier = pltpu.get_barrier_semaphore()
    other = row_by(2 * lax.rem(my_row, 2) - 1)
    peers = [{"row": r, "col": my_col} for r in (sib, beyond, down, up, other)]
    for d in range(1, col_count):
        peers.append({"row": my_row, "col": lax.rem(my_col + d, col_count)})
    for dr, dc in CORNERS:
        peers.append({"row": row_by(dr), "col": lax.rem(my_col + dc + col_count, col_count)})
    for peer in peers:
        pl.semaphore_signal(barrier, 1, device_id=peer, device_id_type=MESH)

    def there(dr, dc):
        ok = None
        for at, step, count in ((my_row, dr, row_count), (my_col, dc, col_count)):
            if step:
                t = at + step >= 0 if step < 0 else at + step < count
                ok = t if ok is None else ok & t
        return ok

    ids = lax.broadcasted_iota(jnp.int32, (rows, vocab), 1)
    codes = codes_ref[...]
    own = jnp.zeros((rows, vocab), F32)
    for c in range(cols):
        own = own + jnp.where(codes[:, c : c + 1] == ids, 1.0, 0.0)
    hist[my_col] = own.astype(BF16)

    pl.semaphore_wait(barrier, len(peers))

    def hist_copy(d, slot):
        return pltpu.make_async_remote_copy(
            src_ref=hist.at[slot], dst_ref=hist.at[slot],
            send_sem=hist_send.at[d], recv_sem=hist_recv.at[slot],
            device_id={"col": lax.rem(my_col + d, col_count)}, device_id_type=MESH,
        )

    for d in range(1, col_count):
        hist_copy(d, my_col).start()

    row_setup(embed_ref, g1_ref, wqkv_ref, wcol_ref, qtab, kz, vz, tri, wq2, rows)
    set_bias(bias, starts_ref, my_row * rows, rows)

    for d in range(1, col_count):
        hist_copy(d, lax.rem(my_col + d, col_count)).wait_recv()
    base = jnp.zeros((rows, vocab), F32)
    for c in range(col_count):
        base = base + jnp.where(c < my_col, 1.0, 0.0) * hist[c].astype(F32)
    seen[...] = base

    def slot_of(r):
        return lax.rem(r, 2) * (slots // 2) + lax.div(r, 2)

    def kv_copy(n, k, r, dest):
        paired = n in PAIRED
        slot = slot_of(r)
        if paired:
            slot = slot - lax.rem(slot, 2)
        part = kv_all.at[pl.ds(slot, 2 if paired else 1), pl.ds(k * PER, PER)]
        sem = slots + lax.div(slot, 2) if paired else slot
        return pltpu.make_async_remote_copy(
            src_ref=part, dst_ref=part,
            send_sem=kv_send.at[n, k], recv_sem=kv_recv.at[sem, k],
            device_id={"row": dest}, device_id_type=MESH,
        )

    def arrived(k, r, n=0):
        kv_copy(n, k, r, sib).wait_recv()

    up_beyond, down_beyond, far_beyond = across(up), across(down), across(far)

    def relay(s):
        k1 = s - 2

        @pl.when((k1 >= 0) & (k1 < chunks))
        def _():
            arrived(k1, beyond)
            kv_copy(3, k1, beyond, down).start()
            kv_copy(4, k1, beyond, up).start()
            kv_copy(5, k1, my_row, sib).start()
            arrived(k1, up)
            arrived(k1, down)
            even = lax.rem(k1, 2) == 0

            @pl.when(even)
            def _():
                kv_copy(6, k1, up, down).start()

            @pl.when(jnp.logical_not(even))
            def _():
                kv_copy(6, k1, down, up).start()

        mid = chunks // 2
        k2 = jnp.where(s < mid + 4, s - 3, s - 4)

        @pl.when((k2 >= 0) & (k2 < chunks) & (s != mid + 4))
        def _():
            arrived(k2, far)
            kv_copy(7, k2, far, beyond).start()
            arrived(k2, up_beyond)
            kv_copy(8, k2, up, sib).start()
            arrived(k2, down_beyond)
            kv_copy(9, k2, down, sib).start()

        k3 = s - 5

        @pl.when((k3 >= 0) & (k3 < chunks))
        def _():
            arrived(k3, far_beyond)
            kv_copy(10, k3, far, sib).start()

    def row_step(k, carry):
        relay(k)
        after, q2, kv = row_tile(
            k, codes_ref, embed_ref, wro_ref, g2_ref, wcol_ref, qtab, kz, vz, seen, tri, wq2
        )
        kv_all[slot_of(my_row), pl.ds(k * PER, PER)] = kv.reshape(PER, rows, 2 * HD)
        kv_copy(0, k, my_row, beyond).start()
        kv_copy(1, k, my_row, down).start()
        kv_copy(2, k, my_row, up).start()
        held[pl.ds(k * tile, tile)] = after
        q2_all[pl.ds(k * PER, PER)] = q2.reshape(PER, rows, 2 * width)
        return carry

    lax.fori_loop(0, chunks, row_step, 0)

    def halo_copy(sem, src, at, size, dr, dc):
        return pltpu.make_async_remote_copy(
            src_ref=src, dst_ref=halo_ref.at[pl.ds(at, size)],
            send_sem=halo_send.at[sem], recv_sem=halo_recv.at[sem],
            device_id={"row": my_row + dr, "col": my_col + dc}, device_id_type=MESH,
        )

    left_at, corner_at = 2 * cols, 2 * cols + 2 * rows
    side_sem = 2 * chunks

    def edge_copy(which, k, dr):
        at = cols if which == 0 else 0
        return halo_copy(
            which * chunks + k, edge.at[which, pl.ds(k * PER, PER)], at + k * PER, PER, dr, 0
        )

    def side_copy(which, dc):
        c = 0 if which == 0 else cols - 1
        at = left_at + rows if which == 0 else left_at
        return halo_copy(side_sem + which, held.at[pl.ds(c * rows, rows)], at, rows, 0, dc)

    def corner_copy(i, dr, dc):
        k = 0 if dc < 0 else chunks - 1
        at = corner_at + (len(CORNERS) - 1 - i) * PER
        return halo_copy(
            side_sem + 2 + i, edge.at[0 if dr < 0 else 1, pl.ds(k * PER, PER)], at, PER, dr, dc
        )

    def out_copy(k):
        return pltpu.make_async_copy(
            held.at[pl.ds(k * tile, tile)], after_ref.at[pl.ds(k * tile, tile)], out_sem.at[k]
        )

    def col_step(j, carry):
        relay(chunks + j)
        k = jnp.where(j < chunks - 2, j, 2 * chunks - 3 - j)
        for r in (my_row, up, down, far):
            arrived(k, sibling(r), PAIRED[0])
        col_tile(
            lambda c: q2_all[k * PER + c],
            lambda c: kv_all[:, k * PER + c].reshape(keys, 2 * HD),
            bias, mixed, rows, keys,
        )
        after = held[pl.ds(k * tile, tile)] + dot(mixed[...], wco_ref[...])
        held[pl.ds(k * tile, tile)] = after
        out_copy(k).start()
        grid = after.reshape(PER, rows, width)
        edge[0, pl.ds(k * PER, PER)] = grid[:, 0]
        edge[1, pl.ds(k * PER, PER)] = grid[:, rows - 1]

        @pl.when(there(-1, 0))
        def _():
            edge_copy(0, k, -1).start()

        @pl.when(there(1, 0))
        def _():
            edge_copy(1, k, 1).start()

        for which, dc in ((0, -1), (1, 1)):
            last = 0 if which == 0 else chunks - 1

            @pl.when(there(0, dc) & (k == last))
            def _():
                side_copy(which, dc).start()

        for i, (dr, dc) in enumerate(CORNERS):
            last = 0 if dc < 0 else chunks - 1

            @pl.when(there(dr, dc) & (k == last))
            def _():
                corner_copy(i, dr, dc).start()

        return carry

    lax.fori_loop(0, chunks, col_step, 0)

    for d in range(1, col_count):
        hist_copy(d, my_col).wait_send()

    def finish(k, carry):
        for n in range(kv_send.shape[0]):
            kv_copy(n, k, my_row, sib).wait_send()
        out_copy(k).wait()

        @pl.when(there(-1, 0))
        def _():
            edge_copy(0, k, -1).wait_send()
            edge_copy(1, k, -1).wait_recv()

        @pl.when(there(1, 0))
        def _():
            edge_copy(1, k, 1).wait_send()
            edge_copy(0, k, 1).wait_recv()

        return carry

    lax.fori_loop(0, chunks, finish, 0)
    for which, dc in ((0, -1), (1, 1)):
        @pl.when(there(0, dc))
        def _():
            side_copy(which, dc).wait_send()
            side_copy(1 - which, dc).wait_recv()
    for i, (dr, dc) in enumerate(CORNERS):
        @pl.when(there(dr, dc))
        def _():
            corner_copy(i, dr, dc).wait_send()
            corner_copy(len(CORNERS) - 1 - i, dr, dc).wait_recv()


def full(shape):
    return pl.BlockSpec(shape, lambda *_: (0,) * len(shape))


def front_call(codes, starts, embed, g1, wqkv, wro, g2, wcol, wco, cols):
    vocab, width = embed.shape
    rows = codes.shape[0]
    row_count, col_count = lax.axis_size("row"), lax.axis_size("col")
    tokens = rows * cols
    tile = rows * PER
    chunks = cols // PER
    halo = -(-(2 * cols + 2 * rows + 4 * PER) // tile) * tile
    dma = pltpu.SemaphoreType.DMA
    args = (codes, starts, embed, g1, wqkv, wro, g2, wcol, wco)
    return pl.pallas_call(
        functools.partial(front_kernel, row_count, col_count),
        in_specs=[pl.BlockSpec(memory_space=pltpu.VMEM)] * len(args),
        out_specs=[
            pl.BlockSpec(memory_space=pl.ANY),
            pl.BlockSpec(memory_space=pltpu.VMEM),
        ],
        out_shape=[
            jax.ShapeDtypeStruct((tokens, width), F32),
            jax.ShapeDtypeStruct((halo, width), F32),
        ],
        scratch_shapes=[
            pltpu.VMEM((vocab, width), BF16),
            pltpu.VMEM((HEADS, vocab, 128), BF16),
            pltpu.VMEM((HEADS, vocab, 128), BF16),
            pltpu.VMEM((rows, vocab), F32),
            pltpu.VMEM((tile, tile), BF16),
            pltpu.VMEM((width, 2 * width), BF16),
            pltpu.VMEM((row_count * rows, 128), BF16),
            pltpu.VMEM((tile, width), BF16),
            pltpu.VMEM((row_count, cols, rows, 2 * HD), BF16),
            pltpu.VMEM((cols, rows, 2 * width), BF16),
            pltpu.VMEM((tokens, width), F32),
            pltpu.VMEM((col_count, rows, vocab), BF16),
            pltpu.VMEM((2, cols, width), F32),
            dma((11, chunks)),
            dma((row_count + row_count // 2, chunks)),
            dma((col_count,)),
            dma((col_count,)),
            dma((2 * chunks + 6,)),
            dma((2 * chunks + 6,)),
            dma((chunks,)),
        ],
        compiler_params=pltpu.CompilerParams(
            vmem_limit_bytes=VMEM_LIMIT, collective_id=0, has_side_effects=True
        ),
        name="front",
    )(*args)


def back_kernel(
    col_steps,
    after_ref, halo_ref, g3_ref, win_ref, wout_ref, wp_ref, k1_ref, k2_ref,
    bo_ref, img_ref,
    ext, w1, w2, cat, fine,
):
    k = pl.program_id(0)
    erows, ring, ch = ext.shape
    rows = erows - 2
    pairs = erows - 1
    cols = img_ref.shape[1] // 2
    fine_step = img_ref.shape[0]
    my_row, my_col = lax.axis_index("row"), lax.axis_index("col")
    at_top, at_bottom = my_row == 0, my_row == lax.axis_size("row") - 1
    at_left, at_right = my_col == 0, my_col == lax.axis_size("col") - 1

    def cells(after):
        normed = norm_round(after, g3_ref[...])
        inner = silu(dot(normed, win_ref[...])).astype(BF16)
        out = after + dot(inner, wout_ref[...])
        coarse = dot(out.astype(BF16), wp_ref[...]).astype(BF16).astype(F32)
        return out, coarse

    @pl.when(k == 0)
    def _():
        ext[...] = jnp.zeros_like(ext)

    @pl.when(k < col_steps)
    def _():
        out, coarse = cells(after_ref[...])
        bo_ref[...] = jnp.swapaxes(out.reshape(PER, rows, out.shape[1]), 0, 1)
        at = pl.multiple_of(k * PER, PER)
        ext[1 : rows + 1, pl.ds(at, PER), :] = jnp.swapaxes(coarse.reshape(PER, rows, ch), 0, 1)

    @pl.when(k == col_steps)
    def _():
        _, coarse = cells(halo_ref[...])
        zero = jnp.float32(0.0)
        ext[0, 0:cols] = jnp.where(at_top, zero, coarse[0:cols])
        ext[rows + 1, 0:cols] = jnp.where(at_bottom, zero, coarse[cols : 2 * cols])
        left = coarse[2 * cols : 2 * cols + rows]
        right = coarse[2 * cols + rows : 2 * cols + 2 * rows]
        ext[1 : rows + 1, ring - 1 : ring, :] = jnp.where(at_left, zero, left).reshape(rows, 1, ch)
        ext[1 : rows + 1, cols : cols + 1, :] = jnp.where(at_right, zero, right).reshape(rows, 1, ch)
        for i, (dr, dc) in enumerate(CORNERS):
            at = 2 * cols + 2 * rows + i * PER + (PER - 1 if dc < 0 else 0)
            outside = (at_top if dr < 0 else at_bottom) | (at_left if dc < 0 else at_right)
            to_row = 0 if dr < 0 else rows + 1
            to_col = ring - 1 if dc < 0 else cols
            ext[to_row, to_col : to_col + 1, :] = jnp.where(outside, zero, coarse[at : at + 1])
        taps = [[k1_ref[y, x].astype(F32) for x in range(3)] for y in range(3)]
        none = jnp.zeros((ch, ch), F32)
        by_half = (
            ([taps[0][x] + taps[1][x] for x in range(3)], taps[2]),
            (taps[0], [taps[1][x] + taps[2][x] for x in range(3)]),
        )
        for half in range(2):
            for dy in range(2):
                t = by_half[half][dy]
                for b in range(2):
                    three = (t[0], t[1] + t[2], none) if b == 0 else (none, t[0] + t[1], t[2])
                    for dx in range(3):
                        w1[
                            (dy * 3 + dx) * ch : (dy * 3 + dx + 1) * ch,
                            (half * 2 + b) * ch : (half * 2 + b + 1) * ch,
                        ] = three[dx].astype(BF16)
        for dy in range(3):
            for s in range(4):
                for b in range(2):
                    w2[(dy * 4 + s) * ch : (dy * 4 + s + 1) * ch, b * ch : (b + 1) * ch] = (
                        k2_ref[dy, s - b] if 0 <= s - b <= 2 else none.astype(BF16)
                    )

        def widen(e, carry):
            x = ext[e]
            cat[e] = jnp.concatenate(
                [pltpu.roll(x, 1, 0), x, pltpu.roll(x, ring - 1, 0)], axis=1
            ).astype(BF16)
            return carry

        lax.fori_loop(0, erows, widen, 0)
        place = lax.broadcasted_iota(jnp.int32, (ring, 128), 0)
        col_keep = jnp.where(
            ((place == ring - 1) & at_left) | ((place == cols) & at_right), 0.0, 1.0
        )
        group = 3

        def first_conv(g, carry):
            e0 = g * group
            left = jnp.concatenate(
                [
                    jnp.concatenate([cat[e0 + i], cat[e0 + i + 1]], axis=1)
                    for i in range(group)
                ],
                axis=0,
            )
            y = silu(dot(left, w1[...]))
            for i in range(group):
                for half in range(2):
                    f = 2 * (e0 + i) + half
                    outside = ((f == 0) & at_top) | ((f == 2 * pairs - 1) & at_bottom)
                    keep = jnp.where(outside, 0.0, 1.0) * col_keep
                    f0 = y[i * ring : (i + 1) * ring, (2 * half) * ch : (2 * half + 1) * ch] * keep
                    f1 = y[i * ring : (i + 1) * ring, (2 * half + 1) * ch : (2 * half + 2) * ch] * keep
                    fine[f] = jnp.concatenate(
                        [pltpu.roll(f1, 1, 0), f0, f1, pltpu.roll(f0, ring - 1, 0)], axis=1
                    ).astype(BF16)
            return carry

        lax.fori_loop(0, pairs // group, first_conv, 0)

    @pl.when(k > col_steps)
    def _():
        m = k - col_steps - 1
        y0 = m * fine_step
        left = jnp.concatenate(
            [
                jnp.concatenate([fine[y0 + i + dy, 0:cols] for dy in range(3)], axis=1)
                for i in range(fine_step)
            ],
            axis=0,
        )
        second = dot(left, w2[...])
        for i in range(fine_step):
            up = ext[m * (fine_step // 2) + i // 2 + 1, 0:cols]
            for b in range(2):
                img_ref[i, pl.ds(b, cols, stride=2), :] = (
                    second[i * cols : (i + 1) * cols, b * ch : (b + 1) * ch] + up
                )


def back_call(after, halo, g3, win, wout, wp, k1, k2, rows, cols):
    width = after.shape[1]
    ch = wp.shape[1]
    tile = rows * PER
    col_steps = cols // PER
    ring = cols + 16
    fine_step = 8
    return pl.pallas_call(
        functools.partial(back_kernel, col_steps),
        grid=(col_steps + 1 + 2 * rows // fine_step,),
        in_specs=[pl.BlockSpec((tile, width), lambda i: (jnp.minimum(i, col_steps - 1), 0))]
        + [full(x.shape) for x in (halo, g3, win, wout, wp, k1, k2)],
        out_specs=[
            pl.BlockSpec((rows, PER, width), lambda i: (0, jnp.minimum(i, col_steps - 1), 0)),
            pl.BlockSpec(
                (fine_step, 2 * cols, ch), lambda i: (jnp.maximum(i - col_steps - 1, 0), 0, 0)
            ),
        ],
        out_shape=[
            jax.ShapeDtypeStruct((rows, cols, width), F32),
            jax.ShapeDtypeStruct((2 * rows, 2 * cols, ch), F32),
        ],
        scratch_shapes=[
            pltpu.VMEM((rows + 2, ring, ch), F32),
            pltpu.VMEM((6 * ch, 4 * ch), BF16),
            pltpu.VMEM((12 * ch, 2 * ch), BF16),
            pltpu.VMEM((rows + 2, ring, 3 * ch), BF16),
            pltpu.VMEM((2 * rows + 2, ring, 4 * ch), BF16),
        ],
        compiler_params=pltpu.CompilerParams(vmem_limit_bytes=VMEM_LIMIT),
        name="back",
    )(after, halo, g3, win, wout, wp, k1, k2)


def per_device(
    codes, starts, embed, gain_one, row_qkv, row_out, gain_two, col_qkv, col_out,
    gain_three, mlp_in, mlp_out, project, conv_one, conv_two,
):
    rows, cols = codes.shape
    wide = jnp.pad(codes, ((0, 0), (0, 128 - cols)))
    my_starts = lax.dynamic_slice_in_dim(starts, lax.axis_index("row") * rows, rows)
    my_starts = jnp.pad(my_starts, (HD, 128 - HD - rows))[None]
    after_col, halo = front_call(
        wide, my_starts, embed, gain_one[None], row_qkv, row_out, gain_two[None],
        col_qkv, col_out, cols,
    )
    return tuple(
        back_call(
            after_col, halo, gain_three[None], mlp_in, mlp_out, project, conv_one, conv_two,
            rows, cols,
        )
    )


def solution(mesh):
    in_specs = (P("row", "col"),) + (P(),) * 14
    out_specs = (P("row", "col", None), P("row", "col", None))
    return jax.shard_map(
        per_device, mesh=mesh, in_specs=in_specs, out_specs=out_specs, check_vma=False
    )
```

```python
import functools
import math
import jax
import jax.numpy as jnp
from jax import lax
from jax.experimental import pallas as pl
from jax.experimental.pallas import tpu as pltpu
from jax.sharding import PartitionSpec as P

HEADS = 8
HD = 64
EPS = 1e-06
NEGATIVE = -1e30
LOG2E = math.log2(math.e)
F32 = jnp.float32
BF16 = jnp.bfloat16
MESH = pl.DeviceIdType.MESH
VMEM_LIMIT = 56 * 1024 * 1024


def dot(left, right):
    return jnp.dot(left, right, preferred_element_type=F32)


def dot_t(left, right):
    return lax.dot_general(left, right, (((1,), (1,)), ((), ())), preferred_element_type=F32)


def norm_round(values, norm_gain):
    scale = lax.rsqrt(jnp.mean(values * values, axis=-1, keepdims=True) + EPS)
    return (values * scale * norm_gain).astype(BF16)


def silu(v):
    return v / (1.0 + jnp.exp(-v))


def lane_low(rows):
    return lax.broadcasted_iota(jnp.int32, (rows, 128), 1) < HD


PER = 8
AHEAD = 2


def row_setup(embed_ref, g1_ref, wqkv_ref, wcol_ref, qtab, kz, vz, tri, wq2, rows):
    vocab, width = embed_ref.shape
    tile = tri.shape[0]
    scale = (HD ** -0.5) * LOG2E
    normed = norm_round(embed_ref[...].astype(F32), g1_ref[...])
    low = lane_low(vocab)
    qtab[...] = (dot(normed, wqkv_ref[:, :width]) * scale).astype(BF16)
    keys = dot(normed, wqkv_ref[:, width : 2 * width])
    values = dot(normed, wqkv_ref[:, 2 * width :])
    for h in range(HEADS):
        p = h // 2
        mine = low if h % 2 == 0 else jnp.logical_not(low)
        sl = slice(p * 128, p * 128 + 128)
        kz[h] = jnp.where(mine, keys[:, sl], 0.0).astype(BF16)
        vz[h] = jnp.where(mine, values[:, sl], 1.0).astype(BF16)
    out_t = lax.broadcasted_iota(jnp.int32, (tile, tile), 0)
    in_t = lax.broadcasted_iota(jnp.int32, (tile, tile), 1)
    tri[...] = jnp.where(
        (out_t % rows == in_t % rows) & (in_t // rows <= out_t // rows), 1.0, 0.0
    ).astype(BF16)
    lowd = lane_low(width)
    for p in range(HEADS // 2):
        w = wcol_ref[:, p * 128 : p * 128 + 128].astype(F32)
        wq2[:, (2 * p) * 128 : (2 * p + 1) * 128] = jnp.where(lowd, w, 0.0).astype(BF16)
        wq2[:, (2 * p + 1) * 128 : (2 * p + 2) * 128] = jnp.where(
            lowd, pltpu.roll(w, HD, 1), 0.0
        ).astype(BF16)


def row_tile(k, codes_ref, embed_ref, wro_ref, g2_ref, wcol_ref, qtab, kz, vz, seen, tri, wq2):
    vocab, width = embed_ref.shape
    rows = codes_ref.shape[0]
    tile = tri.shape[0]
    scale = (HD ** -0.5) * LOG2E
    codes = codes_ref[...]
    rolled = pltpu.roll(jnp.concatenate([codes, codes], axis=1), 128 - PER * k, 1)
    ids = lax.broadcasted_iota(jnp.int32, (rows, vocab), 1)
    one_hot = jnp.concatenate(
        [jnp.where(rolled[:, c : c + 1] == ids, 1.0, 0.0) for c in range(PER)], axis=0
    ).astype(BF16)
    counts = dot(tri[...], one_hot) + jnp.concatenate([seen[...]] * PER, axis=0)
    seen[...] = counts[tile - rows :]
    logn = jnp.where(counts > 0.5, jnp.log2(jnp.maximum(counts, 1.0)), NEGATIVE)
    emb = dot(one_hot, embed_ref[...])
    q = dot(one_hot, qtab[...]).astype(BF16)
    low = lane_low(tile)

    def scores(h):
        return dot_t(q[:, h // 2 * 128 : h // 2 * 128 + 128], kz[h]) + logn

    line = [scores(h) for h in range(AHEAD)]
    mixed, outs = [], []
    for h in range(HEADS):
        s = line.pop(0)
        if h + AHEAD < HEADS:
            line.append(scores(h + AHEAD))
        top = jnp.max(s, axis=-1, keepdims=True)
        e = jnp.exp2(s - top).astype(BF16)
        outs.append(dot(e, vz[h]))
        if h % 2:
            num = jnp.where(low, outs[0], outs[1])
            den = pltpu.roll(jnp.where(low, outs[1], outs[0]), HD, 1)
            mixed.append((num / den).astype(BF16))
            outs = []
    after = emb + dot(jnp.concatenate(mixed, axis=1), wro_ref[...])
    normed = norm_round(after, g2_ref[...])
    q2 = dot(normed, wq2[...]) * scale
    lane = lax.broadcasted_iota(jnp.int32, (tile, 128), 1)
    row = lax.broadcasted_iota(jnp.int32, (tile, 128), 0) % rows
    mark = jnp.where(lane == HD + row, 1.0, 0.0)
    q2 = jnp.concatenate(
        [(q2[:, h * 128 : h * 128 + 128] + mark).astype(BF16) for h in range(HEADS)], axis=1
    )
    return after, q2, dot(normed, wcol_ref[:, width:]).astype(BF16)


def set_bias(bias, starts_ref, first, rows):
    lane = lax.broadcasted_iota(jnp.int32, bias.shape, 1)
    place = lax.broadcasted_iota(jnp.int32, bias.shape, 0)
    slot, line = place // rows, bias.shape[0] // rows // 2
    key_row = ((slot % line) * 2 + slot // line) * rows + place % rows
    query_row = first + lane - HD
    turn = lax.rem(HD - first + starts_ref.shape[1], starts_ref.shape[1])
    here = pltpu.roll(jnp.broadcast_to(starts_ref[...], (8, starts_ref.shape[1])), turn, 1)
    seen = (key_row <= query_row) & (key_row >= here[0:1, :128])
    bias[...] = jnp.where((lane < HD) | seen, 0.0, NEGATIVE).astype(BF16)


def col_tile(q_of, kv_of, bias, mixed, at, rows, keys, between):
    low_f = jnp.where(lane_low(keys), 1.0, 0.0)
    low_k = low_f.astype(BF16)
    high_k = (1.0 - low_f).astype(BF16)
    low = lane_low(rows)

    def scores(c):
        kv = kv_of(c)
        q = q_of(c)
        q = jnp.concatenate([q[:, h * 128 : h * 128 + 128] for h in range(HEADS)], axis=0)
        return dot_t(q, kv * low_k + bias[...]), kv * high_k + low_k

    line = [scores(c) for c in range(AHEAD)]
    for c in range(PER):
        s, va = line.pop(0)
        if c + AHEAD < PER:
            line.append(scores(c + AHEAD))
        top = jnp.max(s, axis=-1, keepdims=True)
        e = jnp.exp2(s - top).astype(BF16)
        o = dot(e, va)
        for p in range(HEADS // 2):
            even = o[(2 * p) * rows : (2 * p + 1) * rows]
            odd = o[(2 * p + 1) * rows : (2 * p + 2) * rows]
            keep = jnp.where(low, even, odd)
            other = pltpu.roll(jnp.where(low, odd, even), HD, 1)
            num = jnp.where(low, other, keep)
            den = jnp.where(low, keep, other)
            mixed[at, c * rows : (c + 1) * rows, p * 128 : p * 128 + 128] = (num / den).astype(BF16)
        next(between, None)


def feed_forward(mix, before, wco, g3_ref, win, wout, wp, keep):
    after = before + dot(mix, wco[...])
    normed = norm_round(after, g3_ref[...])
    yield
    inner, quarter = [], win.shape[1] // 4
    for i in range(4):
        inner.append(silu(dot(normed, win[:, i * quarter : (i + 1) * quarter])).astype(BF16))
        yield
    out = after + dot(jnp.concatenate(inner, axis=1), wout[...])
    yield
    keep(out, dot(out.astype(BF16), wp[...]).astype(BF16).astype(F32))
    yield


CORNERS = ((-1, -1), (-1, 1), (1, -1), (1, 1))


def front_kernel(
    row_count, col_count,
    codes_ref, starts_ref, embed_ref, g1_ref, wqkv_ref, g2_ref, wcol_ref, g3_ref,
    wro_hbm, wco_hbm, win_hbm, wout_hbm, wp_hbm,
    bo_ref, co_ref, halo_ref,
    wro_ref, wco_ref, win_ref, wout_ref, wp_ref,
    qtab, kz, vz, seen, tri, wq2, bias, mixed, kv_all, q2_all, held, coarse_all, hist, edge,
    late_sem, kv_send, kv_recv, hist_send, hist_recv, halo_send, halo_recv, out_sem, co_sem,
):
    rows = codes_ref.shape[0]
    vocab, width = embed_ref.shape
    slots, cols = kv_all.shape[0], kv_all.shape[1]
    keys = slots * rows
    tile = PER * rows
    chunks = cols // PER
    my_row, my_col = lax.axis_index("row"), lax.axis_index("col")

    half = row_count // 4

    def sibling(r):
        return r + 1 - 2 * lax.rem(r, 2)

    def across(r):
        return r + 2 - 4 * lax.rem(lax.div(r, 2), 2)

    def turned(r, steps):
        return lax.rem(r + 4 * steps, row_count)

    sib, beyond = sibling(my_row), across(my_row)
    down, up = turned(my_row, 1), turned(my_row, half - 1)
    far = turned(my_row, 2)

    late = [
        pltpu.make_async_copy(hbm, ref, late_sem.at[i])
        for i, (hbm, ref) in enumerate(
            (
                (wro_hbm, wro_ref), (wco_hbm, wco_ref), (win_hbm, win_ref),
                (wout_hbm, wout_ref), (wp_hbm, wp_ref),
            )
        )
    ]
    for copy in late:
        copy.start()
    halo_ref[...] = jnp.zeros_like(halo_ref)
    def row_by(dr):
        return lax.rem(my_row + dr + row_count, row_count)

    barrier = pltpu.get_barrier_semaphore()
    other = row_by(2 * lax.rem(my_row, 2) - 1)
    peers = [{"row": r, "col": my_col} for r in (sib, beyond, down, up, other)]
    for d in range(1, col_count):
        peers.append({"row": my_row, "col": lax.rem(my_col + d, col_count)})
    for dr, dc in CORNERS:
        peers.append({"row": row_by(dr), "col": lax.rem(my_col + dc + col_count, col_count)})
    for peer in peers:
        pl.semaphore_signal(barrier, 1, device_id=peer, device_id_type=MESH)

    def there(dr, dc):
        ok = None
        for at, step, count in ((my_row, dr, row_count), (my_col, dc, col_count)):
            if step:
                t = at + step >= 0 if step < 0 else at + step < count
                ok = t if ok is None else ok & t
        return ok

    ids = lax.broadcasted_iota(jnp.int32, (rows, vocab), 1)
    codes = codes_ref[...]
    own = jnp.zeros((rows, vocab), F32)
    for c in range(cols):
        own = own + jnp.where(codes[:, c : c + 1] == ids, 1.0, 0.0)
    hist[my_col] = own.astype(BF16)

    pl.semaphore_wait(barrier, len(peers))

    def hist_copy(d, slot):
        return pltpu.make_async_remote_copy(
            src_ref=hist.at[slot], dst_ref=hist.at[slot],
            send_sem=hist_send.at[d], recv_sem=hist_recv.at[slot],
            device_id={"col": lax.rem(my_col + d, col_count)}, device_id_type=MESH,
        )

    for d in range(1, col_count):
        hist_copy(d, my_col).start()

    row_setup(embed_ref, g1_ref, wqkv_ref, wcol_ref, qtab, kz, vz, tri, wq2, rows)
    set_bias(bias, starts_ref, my_row * rows, rows)

    for d in range(1, col_count):
        hist_copy(d, lax.rem(my_col + d, col_count)).wait_recv()
    base = jnp.zeros((rows, vocab), F32)
    for c in range(col_count):
        base = base + jnp.where(c < my_col, 1.0, 0.0) * hist[c].astype(F32)
    seen[...] = base

    def slot_of(r):
        return lax.rem(r, 2) * (slots // 2) + lax.div(r, 2)

    def kv_copy(k, slot, size, stage, dest):
        part = kv_all.at[pl.ds(slot, size), pl.ds(k * PER, PER)]
        return pltpu.make_async_remote_copy(
            src_ref=part, dst_ref=part,
            send_sem=kv_send.at[k], recv_sem=kv_recv.at[stage, k],
            device_id={"row": dest}, device_id_type=MESH,
        )

    def send(k, r, stage, dest):
        kv_copy(k, slot_of(r), 1, stage, dest).start()

    def arrived(k, stage, size):
        kv_copy(k, 0, size, stage, sib).wait_recv()

    def relay(s):
        k1 = s - 2

        @pl.when((k1 >= 0) & (k1 < chunks))
        def _():
            arrived(k1, 0, 3)
            send(k1, beyond, 1, down)
            send(k1, beyond, 1, up)
            even = lax.rem(k1, 2) == 0

            @pl.when(even)
            def _():
                send(k1, up, 1, down)

            @pl.when(jnp.logical_not(even))
            def _():
                send(k1, down, 1, up)

        k2 = s - 4

        @pl.when((k2 >= 0) & (k2 < chunks))
        def _():
            arrived(k2, 1, 3)
            send(k2, far, 2, beyond)

        k3 = s - 6

        @pl.when((k3 >= 0) & (k3 < chunks))
        def _():
            arrived(k3, 2, 1)
            line = lax.rem(my_row, 2) * (slots // 2)
            kv_copy(k3, line, slots // 2, 3, sib).start()

    late[0].wait()

    def row_step(k, carry):
        relay(k)
        after, q2, kv = row_tile(
            k, codes_ref, embed_ref, wro_ref, g2_ref, wcol_ref, qtab, kz, vz, seen, tri, wq2
        )
        kv_all[slot_of(my_row), pl.ds(k * PER, PER)] = kv.reshape(PER, rows, 2 * HD)
        send(k, my_row, 0, beyond)
        send(k, my_row, 0, down)
        send(k, my_row, 0, up)
        held[k] = after.reshape(rows, PER, width)
        q2_all[pl.ds(k * PER, PER)] = q2.reshape(PER, rows, 2 * width)
        return carry

    lax.fori_loop(0, chunks, row_step, 0)

    def halo_copy(sem, src, at, size, dr, dc):
        return pltpu.make_async_remote_copy(
            src_ref=src, dst_ref=halo_ref.at[pl.ds(at, size)],
            send_sem=halo_send.at[sem], recv_sem=halo_recv.at[sem],
            device_id={"row": my_row + dr, "col": my_col + dc}, device_id_type=MESH,
        )

    left_at, corner_at = 2 * cols, 2 * cols + 2 * rows
    side_sem = 2 * chunks

    def edge_copy(which, k, dr):
        at = cols if which == 0 else 0
        return halo_copy(
            which * chunks + k, edge.at[which, pl.ds(k * PER, PER)], at + k * PER, PER, dr, 0
        )

    def side_copy(which, dc):
        c = 0 if which == 0 else cols - 1
        at = left_at + rows if which == 0 else left_at
        return halo_copy(side_sem + which, coarse_all.at[pl.ds(c * rows, rows)], at, rows, 0, dc)

    def corner_copy(i, dr, dc):
        k = 0 if dc < 0 else chunks - 1
        at = corner_at + (len(CORNERS) - 1 - i) * PER
        return halo_copy(
            side_sem + 2 + i, edge.at[0 if dr < 0 else 1, pl.ds(k * PER, PER)], at, PER, dr, dc
        )

    def out_copies(k):
        part = pl.ds(k * tile, tile)
        return (
            pltpu.make_async_copy(
                held.at[k], bo_ref.at[pl.ds(0, rows), pl.ds(k * PER, PER)], out_sem.at[k]
            ),
            pltpu.make_async_copy(coarse_all.at[part], co_ref.at[part], co_sem.at[k]),
        )

    def chunk_of(j):
        return jnp.where(j < chunks - 2, j, 2 * chunks - 3 - j)

    def feed(j):
        k = chunk_of(j)

        def keep(out, coarse):
            held[k] = jnp.swapaxes(out.reshape(PER, rows, width), 0, 1)
            coarse_all[pl.ds(k * tile, tile)] = coarse
            grid = coarse.reshape(PER, rows, coarse.shape[1])
            edge[0, pl.ds(k * PER, PER)] = grid[:, 0]
            edge[1, pl.ds(k * PER, PER)] = grid[:, rows - 1]

        return feed_forward(
            mixed[lax.rem(j, 2)], held[k].reshape(tile, width), wco_ref, g3_ref, win_ref,
            wout_ref, wp_ref, keep,
        )

    def pass_on(j):
        k = chunk_of(j)
        for copy in out_copies(k):
            copy.start()

        @pl.when(there(-1, 0))
        def _():
            edge_copy(0, k, -1).start()

        @pl.when(there(1, 0))
        def _():
            edge_copy(1, k, 1).start()

        for which, dc in ((0, -1), (1, 1)):
            last = 0 if which == 0 else chunks - 1

            @pl.when(there(0, dc) & (k == last))
            def _():
                side_copy(which, dc).start()

        for i, (dr, dc) in enumerate(CORNERS):
            last = 0 if dc < 0 else chunks - 1

            @pl.when(there(dr, dc) & (k == last))
            def _():
                corner_copy(i, dr, dc).start()

    def attend(j, between):
        relay(chunks + j)
        k = chunk_of(j)
        arrived(k, 3, slots // 2)
        col_tile(
            lambda c: q2_all[k * PER + c],
            lambda c: kv_all[:, k * PER + c].reshape(keys, 2 * HD),
            bias, mixed, lax.rem(j, 2), rows, keys, between,
        )
        for _ in between:
            pass

    def col_step(j, carry):
        attend(j, feed(j - 1))
        pass_on(j - 1)
        return carry

    attend(0, iter(()))
    for copy in late[1:]:
        copy.wait()
    lax.fori_loop(1, chunks, col_step, 0)
    for _ in feed(chunks - 1):
        pass
    pass_on(chunks - 1)

    for d in range(1, col_count):
        hist_copy(d, my_col).wait_send()

    def finish(k, carry):
        kv_copy(k, 0, 7 + slots // 2, 0, sib).wait_send()
        for copy in out_copies(k):
            copy.wait()

        @pl.when(there(-1, 0))
        def _():
            edge_copy(0, k, -1).wait_send()
            edge_copy(1, k, -1).wait_recv()

        @pl.when(there(1, 0))
        def _():
            edge_copy(1, k, 1).wait_send()
            edge_copy(0, k, 1).wait_recv()

        return carry

    lax.fori_loop(0, chunks, finish, 0)
    for which, dc in ((0, -1), (1, 1)):
        @pl.when(there(0, dc))
        def _():
            side_copy(which, dc).wait_send()
            side_copy(1 - which, dc).wait_recv()
    for i, (dr, dc) in enumerate(CORNERS):
        @pl.when(there(dr, dc))
        def _():
            corner_copy(i, dr, dc).wait_send()
            corner_copy(len(CORNERS) - 1 - i, dr, dc).wait_recv()


def full(shape):
    return pl.BlockSpec(shape, lambda *_: (0,) * len(shape))


def front_call(codes, starts, embed, g1, wqkv, g2, wcol, g3, wro, wco, win, wout, wp):
    vocab, width = embed.shape
    rows, cols = codes.shape
    ch = wp.shape[1]
    row_count, col_count = lax.axis_size("row"), lax.axis_size("col")
    tokens = rows * cols
    tile = rows * PER
    chunks = cols // PER
    halo = 2 * cols + 2 * rows + 4 * PER
    dma = pltpu.SemaphoreType.DMA
    early = (codes, starts, embed, g1, wqkv, g2, wcol, g3)
    late = (wro, wco, win, wout, wp)
    anywhere, vmem = pl.BlockSpec(memory_space=pl.ANY), pl.BlockSpec(memory_space=pltpu.VMEM)
    return pl.pallas_call(
        functools.partial(front_kernel, row_count, col_count),
        in_specs=[vmem] * len(early) + [anywhere] * len(late),
        out_specs=[anywhere, anywhere, vmem],
        out_shape=[
            jax.ShapeDtypeStruct((rows, cols, width), F32),
            jax.ShapeDtypeStruct((tokens, ch), F32),
            jax.ShapeDtypeStruct((halo, ch), F32),
        ],
        scratch_shapes=[pltpu.VMEM(x.shape, x.dtype) for x in late]
        + [
            pltpu.VMEM((vocab, width), BF16),
            pltpu.VMEM((HEADS, vocab, 128), BF16),
            pltpu.VMEM((HEADS, vocab, 128), BF16),
            pltpu.VMEM((rows, vocab), F32),
            pltpu.VMEM((tile, tile), BF16),
            pltpu.VMEM((width, 2 * width), BF16),
            pltpu.VMEM((row_count * rows, 128), BF16),
            pltpu.VMEM((2, tile, width), BF16),
            pltpu.VMEM((row_count, cols, rows, 2 * HD), BF16),
            pltpu.VMEM((cols, rows, 2 * width), BF16),
            pltpu.VMEM((chunks, rows, PER, width), F32),
            pltpu.VMEM((tokens, ch), F32),
            pltpu.VMEM((col_count, rows, vocab), BF16),
            pltpu.VMEM((2, cols, ch), F32),
            dma((len(late),)),
            dma((chunks,)),
            dma((4, chunks)),
            dma((col_count,)),
            dma((col_count,)),
            dma((2 * chunks + 6,)),
            dma((2 * chunks + 6,)),
            dma((chunks,)),
            dma((chunks,)),
        ],
        compiler_params=pltpu.CompilerParams(
            vmem_limit_bytes=VMEM_LIMIT, collective_id=0, has_side_effects=True
        ),
        name="front",
    )(*early, *late)


def back_kernel(bo_in, co_ref, halo_ref, k1_ref, k2_ref, bo_ref, img_ref, ext, w1, w2, cat, fine, hold, in_sem, out_sem):
    k = pl.program_id(0)
    erows, ring, ch = ext.shape
    rows = erows - 2
    pairs = erows - 1
    cols = img_ref.shape[1] // 2
    fine_step = img_ref.shape[0]
    my_row, my_col = lax.axis_index("row"), lax.axis_index("col")
    at_top, at_bottom = my_row == 0, my_row == lax.axis_size("row") - 1
    at_left, at_right = my_col == 0, my_col == lax.axis_size("col") - 1
    per = rows // in_sem.shape[0]

    def taken(i):
        part = pl.ds(i * per, per)
        return pltpu.make_async_copy(bo_in.at[part], hold.at[part], in_sem.at[i])

    def given(i):
        part = pl.ds(i * per, per)
        return pltpu.make_async_copy(hold.at[part], bo_ref.at[part], out_sem.at[i])

    @pl.when(k == 0)
    def _():
        for i in range(in_sem.shape[0]):
            taken(i).start()
        ext[...] = jnp.zeros_like(ext)
        for c in range(0, cols, PER):
            part = co_ref[c * rows : (c + PER) * rows].reshape(PER, rows, ch)
            ext[1 : rows + 1, c : c + PER, :] = jnp.swapaxes(part, 0, 1)
        coarse = halo_ref[...]
        zero = jnp.float32(0.0)
        ext[0, 0:cols] = jnp.where(at_top, zero, coarse[0:cols])
        ext[rows + 1, 0:cols] = jnp.where(at_bottom, zero, coarse[cols : 2 * cols])
        left = coarse[2 * cols : 2 * cols + rows]
        right = coarse[2 * cols + rows : 2 * cols + 2 * rows]
        ext[1 : rows + 1, ring - 1 : ring, :] = jnp.where(at_left, zero, left).reshape(rows, 1, ch)
        ext[1 : rows + 1, cols : cols + 1, :] = jnp.where(at_right, zero, right).reshape(rows, 1, ch)
        for i, (dr, dc) in enumerate(CORNERS):
            at = 2 * cols + 2 * rows + i * PER + (PER - 1 if dc < 0 else 0)
            outside = (at_top if dr < 0 else at_bottom) | (at_left if dc < 0 else at_right)
            to_row = 0 if dr < 0 else rows + 1
            to_col = ring - 1 if dc < 0 else cols
            ext[to_row, to_col : to_col + 1, :] = jnp.where(outside, zero, coarse[at : at + 1])
        taps = [[k1_ref[y, x].astype(F32) for x in range(3)] for y in range(3)]
        none = jnp.zeros((ch, ch), F32)
        by_half = (
            ([taps[0][x] + taps[1][x] for x in range(3)], taps[2]),
            (taps[0], [taps[1][x] + taps[2][x] for x in range(3)]),
        )
        for half in range(2):
            for dy in range(2):
                t = by_half[half][dy]
                for b in range(2):
                    three = (t[0], t[1] + t[2], none) if b == 0 else (none, t[0] + t[1], t[2])
                    for dx in range(3):
                        w1[
                            (dy * 3 + dx) * ch : (dy * 3 + dx + 1) * ch,
                            (half * 2 + b) * ch : (half * 2 + b + 1) * ch,
                        ] = three[dx].astype(BF16)
        for dy in range(3):
            for s in range(4):
                for b in range(2):
                    w2[(dy * 4 + s) * ch : (dy * 4 + s + 1) * ch, b * ch : (b + 1) * ch] = (
                        k2_ref[dy, s - b] if 0 <= s - b <= 2 else none.astype(BF16)
                    )

        def widen(e, carry):
            x = ext[e]
            cat[e] = jnp.concatenate(
                [pltpu.roll(x, 1, 0), x, pltpu.roll(x, ring - 1, 0)], axis=1
            ).astype(BF16)
            return carry

        lax.fori_loop(0, erows, widen, 0)
        place = lax.broadcasted_iota(jnp.int32, (ring, 128), 0)
        col_keep = jnp.where(
            ((place == ring - 1) & at_left) | ((place == cols) & at_right), 0.0, 1.0
        )
        group = 11

        def first_conv(g, carry):
            e0 = g * group
            left = jnp.concatenate(
                [
                    jnp.concatenate([cat[e0 + i], cat[e0 + i + 1]], axis=1)
                    for i in range(group)
                ],
                axis=0,
            )
            y = silu(dot(left, w1[...]))
            for i in range(group):
                for half in range(2):
                    f = 2 * (e0 + i) + half
                    outside = ((f == 0) & at_top) | ((f == 2 * pairs - 1) & at_bottom)
                    keep = jnp.where(outside, 0.0, 1.0) * col_keep
                    f0 = y[i * ring : (i + 1) * ring, (2 * half) * ch : (2 * half + 1) * ch] * keep
                    f1 = y[i * ring : (i + 1) * ring, (2 * half + 1) * ch : (2 * half + 2) * ch] * keep
                    fine[f] = jnp.concatenate(
                        [pltpu.roll(f1, 1, 0), f0, f1, pltpu.roll(f0, ring - 1, 0)], axis=1
                    ).astype(BF16)
            return carry

        lax.fori_loop(0, pairs // group, first_conv, 0)

    if True:
        m = k
        y0 = m * fine_step
        left = jnp.concatenate(
            [
                jnp.concatenate([fine[y0 + i + dy, 0:cols] for dy in range(3)], axis=1)
                for i in range(fine_step)
            ],
            axis=0,
        )
        second = dot(left, w2[...])
        for i in range(fine_step):
            up = ext[m * (fine_step // 2) + i // 2 + 1, 0:cols]
            for b in range(2):
                img_ref[i, pl.ds(b, cols, stride=2), :] = (
                    second[i * cols : (i + 1) * cols, b * ch : (b + 1) * ch] + up
                )
    taken(k).wait()
    given(k).start()

    @pl.when(k == pl.num_programs(0) - 1)
    def _():
        for i in range(in_sem.shape[0]):
            given(i).wait()


def back_call(block_out, coarse, halo, k1, k2):
    rows, cols, _ = block_out.shape
    ch = coarse.shape[1]
    ring = cols + 16
    fine_step = 16
    anywhere = pl.BlockSpec(memory_space=pl.ANY)
    return pl.pallas_call(
        back_kernel,
        grid=(2 * rows // fine_step,),
        in_specs=[anywhere] + [full(x.shape) for x in (coarse, halo, k1, k2)],
        out_specs=[anywhere, pl.BlockSpec((fine_step, 2 * cols, ch), lambda i: (i, 0, 0))],
        out_shape=[
            jax.ShapeDtypeStruct(block_out.shape, F32),
            jax.ShapeDtypeStruct((2 * rows, 2 * cols, ch), F32),
        ],
        scratch_shapes=[
            pltpu.VMEM((rows + 2, ring, ch), F32),
            pltpu.VMEM((6 * ch, 4 * ch), BF16),
            pltpu.VMEM((12 * ch, 2 * ch), BF16),
            pltpu.VMEM((rows + 2, ring, 3 * ch), BF16),
            pltpu.VMEM((2 * rows + 2, ring, 4 * ch), BF16),
            pltpu.VMEM(block_out.shape, F32),
            pltpu.SemaphoreType.DMA((2 * rows // fine_step,)),
            pltpu.SemaphoreType.DMA((2 * rows // fine_step,)),
        ],
        compiler_params=pltpu.CompilerParams(vmem_limit_bytes=VMEM_LIMIT),
        name="back",
    )(block_out, coarse, halo, k1, k2)


def per_device(
    codes, starts, embed, gain_one, row_qkv, row_out, gain_two, col_qkv, col_out,
    gain_three, mlp_in, mlp_out, project, conv_one, conv_two,
):
    block_out, coarse, halo = front_call(
        codes, starts[None], embed, gain_one[None], row_qkv, gain_two[None], col_qkv,
        gain_three[None], row_out, col_out, mlp_in, mlp_out, project,
    )
    return tuple(back_call(block_out, coarse, halo, conv_one, conv_two))


def solution(mesh):
    in_specs = (P("row", "col"),) + (P(),) * 14
    out_specs = (P("row", "col", None), P("row", "col", None))
    return jax.shard_map(
        per_device, mesh=mesh, in_specs=in_specs, out_specs=out_specs, check_vma=False
    )
```

```python
import functools
import math
import jax
import jax.numpy as jnp
from jax import lax
from jax.experimental import pallas as pl
from jax.experimental.pallas import tpu as pltpu
from jax.sharding import PartitionSpec as P

HEADS = 8
HD = 64
EPS = 1e-06
NEGATIVE = -1e30
LOG2E = math.log2(math.e)
F32 = jnp.float32
BF16 = jnp.bfloat16
MESH = pl.DeviceIdType.MESH
VMEM_LIMIT = 56 * 1024 * 1024


def dot(left, right):
    return jnp.dot(left, right, preferred_element_type=F32)


def dot_t(left, right):
    return lax.dot_general(left, right, (((1,), (1,)), ((), ())), preferred_element_type=F32)


def norm_round(values, norm_gain):
    scale = lax.rsqrt(jnp.mean(values * values, axis=-1, keepdims=True) + EPS)
    return (values * scale * norm_gain).astype(BF16)


def silu(v):
    h = 0.5 * v
    return h + h * jnp.tanh(h)


def lane_low(rows):
    return lax.broadcasted_iota(jnp.int32, (rows, 128), 1) < HD


PER = 8
AHEAD = 2


def row_setup(embed_ref, g1_ref, wqkv_ref, qtab, kz, vz, tri, rows):
    vocab, width = embed_ref.shape
    tile = tri.shape[0]
    scale = (HD ** -0.5) * LOG2E
    normed = norm_round(embed_ref[...].astype(F32), g1_ref[...])
    low = lane_low(vocab)
    qtab[...] = (dot(normed, wqkv_ref[:, :width]) * scale).astype(BF16)
    keys = dot(normed, wqkv_ref[:, width : 2 * width])
    values = dot(normed, wqkv_ref[:, 2 * width :])
    for h in range(HEADS):
        p = h // 2
        mine = low if h % 2 == 0 else jnp.logical_not(low)
        sl = slice(p * 128, p * 128 + 128)
        kz[h] = jnp.where(mine, keys[:, sl], 0.0).astype(BF16)
        vz[h] = jnp.where(mine, values[:, sl], 1.0).astype(BF16)
    out_t = lax.broadcasted_iota(jnp.int32, (tile, tile), 0)
    in_t = lax.broadcasted_iota(jnp.int32, (tile, tile), 1)
    tri[...] = jnp.where(
        (out_t % rows == in_t % rows) & (in_t // rows <= out_t // rows), 1.0, 0.0
    ).astype(BF16)


def row_tile(k, codes_ref, embed_ref, wro_ref, g2_ref, wcol_ref, qtab, kz, vz, seen, tri):
    vocab, width = embed_ref.shape
    rows = codes_ref.shape[0]
    tile = tri.shape[0]
    scale = (HD ** -0.5) * LOG2E
    codes = codes_ref[...]
    rolled = pltpu.roll(jnp.concatenate([codes, codes], axis=1), 128 - PER * k, 1)
    ids = lax.broadcasted_iota(jnp.int32, (rows, vocab), 1)
    one_hot = jnp.concatenate(
        [jnp.where(rolled[:, c : c + 1] == ids, 1.0, 0.0) for c in range(PER)], axis=0
    ).astype(BF16)
    counts = dot(tri[...], one_hot) + jnp.concatenate([seen[...]] * PER, axis=0)
    seen[...] = counts[tile - rows :]
    logn = jnp.where(counts > 0.5, jnp.log2(jnp.maximum(counts, 1.0)), NEGATIVE)
    emb = dot(one_hot, embed_ref[...])
    q = dot(one_hot, qtab[...]).astype(BF16)
    low = lane_low(tile)

    def scores(h):
        return dot_t(q[:, h // 2 * 128 : h // 2 * 128 + 128], kz[h]) + logn

    line = [scores(h) for h in range(AHEAD)]
    mixed, outs = [], []
    for h in range(HEADS):
        s = line.pop(0)
        if h + AHEAD < HEADS:
            line.append(scores(h + AHEAD))
        top = jnp.max(s, axis=-1, keepdims=True)
        e = jnp.exp2(s - top).astype(BF16)
        outs.append(dot(e, vz[h]))
        if h % 2:
            num = jnp.where(low, outs[0], outs[1])
            den = pltpu.roll(jnp.where(low, outs[1], outs[0]), HD, 1)
            mixed.append((num / den).astype(BF16))
            outs = []
    after = emb + dot(jnp.concatenate(mixed, axis=1), wro_ref[...])
    normed = norm_round(after, g2_ref[...])
    proj = dot(normed, wcol_ref[...])
    lane = lax.broadcasted_iota(jnp.int32, (tile, 128), 1)
    row = lax.broadcasted_iota(jnp.int32, (tile, 128), 0) % rows
    mark = jnp.where(lane == HD + row, 1.0, 0.0)
    q2 = []
    for p in range(HEADS // 2):
        pair = proj[:, p * 128 : p * 128 + 128] * scale
        q2.append(jnp.where(low, pair, mark).astype(BF16))
        q2.append(jnp.where(low, pltpu.roll(pair, HD, 1), mark).astype(BF16))
    return after, jnp.concatenate(q2, axis=1), proj[:, width:].astype(BF16)


def set_bias(bias, starts_ref, first, rows):
    lane = lax.broadcasted_iota(jnp.int32, bias.shape, 1)
    place = lax.broadcasted_iota(jnp.int32, bias.shape, 0)
    slot, line = place // rows, bias.shape[0] // rows // 2
    key_row = ((slot % line) * 2 + slot // line) * rows + place % rows
    query_row = first + lane - HD
    turn = lax.rem(HD - first + starts_ref.shape[1], starts_ref.shape[1])
    here = pltpu.roll(jnp.broadcast_to(starts_ref[...], (8, starts_ref.shape[1])), turn, 1)
    seen = (key_row <= query_row) & (key_row >= here[0:1, :128])
    bias[...] = jnp.where((lane < HD) | seen, 0.0, NEGATIVE).astype(BF16)


def col_tile(q_of, kv_of, bias, mixed, at, rows, keys, between):
    low_f = jnp.where(lane_low(keys), 1.0, 0.0)
    low_k = low_f.astype(BF16)
    high_k = (1.0 - low_f).astype(BF16)
    low = lane_low(rows)

    def scores(c):
        kv = kv_of(c)
        q = q_of(c)
        q = jnp.concatenate([q[:, h * 128 : h * 128 + 128] for h in range(HEADS)], axis=0)
        return dot_t(q, kv * low_k + bias[...]), kv * high_k + low_k

    line = [scores(c) for c in range(AHEAD)]
    for c in range(PER):
        s, va = line.pop(0)
        if c + AHEAD < PER:
            line.append(scores(c + AHEAD))
        top = jnp.max(s, axis=-1, keepdims=True)
        e = jnp.exp2(s - top).astype(BF16)
        o = dot(e, va)
        for p in range(HEADS // 2):
            even = o[(2 * p) * rows : (2 * p + 1) * rows]
            odd = o[(2 * p + 1) * rows : (2 * p + 2) * rows]
            keep = jnp.where(low, even, odd)
            other = pltpu.roll(jnp.where(low, odd, even), HD, 1)
            num = jnp.where(low, other, keep)
            den = jnp.where(low, keep, other)
            mixed[at, c * rows : (c + 1) * rows, p * 128 : p * 128 + 128] = (num / den).astype(BF16)
        next(between, None)


def feed_forward(mix, before, wco, g3_ref, win, wout, wp, keep):
    after = before + dot(mix, wco[...])
    normed = norm_round(after, g3_ref[...])
    yield
    inner, quarter = [], win.shape[1] // 4
    for i in range(4):
        inner.append(silu(dot(normed, win[:, i * quarter : (i + 1) * quarter])).astype(BF16))
        yield
    out = after + dot(jnp.concatenate(inner, axis=1), wout[...])
    yield
    keep(out, dot(out.astype(BF16), wp[...]).astype(BF16).astype(F32))
    yield


CORNERS = ((-1, -1), (-1, 1), (1, -1), (1, 1))


def front_kernel(
    row_count, col_count,
    codes_ref, starts_ref, g1_ref, g2_ref, g3_ref,
    embed_hbm, wqkv_hbm, wcol_hbm, wro_hbm, wco_hbm, win_hbm, wout_hbm, wp_hbm,
    bo_ref, co_ref, halo_ref,
    embed_ref, wqkv_ref, wcol_ref, wro_ref, wco_ref, win_ref, wout_ref, wp_ref,
    qtab, kz, vz, seen, tri, bias, mixed, kv_all, q2_all, held, coarse_all, hist, edge,
    late_sem, kv_send, kv_recv, hist_send, hist_recv, halo_send, halo_recv, out_sem, co_sem,
):
    rows = codes_ref.shape[0]
    vocab, width = embed_hbm.shape
    slots, cols = kv_all.shape[0], kv_all.shape[1]
    keys = slots * rows
    tile = PER * rows
    chunks = cols // PER
    my_row, my_col = lax.axis_index("row"), lax.axis_index("col")

    half = row_count // 4

    def sibling(r):
        return r + 1 - 2 * lax.rem(r, 2)

    def across(r):
        return r + 2 - 4 * lax.rem(lax.div(r, 2), 2)

    def turned(r, steps):
        return lax.rem(r + 4 * steps, row_count)

    sib, beyond = sibling(my_row), across(my_row)
    down, up = turned(my_row, 1), turned(my_row, half - 1)
    far = turned(my_row, 2)

    halo_ref[...] = jnp.zeros_like(halo_ref)
    hist[...] = jnp.zeros_like(hist)
    def row_by(dr):
        return lax.rem(my_row + dr + row_count, row_count)

    barrier = pltpu.get_barrier_semaphore()
    other = row_by(2 * lax.rem(my_row, 2) - 1)
    peers = [{"row": r, "col": my_col} for r in (sib, beyond, down, up, other)]
    for d in range(1, col_count):
        peers.append({"row": my_row, "col": lax.rem(my_col + d, col_count)})
    for dr, dc in CORNERS:
        peers.append({"row": row_by(dr), "col": lax.rem(my_col + dc + col_count, col_count)})
    for peer in peers:
        pl.semaphore_signal(barrier, 1, device_id=peer, device_id_type=MESH)

    def there(dr, dc):
        ok = None
        for at, step, count in ((my_row, dr, row_count), (my_col, dc, col_count)):
            if step:
                t = at + step >= 0 if step < 0 else at + step < count
                ok = t if ok is None else ok & t
        return ok

    late = [
        pltpu.make_async_copy(hbm, ref, late_sem.at[i])
        for i, (hbm, ref) in enumerate(
            (
                (embed_hbm, embed_ref), (wqkv_hbm, wqkv_ref), (wcol_hbm, wcol_ref),
                (wro_hbm, wro_ref), (wco_hbm, wco_ref), (win_hbm, win_ref),
                (wout_hbm, wout_ref), (wp_hbm, wp_ref),
            )
        )
    ]
    for copy in late:
        copy.start()

    ids = lax.broadcasted_iota(jnp.int32, (rows, vocab), 1)
    codes = codes_ref[...]
    own = jnp.zeros((rows, vocab), F32)
    for c in range(cols):
        own = own + jnp.where(codes[:, c : c + 1] == ids, 1.0, 0.0)
    hist[my_col] = own.astype(BF16)

    pl.semaphore_wait(barrier, len(peers))

    def hist_copy(d, slot):
        return pltpu.make_async_remote_copy(
            src_ref=hist.at[slot], dst_ref=hist.at[slot],
            send_sem=hist_send.at[d], recv_sem=hist_recv.at[slot],
            device_id={"col": lax.rem(my_col + d, col_count)}, device_id_type=MESH,
        )

    for d in range(1, col_count):
        @pl.when(my_col + d < col_count)
        def _():
            hist_copy(d, my_col).start()

    for copy in late[:2]:
        copy.wait()
    row_setup(embed_ref, g1_ref, wqkv_ref, qtab, kz, vz, tri, rows)

    for d in range(1, col_count):
        @pl.when(my_col >= d)
        def _():
            hist_copy(d, lax.rem(my_col - d + col_count, col_count)).wait_recv()
    base = jnp.zeros((rows, vocab), F32)
    for c in range(col_count):
        base = base + jnp.where(c < my_col, hist[c].astype(F32), 0.0)
    seen[...] = base

    def slot_of(r):
        return lax.rem(r, 2) * (slots // 2) + lax.div(r, 2)

    def kv_copy(k, slot, size, stage, dest):
        part = kv_all.at[pl.ds(slot, size), pl.ds(k * PER, PER)]
        return pltpu.make_async_remote_copy(
            src_ref=part, dst_ref=part,
            send_sem=kv_send.at[k], recv_sem=kv_recv.at[stage, k],
            device_id={"row": dest}, device_id_type=MESH,
        )

    def send(k, r, stage, dest):
        kv_copy(k, slot_of(r), 1, stage, dest).start()

    def arrived(k, stage, size):
        kv_copy(k, 0, size, stage, sib).wait_recv()

    def relay(s):
        k1 = s - 3

        @pl.when((k1 >= 0) & (k1 < chunks))
        def _():
            arrived(k1, 0, 3)
            send(k1, beyond, 1, down)
            send(k1, beyond, 1, up)
            even = lax.rem(k1, 2) == 0

            @pl.when(even)
            def _():
                send(k1, up, 1, down)

            @pl.when(jnp.logical_not(even))
            def _():
                send(k1, down, 1, up)

        k2 = s - 5

        @pl.when((k2 >= 0) & (k2 < chunks))
        def _():
            arrived(k2, 1, 3)
            send(k2, far, 2, beyond)

        k3 = s - 7

        @pl.when((k3 >= 0) & (k3 < chunks))
        def _():
            arrived(k3, 2, 1)
            line = lax.rem(my_row, 2) * (slots // 2)
            kv_copy(k3, line, slots // 2, 3, sib).start()

    for copy in late[2:4]:
        copy.wait()

    def row_step(k, carry):
        relay(k)
        after, q2, kv = row_tile(
            k, codes_ref, embed_ref, wro_ref, g2_ref, wcol_ref, qtab, kz, vz, seen, tri
        )
        kv_all[slot_of(my_row), pl.ds(k * PER, PER)] = kv.reshape(PER, rows, 2 * HD)
        send(k, my_row, 0, beyond)
        send(k, my_row, 0, down)
        send(k, my_row, 0, up)
        held[k] = after.reshape(rows, PER, width)
        q2_all[pl.ds(k * PER, PER)] = q2.reshape(PER, rows, 2 * width)
        return carry

    lax.fori_loop(0, chunks, row_step, 0)

    def halo_copy(sem, src, at, size, dr, dc):
        return pltpu.make_async_remote_copy(
            src_ref=src, dst_ref=halo_ref.at[pl.ds(at, size)],
            send_sem=halo_send.at[sem], recv_sem=halo_recv.at[sem],
            device_id={"row": my_row + dr, "col": my_col + dc}, device_id_type=MESH,
        )

    left_at, corner_at = 2 * cols, 2 * cols + 2 * rows
    side_sem = 2 * chunks

    def edge_copy(which, k, dr):
        at = cols if which == 0 else 0
        return halo_copy(
            which * chunks + k, edge.at[which, pl.ds(k * PER, PER)], at + k * PER, PER, dr, 0
        )

    def side_copy(which, dc):
        c = 0 if which == 0 else cols - 1
        at = left_at + rows if which == 0 else left_at
        return halo_copy(side_sem + which, coarse_all.at[pl.ds(c * rows, rows)], at, rows, 0, dc)

    def corner_copy(i, dr, dc):
        k = 0 if dc < 0 else chunks - 1
        at = corner_at + (len(CORNERS) - 1 - i) * PER
        return halo_copy(
            side_sem + 2 + i, edge.at[0 if dr < 0 else 1, pl.ds(k * PER, PER)], at, PER, dr, dc
        )

    def out_copies(k):
        part = pl.ds(k * tile, tile)
        return (
            pltpu.make_async_copy(
                held.at[k], bo_ref.at[pl.ds(0, rows), pl.ds(k * PER, PER)], out_sem.at[k]
            ),
            pltpu.make_async_copy(coarse_all.at[part], co_ref.at[part], co_sem.at[k]),
        )

    def chunk_of(j):
        return j

    def feed(j):
        k = chunk_of(j)

        def keep(out, coarse):
            held[k] = jnp.swapaxes(out.reshape(PER, rows, width), 0, 1)
            coarse_all[pl.ds(k * tile, tile)] = coarse
            grid = coarse.reshape(PER, rows, coarse.shape[1])
            edge[0, pl.ds(k * PER, PER)] = grid[:, 0]
            edge[1, pl.ds(k * PER, PER)] = grid[:, rows - 1]

        return feed_forward(
            mixed[lax.rem(j, 2)], held[k].reshape(tile, width), wco_ref, g3_ref, win_ref,
            wout_ref, wp_ref, keep,
        )

    def pass_on(j):
        k = chunk_of(j)
        for copy in out_copies(k):
            copy.start()

        @pl.when(there(-1, 0))
        def _():
            edge_copy(0, k, -1).start()

        @pl.when(there(1, 0))
        def _():
            edge_copy(1, k, 1).start()

        for which, dc in ((0, -1), (1, 1)):
            last = 0 if which == 0 else chunks - 1

            @pl.when(there(0, dc) & (k == last))
            def _():
                side_copy(which, dc).start()

        for i, (dr, dc) in enumerate(CORNERS):
            last = 0 if dc < 0 else chunks - 1

            @pl.when(there(dr, dc) & (k == last))
            def _():
                corner_copy(i, dr, dc).start()

    def attend(j, between):
        relay(chunks + j)
        k = chunk_of(j)
        arrived(k, 3, slots // 2)
        col_tile(
            lambda c: q2_all[k * PER + c],
            lambda c: kv_all[:, k * PER + c].reshape(keys, 2 * HD),
            bias, mixed, lax.rem(j, 2), rows, keys, between,
        )
        for _ in between:
            pass

    def col_step(j, carry):
        attend(j, feed(j - 1))
        pass_on(j - 1)
        return carry

    set_bias(bias, starts_ref, my_row * rows, rows)
    attend(0, iter(()))
    for copy in late[4:]:
        copy.wait()
    lax.fori_loop(1, chunks, col_step, 0)
    for _ in feed(chunks - 1):
        pass
    pass_on(chunks - 1)

    for d in range(1, col_count):
        @pl.when(my_col + d < col_count)
        def _():
            hist_copy(d, my_col).wait_send()

    def finish(k, carry):
        kv_copy(k, 0, 7 + slots // 2, 0, sib).wait_send()
        for copy in out_copies(k):
            copy.wait()

        @pl.when(there(-1, 0))
        def _():
            edge_copy(0, k, -1).wait_send()
            edge_copy(1, k, -1).wait_recv()

        @pl.when(there(1, 0))
        def _():
            edge_copy(1, k, 1).wait_send()
            edge_copy(0, k, 1).wait_recv()

        return carry

    lax.fori_loop(0, chunks, finish, 0)
    for which, dc in ((0, -1), (1, 1)):
        @pl.when(there(0, dc))
        def _():
            side_copy(which, dc).wait_send()
            side_copy(1 - which, dc).wait_recv()
    for i, (dr, dc) in enumerate(CORNERS):
        @pl.when(there(dr, dc))
        def _():
            corner_copy(i, dr, dc).wait_send()
            corner_copy(len(CORNERS) - 1 - i, dr, dc).wait_recv()


def full(shape):
    return pl.BlockSpec(shape, lambda *_: (0,) * len(shape))


def front_call(codes, starts, embed, g1, wqkv, g2, wcol, g3, wro, wco, win, wout, wp):
    vocab, width = embed.shape
    rows, cols = codes.shape
    ch = wp.shape[1]
    row_count, col_count = lax.axis_size("row"), lax.axis_size("col")
    tokens = rows * cols
    tile = rows * PER
    chunks = cols // PER
    halo = 2 * cols + 2 * rows + 4 * PER
    dma = pltpu.SemaphoreType.DMA
    early = (codes, starts, g1, g2, g3)
    late = (embed, wqkv, wcol, wro, wco, win, wout, wp)
    anywhere, vmem = pl.BlockSpec(memory_space=pl.ANY), pl.BlockSpec(memory_space=pltpu.VMEM)
    return pl.pallas_call(
        functools.partial(front_kernel, row_count, col_count),
        in_specs=[vmem] * len(early) + [anywhere] * len(late),
        out_specs=[anywhere, anywhere, vmem],
        out_shape=[
            jax.ShapeDtypeStruct((rows, cols, width), F32),
            jax.ShapeDtypeStruct((tokens, ch), F32),
            jax.ShapeDtypeStruct((halo, ch), F32),
        ],
        scratch_shapes=[pltpu.VMEM(x.shape, x.dtype) for x in late]
        + [
            pltpu.VMEM((vocab, width), BF16),
            pltpu.VMEM((HEADS, vocab, 128), BF16),
            pltpu.VMEM((HEADS, vocab, 128), BF16),
            pltpu.VMEM((rows, vocab), F32),
            pltpu.VMEM((tile, tile), BF16),
            pltpu.VMEM((row_count * rows, 128), BF16),
            pltpu.VMEM((2, tile, width), BF16),
            pltpu.VMEM((row_count, cols, rows, 2 * HD), BF16),
            pltpu.VMEM((cols, rows, 2 * width), BF16),
            pltpu.VMEM((chunks, rows, PER, width), F32),
            pltpu.VMEM((tokens, ch), F32),
            pltpu.VMEM((col_count, rows, vocab), BF16),
            pltpu.VMEM((2, cols, ch), F32),
            dma((len(late),)),
            dma((chunks,)),
            dma((4, chunks)),
            dma((col_count,)),
            dma((col_count,)),
            dma((2 * chunks + 6,)),
            dma((2 * chunks + 6,)),
            dma((chunks,)),
            dma((chunks,)),
        ],
        compiler_params=pltpu.CompilerParams(
            vmem_limit_bytes=VMEM_LIMIT, collective_id=0, has_side_effects=True
        ),
        name="front",
    )(*early, *late)


def back_kernel(bo_in, co_ref, halo_ref, k1_ref, k2_ref, bo_ref, img_ref, ext, w1, w2, cat, fine, hold, in_sem, out_sem):
    k = pl.program_id(0)
    erows, ring, ch = ext.shape
    rows = erows - 2
    pairs = erows - 1
    cols = img_ref.shape[1] // 2
    fine_step = img_ref.shape[0]
    my_row, my_col = lax.axis_index("row"), lax.axis_index("col")
    at_top, at_bottom = my_row == 0, my_row == lax.axis_size("row") - 1
    at_left, at_right = my_col == 0, my_col == lax.axis_size("col") - 1
    per = rows // in_sem.shape[0]

    def taken(i):
        part = pl.ds(i * per, per)
        return pltpu.make_async_copy(bo_in.at[part], hold.at[part], in_sem.at[i])

    def given(i):
        part = pl.ds(i * per, per)
        return pltpu.make_async_copy(hold.at[part], bo_ref.at[part], out_sem.at[i])

    @pl.when(k == 0)
    def _():
        for i in range(in_sem.shape[0]):
            taken(i).start()
        ext[...] = jnp.zeros_like(ext)
        for c in range(0, cols, PER):
            part = co_ref[c * rows : (c + PER) * rows].reshape(PER, rows, ch)
            ext[1 : rows + 1, c : c + PER, :] = jnp.swapaxes(part, 0, 1)
        coarse = halo_ref[...]
        zero = jnp.float32(0.0)
        ext[0, 0:cols] = jnp.where(at_top, zero, coarse[0:cols])
        ext[rows + 1, 0:cols] = jnp.where(at_bottom, zero, coarse[cols : 2 * cols])
        left = coarse[2 * cols : 2 * cols + rows]
        right = coarse[2 * cols + rows : 2 * cols + 2 * rows]
        ext[1 : rows + 1, ring - 1 : ring, :] = jnp.where(at_left, zero, left).reshape(rows, 1, ch)
        ext[1 : rows + 1, cols : cols + 1, :] = jnp.where(at_right, zero, right).reshape(rows, 1, ch)
        for i, (dr, dc) in enumerate(CORNERS):
            at = 2 * cols + 2 * rows + i * PER + (PER - 1 if dc < 0 else 0)
            outside = (at_top if dr < 0 else at_bottom) | (at_left if dc < 0 else at_right)
            to_row = 0 if dr < 0 else rows + 1
            to_col = ring - 1 if dc < 0 else cols
            ext[to_row, to_col : to_col + 1, :] = jnp.where(outside, zero, coarse[at : at + 1])
        taps = [[k1_ref[y, x].astype(F32) for x in range(3)] for y in range(3)]
        none = jnp.zeros((ch, ch), F32)
        by_half = (
            ([taps[0][x] + taps[1][x] for x in range(3)], taps[2]),
            (taps[0], [taps[1][x] + taps[2][x] for x in range(3)]),
        )
        for half in range(2):
            for dy in range(2):
                t = by_half[half][dy]
                for b in range(2):
                    three = (t[0], t[1] + t[2], none) if b == 0 else (none, t[0] + t[1], t[2])
                    for dx in range(3):
                        w1[
                            (dy * 3 + dx) * ch : (dy * 3 + dx + 1) * ch,
                            (half * 2 + b) * ch : (half * 2 + b + 1) * ch,
                        ] = three[dx].astype(BF16)
        for dy in range(3):
            for s in range(4):
                for b in range(2):
                    w2[(dy * 4 + s) * ch : (dy * 4 + s + 1) * ch, b * ch : (b + 1) * ch] = (
                        k2_ref[dy, s - b] if 0 <= s - b <= 2 else none.astype(BF16)
                    )

        def widen(e, carry):
            x = ext[e]
            cat[e] = jnp.concatenate(
                [pltpu.roll(x, 1, 0), x, pltpu.roll(x, ring - 1, 0)], axis=1
            ).astype(BF16)
            return carry

        lax.fori_loop(0, erows, widen, 0)
        place = lax.broadcasted_iota(jnp.int32, (ring, 128), 0)
        col_keep = jnp.where(
            ((place == ring - 1) & at_left) | ((place == cols) & at_right), 0.0, 1.0
        )
        group = 11

        def first_conv(g, carry):
            e0 = g * group
            left = jnp.concatenate(
                [
                    jnp.concatenate([cat[e0 + i], cat[e0 + i + 1]], axis=1)
                    for i in range(group)
                ],
                axis=0,
            )
            y = silu(dot(left, w1[...]))
            for i in range(group):
                for half in range(2):
                    f = 2 * (e0 + i) + half
                    outside = ((f == 0) & at_top) | ((f == 2 * pairs - 1) & at_bottom)
                    keep = jnp.where(outside, 0.0, 1.0) * col_keep
                    f0 = y[i * ring : (i + 1) * ring, (2 * half) * ch : (2 * half + 1) * ch] * keep
                    f1 = y[i * ring : (i + 1) * ring, (2 * half + 1) * ch : (2 * half + 2) * ch] * keep
                    fine[f] = jnp.concatenate(
                        [pltpu.roll(f1, 1, 0), f0, f1, pltpu.roll(f0, ring - 1, 0)], axis=1
                    ).astype(BF16)
            return carry

        lax.fori_loop(0, pairs // group, first_conv, 0)

    if True:
        m = k
        y0 = m * fine_step
        left = jnp.concatenate(
            [
                jnp.concatenate([fine[y0 + i + dy, 0:cols] for dy in range(3)], axis=1)
                for i in range(fine_step)
            ],
            axis=0,
        )
        second = dot(left, w2[...])
        for i in range(fine_step):
            up = ext[m * (fine_step // 2) + i // 2 + 1, 0:cols]
            for b in range(2):
                img_ref[i, pl.ds(b, cols, stride=2), :] = (
                    second[i * cols : (i + 1) * cols, b * ch : (b + 1) * ch] + up
                )
    taken(k).wait()
    given(k).start()

    @pl.when(k == pl.num_programs(0) - 1)
    def _():
        for i in range(in_sem.shape[0]):
            given(i).wait()


def back_call(block_out, coarse, halo, k1, k2):
    rows, cols, _ = block_out.shape
    ch = coarse.shape[1]
    ring = cols + 16
    fine_step = 16
    anywhere = pl.BlockSpec(memory_space=pl.ANY)
    return pl.pallas_call(
        back_kernel,
        grid=(2 * rows // fine_step,),
        in_specs=[anywhere] + [full(x.shape) for x in (coarse, halo, k1, k2)],
        out_specs=[anywhere, pl.BlockSpec((fine_step, 2 * cols, ch), lambda i: (i, 0, 0))],
        out_shape=[
            jax.ShapeDtypeStruct(block_out.shape, F32),
            jax.ShapeDtypeStruct((2 * rows, 2 * cols, ch), F32),
        ],
        scratch_shapes=[
            pltpu.VMEM((rows + 2, ring, ch), F32),
            pltpu.VMEM((6 * ch, 4 * ch), BF16),
            pltpu.VMEM((12 * ch, 2 * ch), BF16),
            pltpu.VMEM((rows + 2, ring, 3 * ch), BF16),
            pltpu.VMEM((2 * rows + 2, ring, 4 * ch), BF16),
            pltpu.VMEM(block_out.shape, F32),
            pltpu.SemaphoreType.DMA((2 * rows // fine_step,)),
            pltpu.SemaphoreType.DMA((2 * rows // fine_step,)),
        ],
        compiler_params=pltpu.CompilerParams(vmem_limit_bytes=VMEM_LIMIT),
        name="back",
    )(block_out, coarse, halo, k1, k2)


def per_device(
    codes, starts, embed, gain_one, row_qkv, row_out, gain_two, col_qkv, col_out,
    gain_three, mlp_in, mlp_out, project, conv_one, conv_two,
):
    block_out, coarse, halo = front_call(
        codes, starts[None], embed, gain_one[None], row_qkv, gain_two[None], col_qkv,
        gain_three[None], row_out, col_out, mlp_in, mlp_out, project,
    )
    return tuple(back_call(block_out, coarse, halo, conv_one, conv_two))


def solution(mesh):
    in_specs = (P("row", "col"),) + (P(),) * 14
    out_specs = (P("row", "col", None), P("row", "col", None))
    return jax.shard_map(
        per_device, mesh=mesh, in_specs=in_specs, out_specs=out_specs, check_vma=False
    )
```

```python
import functools
import math
import jax
import jax.numpy as jnp
from jax import lax
from jax.experimental import pallas as pl
from jax.experimental.pallas import tpu as pltpu
from jax.sharding import PartitionSpec as P

HEADS = 8
HD = 64
EPS = 1e-06
NEGATIVE = -1e30
LOG2E = math.log2(math.e)
F32 = jnp.float32
BF16 = jnp.bfloat16
MESH = pl.DeviceIdType.MESH
VMEM_LIMIT = 56 * 1024 * 1024


def dot(left, right):
    return jnp.dot(left, right, preferred_element_type=F32)


def dot_t(left, right):
    return lax.dot_general(left, right, (((1,), (1,)), ((), ())), preferred_element_type=F32)


def norm_round(values, norm_gain):
    scale = lax.rsqrt(jnp.mean(values * values, axis=-1, keepdims=True) + EPS)
    return (values * scale * norm_gain).astype(BF16)


def silu(v):
    h = 0.5 * v
    return h + h * jnp.tanh(h)


def lane_low(rows):
    return lax.broadcasted_iota(jnp.int32, (rows, 128), 1) < HD


PER = 8
AHEAD = 2


def row_setup(embed_ref, g1_ref, wqkv_ref, qtab, kz, vz, tri, rows):
    vocab, width = embed_ref.shape
    tile = tri.shape[0]
    scale = (HD ** -0.5) * LOG2E
    normed = norm_round(embed_ref[...].astype(F32), g1_ref[...])
    low = lane_low(vocab)
    qtab[...] = (dot(normed, wqkv_ref[:, :width]) * scale).astype(BF16)
    keys = dot(normed, wqkv_ref[:, width : 2 * width])
    values = dot(normed, wqkv_ref[:, 2 * width :])
    for h in range(HEADS):
        p = h // 2
        mine = low if h % 2 == 0 else jnp.logical_not(low)
        sl = slice(p * 128, p * 128 + 128)
        kz[h] = jnp.where(mine, keys[:, sl], 0.0).astype(BF16)
        vz[h] = jnp.where(mine, values[:, sl], 1.0).astype(BF16)
    out_t = lax.broadcasted_iota(jnp.int32, (tile, tile), 0)
    in_t = lax.broadcasted_iota(jnp.int32, (tile, tile), 1)
    tri[...] = jnp.where(
        (out_t % rows == in_t % rows) & (in_t // rows <= out_t // rows), 1.0, 0.0
    ).astype(BF16)


def row_tile(k, codes_ref, embed_ref, wro_ref, g2_ref, wcol_ref, qtab, kz, vz, seen, tri):
    vocab, width = embed_ref.shape
    rows = codes_ref.shape[0]
    tile = tri.shape[0]
    scale = (HD ** -0.5) * LOG2E
    codes = codes_ref[...]
    rolled = pltpu.roll(jnp.concatenate([codes, codes], axis=1), 128 - PER * k, 1)
    ids = lax.broadcasted_iota(jnp.int32, (rows, vocab), 1)
    one_hot = jnp.concatenate(
        [jnp.where(rolled[:, c : c + 1] == ids, 1.0, 0.0) for c in range(PER)], axis=0
    ).astype(BF16)
    counts = dot(tri[...], one_hot) + jnp.concatenate([seen[...]] * PER, axis=0)
    seen[...] = counts[tile - rows :]
    logn = jnp.where(counts > 0.5, jnp.log2(jnp.maximum(counts, 1.0)), NEGATIVE)
    emb = dot(one_hot, embed_ref[...])
    q = dot(one_hot, qtab[...]).astype(BF16)
    low = lane_low(tile)

    def scores(h):
        return dot_t(q[:, h // 2 * 128 : h // 2 * 128 + 128], kz[h]) + logn

    line = [scores(h) for h in range(AHEAD)]
    mixed, outs = [], []
    for h in range(HEADS):
        s = line.pop(0)
        if h + AHEAD < HEADS:
            line.append(scores(h + AHEAD))
        top = jnp.max(s, axis=-1, keepdims=True)
        e = jnp.exp2(s - top).astype(BF16)
        outs.append(dot(e, vz[h]))
        if h % 2:
            num = jnp.where(low, outs[0], outs[1])
            den = pltpu.roll(jnp.where(low, outs[1], outs[0]), HD, 1)
            mixed.append((num / den).astype(BF16))
            outs = []
    after = emb + dot(jnp.concatenate(mixed, axis=1), wro_ref[...])
    normed = norm_round(after, g2_ref[...])
    proj = dot(normed, wcol_ref[...])
    lane = lax.broadcasted_iota(jnp.int32, (tile, 128), 1)
    row = lax.broadcasted_iota(jnp.int32, (tile, 128), 0) % rows
    mark = jnp.where(lane == HD + row, 1.0, 0.0)
    q2 = []
    for p in range(HEADS // 2):
        pair = proj[:, p * 128 : p * 128 + 128] * scale
        q2.append(jnp.where(low, pair, mark).astype(BF16))
        q2.append(jnp.where(low, pltpu.roll(pair, HD, 1), mark).astype(BF16))
    return after, jnp.concatenate(q2, axis=1), proj[:, width:].astype(BF16)


def set_bias(bias, starts_ref, first, rows):
    lane = lax.broadcasted_iota(jnp.int32, bias.shape, 1)
    place = lax.broadcasted_iota(jnp.int32, bias.shape, 0)
    slot, line = place // rows, bias.shape[0] // rows // 2
    key_row = ((slot % line) * 2 + slot // line) * rows + place % rows
    query_row = first + lane - HD
    turn = lax.rem(HD - first + starts_ref.shape[1], starts_ref.shape[1])
    here = pltpu.roll(jnp.broadcast_to(starts_ref[...], (8, starts_ref.shape[1])), turn, 1)
    seen = (key_row <= query_row) & (key_row >= here[0:1, :128])
    bias[...] = jnp.where((lane < HD) | seen, 0.0, NEGATIVE).astype(BF16)


def col_tile(q_of, kv_of, bias, mixed, at, rows, keys, between):
    low_f = jnp.where(lane_low(keys), 1.0, 0.0)
    low_k = low_f.astype(BF16)
    high_k = (1.0 - low_f).astype(BF16)
    low = lane_low(rows)

    def scores(c):
        kv = kv_of(c)
        q = q_of(c)
        q = jnp.concatenate([q[:, h * 128 : h * 128 + 128] for h in range(HEADS)], axis=0)
        return dot_t(q, kv * low_k + bias[...]), kv * high_k + low_k

    line = [scores(c) for c in range(AHEAD)]
    for c in range(PER):
        s, va = line.pop(0)
        if c + AHEAD < PER:
            line.append(scores(c + AHEAD))
        top = jnp.max(s, axis=-1, keepdims=True)
        e = jnp.exp2(s - top).astype(BF16)
        o = dot(e, va)
        for p in range(HEADS // 2):
            even = o[(2 * p) * rows : (2 * p + 1) * rows]
            odd = o[(2 * p + 1) * rows : (2 * p + 2) * rows]
            keep = jnp.where(low, even, odd)
            other = pltpu.roll(jnp.where(low, odd, even), HD, 1)
            num = jnp.where(low, other, keep)
            den = jnp.where(low, keep, other)
            mixed[at, c * rows : (c + 1) * rows, p * 128 : p * 128 + 128] = (num / den).astype(BF16)
        next(between, None)


def feed_forward(mix, before, wco, g3_ref, win, wout, wp, keep):
    after = before + dot(mix, wco[...])
    normed = norm_round(after, g3_ref[...])
    yield
    inner, quarter = [], win.shape[1] // 4
    for i in range(4):
        inner.append(silu(dot(normed, win[:, i * quarter : (i + 1) * quarter])).astype(BF16))
        yield
    out = after + dot(jnp.concatenate(inner, axis=1), wout[...])
    yield
    keep(out, dot(out.astype(BF16), wp[...]).astype(BF16).astype(F32))
    yield


CORNERS = ((-1, -1), (-1, 1), (1, -1), (1, 1))


def front_kernel(
    row_count, col_count,
    codes_ref, starts_ref, g1_ref, g2_ref, g3_ref,
    embed_hbm, wqkv_hbm, wcol_hbm, wro_hbm, wco_hbm, win_hbm, wout_hbm, wp_hbm,
    bo_ref, co_ref, halo_ref,
    embed_ref, wqkv_ref, wcol_ref, wro_ref, wco_ref, win_ref, wout_ref, wp_ref,
    qtab, kz, vz, seen, tri, bias, mixed, kv_all, q2_all, held, coarse_all, hist, edge,
    late_sem, kv_send, kv_recv, hist_send, hist_recv, halo_send, halo_recv, out_sem, co_sem,
):
    rows = codes_ref.shape[0]
    vocab, width = embed_hbm.shape
    slots, cols = kv_all.shape[0], kv_all.shape[1]
    keys = slots * rows
    tile = PER * rows
    chunks = cols // PER
    my_row, my_col = lax.axis_index("row"), lax.axis_index("col")

    half = row_count // 4

    def sibling(r):
        return r + 1 - 2 * lax.rem(r, 2)

    def across(r):
        return r + 2 - 4 * lax.rem(lax.div(r, 2), 2)

    def turned(r, steps):
        return lax.rem(r + 4 * steps, row_count)

    sib, beyond = sibling(my_row), across(my_row)
    down, up = turned(my_row, 1), turned(my_row, half - 1)
    far = turned(my_row, 2)

    halo_ref[...] = jnp.zeros_like(halo_ref)
    hist[...] = jnp.zeros_like(hist)
    def row_by(dr):
        return lax.rem(my_row + dr + row_count, row_count)

    barrier = pltpu.get_barrier_semaphore()
    other = row_by(2 * lax.rem(my_row, 2) - 1)
    peers = [{"row": r, "col": my_col} for r in (sib, beyond, down, up, other)]
    for d in range(1, col_count):
        peers.append({"row": my_row, "col": lax.rem(my_col + d, col_count)})
    for dr, dc in CORNERS:
        peers.append({"row": row_by(dr), "col": lax.rem(my_col + dc + col_count, col_count)})
    for peer in peers:
        pl.semaphore_signal(barrier, 1, device_id=peer, device_id_type=MESH)

    def there(dr, dc):
        ok = None
        for at, step, count in ((my_row, dr, row_count), (my_col, dc, col_count)):
            if step:
                t = at + step >= 0 if step < 0 else at + step < count
                ok = t if ok is None else ok & t
        return ok

    late = [
        pltpu.make_async_copy(hbm, ref, late_sem.at[i])
        for i, (hbm, ref) in enumerate(
            (
                (embed_hbm, embed_ref), (wqkv_hbm, wqkv_ref), (wcol_hbm, wcol_ref),
                (wro_hbm, wro_ref), (wco_hbm, wco_ref), (win_hbm, win_ref),
                (wout_hbm, wout_ref), (wp_hbm, wp_ref),
            )
        )
    ]
    for copy in late:
        copy.start()

    ids = lax.broadcasted_iota(jnp.int32, (rows, vocab), 1)
    codes = codes_ref[...]
    own = jnp.zeros((rows, vocab), F32)
    for c in range(cols):
        own = own + jnp.where(codes[:, c : c + 1] == ids, 1.0, 0.0)
    hist[my_col] = own.astype(BF16)

    pl.semaphore_wait(barrier, len(peers))

    def hist_copy(d, slot):
        return pltpu.make_async_remote_copy(
            src_ref=hist.at[slot], dst_ref=hist.at[slot],
            send_sem=hist_send.at[d], recv_sem=hist_recv.at[slot],
            device_id={"col": lax.rem(my_col + d, col_count)}, device_id_type=MESH,
        )

    for d in range(1, col_count):
        @pl.when(my_col + d < col_count)
        def _():
            hist_copy(d, my_col).start()

    for copy in late[:2]:
        copy.wait()
    row_setup(embed_ref, g1_ref, wqkv_ref, qtab, kz, vz, tri, rows)

    for d in range(1, col_count):
        @pl.when(my_col >= d)
        def _():
            hist_copy(d, lax.rem(my_col - d + col_count, col_count)).wait_recv()
    base = jnp.zeros((rows, vocab), F32)
    for c in range(col_count):
        base = base + jnp.where(c < my_col, hist[c].astype(F32), 0.0)
    seen[...] = base

    def slot_of(r):
        return lax.rem(r, 2) * (slots // 2) + lax.div(r, 2)

    def kv_copy(k, slot, size, stage, dest):
        part = kv_all.at[pl.ds(slot, size), pl.ds(k * PER, PER)]
        return pltpu.make_async_remote_copy(
            src_ref=part, dst_ref=part,
            send_sem=kv_send.at[k], recv_sem=kv_recv.at[stage, k],
            device_id={"row": dest}, device_id_type=MESH,
        )

    def send(k, r, stage, dest):
        kv_copy(k, slot_of(r), 1, stage, dest).start()

    def arrived(k, stage, size):
        kv_copy(k, 0, size, stage, sib).wait_recv()

    def relay(s):
        k1 = s - 3

        @pl.when((k1 >= 0) & (k1 < chunks))
        def _():
            arrived(k1, 0, 3)
            send(k1, beyond, 1, down)
            send(k1, beyond, 1, up)
            even = lax.rem(k1, 2) == 0

            @pl.when(even)
            def _():
                send(k1, up, 1, down)

            @pl.when(jnp.logical_not(even))
            def _():
                send(k1, down, 1, up)

        k2 = s - 5

        @pl.when((k2 >= 0) & (k2 < chunks))
        def _():
            arrived(k2, 1, 3)
            send(k2, far, 2, beyond)

        k3 = s - 7

        @pl.when((k3 >= 0) & (k3 < chunks))
        def _():
            arrived(k3, 2, 1)
            line = lax.rem(my_row, 2) * (slots // 2)
            kv_copy(k3, line, slots // 2, 3, sib).start()

    for copy in late[2:4]:
        copy.wait()

    def row_step(k, carry):
        relay(k)
        after, q2, kv = row_tile(
            k, codes_ref, embed_ref, wro_ref, g2_ref, wcol_ref, qtab, kz, vz, seen, tri
        )
        kv_all[slot_of(my_row), pl.ds(k * PER, PER)] = kv.reshape(PER, rows, 2 * HD)
        send(k, my_row, 0, beyond)
        send(k, my_row, 0, down)
        send(k, my_row, 0, up)
        held[k] = after.reshape(rows, PER, width)
        q2_all[pl.ds(k * PER, PER)] = q2.reshape(PER, rows, 2 * width)
        return carry

    lax.fori_loop(0, chunks, row_step, 0)

    def halo_copy(sem, src, at, size, dr, dc):
        return pltpu.make_async_remote_copy(
            src_ref=src, dst_ref=halo_ref.at[pl.ds(at, size)],
            send_sem=halo_send.at[sem], recv_sem=halo_recv.at[sem],
            device_id={"row": my_row + dr, "col": my_col + dc}, device_id_type=MESH,
        )

    left_at, corner_at = 2 * cols, 2 * cols + 2 * rows
    side_sem = 2 * chunks

    def edge_copy(which, k, dr):
        at = cols if which == 0 else 0
        return halo_copy(
            which * chunks + k, edge.at[which, pl.ds(k * PER, PER)], at + k * PER, PER, dr, 0
        )

    def side_copy(which, dc):
        c = 0 if which == 0 else cols - 1
        at = left_at + rows if which == 0 else left_at
        return halo_copy(side_sem + which, coarse_all.at[pl.ds(c * rows, rows)], at, rows, 0, dc)

    def corner_copy(i, dr, dc):
        k = 0 if dc < 0 else chunks - 1
        at = corner_at + (len(CORNERS) - 1 - i) * PER
        return halo_copy(
            side_sem + 2 + i, edge.at[0 if dr < 0 else 1, pl.ds(k * PER, PER)], at, PER, dr, dc
        )

    def out_copies(k):
        part = pl.ds(k * tile, tile)
        return (
            pltpu.make_async_copy(
                held.at[k], bo_ref.at[pl.ds(0, rows), pl.ds(k * PER, PER)], out_sem.at[k]
            ),
            pltpu.make_async_copy(coarse_all.at[part], co_ref.at[part], co_sem.at[k]),
        )

    def chunk_of(j):
        return j

    def feed(j):
        k = chunk_of(j)

        def keep(out, coarse):
            held[k] = jnp.swapaxes(out.reshape(PER, rows, width), 0, 1)
            coarse_all[pl.ds(k * tile, tile)] = coarse
            grid = coarse.reshape(PER, rows, coarse.shape[1])
            edge[0, pl.ds(k * PER, PER)] = grid[:, 0]
            edge[1, pl.ds(k * PER, PER)] = grid[:, rows - 1]

        return feed_forward(
            mixed[lax.rem(j, 2)], held[k].reshape(tile, width), wco_ref, g3_ref, win_ref,
            wout_ref, wp_ref, keep,
        )

    def pass_on(j):
        k = chunk_of(j)
        for copy in out_copies(k):
            copy.start()

        @pl.when(there(-1, 0))
        def _():
            edge_copy(0, k, -1).start()

        @pl.when(there(1, 0))
        def _():
            edge_copy(1, k, 1).start()

        for which, dc in ((0, -1), (1, 1)):
            last = 0 if which == 0 else chunks - 1

            @pl.when(there(0, dc) & (k == last))
            def _():
                side_copy(which, dc).start()

        for i, (dr, dc) in enumerate(CORNERS):
            last = 0 if dc < 0 else chunks - 1

            @pl.when(there(dr, dc) & (k == last))
            def _():
                corner_copy(i, dr, dc).start()

    def attend(j, between):
        relay(chunks + j)
        k = chunk_of(j)
        arrived(k, 3, slots // 2)
        col_tile(
            lambda c: q2_all[k * PER + c],
            lambda c: kv_all[:, k * PER + c].reshape(keys, 2 * HD),
            bias, mixed, lax.rem(j, 2), rows, keys, between,
        )
        for _ in between:
            pass

    def col_step(j, carry):
        attend(j, feed(j - 1))
        pass_on(j - 1)
        return carry

    set_bias(bias, starts_ref, my_row * rows, rows)
    attend(0, iter(()))
    for copy in late[4:]:
        copy.wait()
    lax.fori_loop(1, chunks, col_step, 0)
    for _ in feed(chunks - 1):
        pass
    pass_on(chunks - 1)

    for d in range(1, col_count):
        @pl.when(my_col + d < col_count)
        def _():
            hist_copy(d, my_col).wait_send()

    def finish(k, carry):
        kv_copy(k, 0, 7 + slots // 2, 0, sib).wait_send()
        for copy in out_copies(k):
            copy.wait()

        @pl.when(there(-1, 0))
        def _():
            edge_copy(0, k, -1).wait_send()
            edge_copy(1, k, -1).wait_recv()

        @pl.when(there(1, 0))
        def _():
            edge_copy(1, k, 1).wait_send()
            edge_copy(0, k, 1).wait_recv()

        return carry

    lax.fori_loop(0, chunks, finish, 0)
    for which, dc in ((0, -1), (1, 1)):
        @pl.when(there(0, dc))
        def _():
            side_copy(which, dc).wait_send()
            side_copy(1 - which, dc).wait_recv()
    for i, (dr, dc) in enumerate(CORNERS):
        @pl.when(there(dr, dc))
        def _():
            corner_copy(i, dr, dc).wait_send()
            corner_copy(len(CORNERS) - 1 - i, dr, dc).wait_recv()


def full(shape):
    return pl.BlockSpec(shape, lambda *_: (0,) * len(shape))


def front_call(codes, starts, embed, g1, wqkv, g2, wcol, g3, wro, wco, win, wout, wp):
    vocab, width = embed.shape
    rows, cols = codes.shape
    ch = wp.shape[1]
    row_count, col_count = lax.axis_size("row"), lax.axis_size("col")
    tokens = rows * cols
    tile = rows * PER
    chunks = cols // PER
    halo = 2 * cols + 2 * rows + 4 * PER
    dma = pltpu.SemaphoreType.DMA
    early = (codes, starts, g1, g2, g3)
    late = (embed, wqkv, wcol, wro, wco, win, wout, wp)
    anywhere, vmem = pl.BlockSpec(memory_space=pl.ANY), pl.BlockSpec(memory_space=pltpu.VMEM)
    return pl.pallas_call(
        functools.partial(front_kernel, row_count, col_count),
        in_specs=[vmem] * len(early) + [anywhere] * len(late),
        out_specs=[anywhere, anywhere, vmem],
        out_shape=[
            jax.ShapeDtypeStruct((rows, cols, width), F32),
            jax.ShapeDtypeStruct((tokens, ch), F32),
            jax.ShapeDtypeStruct((halo, ch), F32),
        ],
        scratch_shapes=[pltpu.VMEM(x.shape, x.dtype) for x in late]
        + [
            pltpu.VMEM((vocab, width), BF16),
            pltpu.VMEM((HEADS, vocab, 128), BF16),
            pltpu.VMEM((HEADS, vocab, 128), BF16),
            pltpu.VMEM((rows, vocab), F32),
            pltpu.VMEM((tile, tile), BF16),
            pltpu.VMEM((row_count * rows, 128), BF16),
            pltpu.VMEM((2, tile, width), BF16),
            pltpu.VMEM((row_count, cols, rows, 2 * HD), BF16),
            pltpu.VMEM((cols, rows, 2 * width), BF16),
            pltpu.VMEM((chunks, rows, PER, width), F32),
            pltpu.VMEM((tokens, ch), F32),
            pltpu.VMEM((col_count, rows, vocab), BF16),
            pltpu.VMEM((2, cols, ch), F32),
            dma((len(late),)),
            dma((chunks,)),
            dma((4, chunks)),
            dma((col_count,)),
            dma((col_count,)),
            dma((2 * chunks + 6,)),
            dma((2 * chunks + 6,)),
            dma((chunks,)),
            dma((chunks,)),
        ],
        compiler_params=pltpu.CompilerParams(
            vmem_limit_bytes=VMEM_LIMIT, collective_id=0, has_side_effects=True
        ),
        name="front",
    )(*early, *late)


def back_kernel(bo_in, co_ref, halo_ref, k1_ref, k2_ref, bo_ref, img_ref, ext, w1, w2, cat, fine, hold, in_sem, out_sem):
    k = pl.program_id(0)
    erows, ring, ch = ext.shape
    rows = erows - 2
    pairs = erows - 1
    cols = img_ref.shape[1] // 2
    fine_step = img_ref.shape[0]
    my_row, my_col = lax.axis_index("row"), lax.axis_index("col")
    at_top, at_bottom = my_row == 0, my_row == lax.axis_size("row") - 1
    at_left, at_right = my_col == 0, my_col == lax.axis_size("col") - 1
    per = rows // in_sem.shape[0]

    def taken(i):
        part = pl.ds(i * per, per)
        return pltpu.make_async_copy(bo_in.at[part], hold.at[part], in_sem.at[i])

    def given(i):
        part = pl.ds(i * per, per)
        return pltpu.make_async_copy(hold.at[part], bo_ref.at[part], out_sem.at[i])

    @pl.when(k == 0)
    def _():
        for i in range(in_sem.shape[0]):
            taken(i).start()
        ext[...] = jnp.zeros_like(ext)
        for c in range(0, cols, PER):
            part = co_ref[c * rows : (c + PER) * rows].reshape(PER, rows, ch)
            ext[1 : rows + 1, c : c + PER, :] = jnp.swapaxes(part, 0, 1)
        coarse = halo_ref[...]
        zero = jnp.float32(0.0)
        ext[0, 0:cols] = jnp.where(at_top, zero, coarse[0:cols])
        ext[rows + 1, 0:cols] = jnp.where(at_bottom, zero, coarse[cols : 2 * cols])
        left = coarse[2 * cols : 2 * cols + rows]
        right = coarse[2 * cols + rows : 2 * cols + 2 * rows]
        ext[1 : rows + 1, ring - 1 : ring, :] = jnp.where(at_left, zero, left).reshape(rows, 1, ch)
        ext[1 : rows + 1, cols : cols + 1, :] = jnp.where(at_right, zero, right).reshape(rows, 1, ch)
        for i, (dr, dc) in enumerate(CORNERS):
            at = 2 * cols + 2 * rows + i * PER + (PER - 1 if dc < 0 else 0)
            outside = (at_top if dr < 0 else at_bottom) | (at_left if dc < 0 else at_right)
            to_row = 0 if dr < 0 else rows + 1
            to_col = ring - 1 if dc < 0 else cols
            ext[to_row, to_col : to_col + 1, :] = jnp.where(outside, zero, coarse[at : at + 1])
        taps = [[k1_ref[y, x].astype(F32) for x in range(3)] for y in range(3)]
        none = jnp.zeros((ch, ch), F32)
        by_half = (
            ([taps[0][x] + taps[1][x] for x in range(3)], taps[2]),
            (taps[0], [taps[1][x] + taps[2][x] for x in range(3)]),
        )
        for half in range(2):
            for dy in range(2):
                t = by_half[half][dy]
                for b in range(2):
                    three = (t[0], t[1] + t[2], none) if b == 0 else (none, t[0] + t[1], t[2])
                    for dx in range(3):
                        w1[
                            (dy * 3 + dx) * ch : (dy * 3 + dx + 1) * ch,
                            (half * 2 + b) * ch : (half * 2 + b + 1) * ch,
                        ] = three[dx].astype(BF16)
        for dy in range(3):
            for s in range(4):
                for b in range(2):
                    w2[(dy * 4 + s) * ch : (dy * 4 + s + 1) * ch, b * ch : (b + 1) * ch] = (
                        k2_ref[dy, s - b] if 0 <= s - b <= 2 else none.astype(BF16)
                    )

        def widen(e, carry):
            x = ext[e]
            cat[e] = jnp.concatenate(
                [pltpu.roll(x, 1, 0), x, pltpu.roll(x, ring - 1, 0)], axis=1
            ).astype(BF16)
            return carry

        lax.fori_loop(0, erows, widen, 0)
        place = lax.broadcasted_iota(jnp.int32, (ring, 128), 0)
        col_keep = jnp.where(
            ((place == ring - 1) & at_left) | ((place == cols) & at_right), 0.0, 1.0
        )
        group = 11

        def first_sums(e0):
            left = jnp.concatenate(
                [
                    jnp.concatenate([cat[e0 + i], cat[e0 + i + 1]], axis=1)
                    for i in range(group)
                ],
                axis=0,
            )
            return dot(left, w1[...])

        def first_keep(e0, sums):
            y = silu(sums)
            for i in range(group):
                for half in range(2):
                    f = 2 * (e0 + i) + half
                    outside = ((f == 0) & at_top) | ((f == 2 * pairs - 1) & at_bottom)
                    keep = jnp.where(outside, 0.0, 1.0) * col_keep
                    f0 = y[i * ring : (i + 1) * ring, (2 * half) * ch : (2 * half + 1) * ch] * keep
                    f1 = y[i * ring : (i + 1) * ring, (2 * half + 1) * ch : (2 * half + 2) * ch] * keep
                    fine[f] = jnp.concatenate(
                        [pltpu.roll(f1, 1, 0), f0, f1, pltpu.roll(f0, ring - 1, 0)], axis=1
                    ).astype(BF16)

        nxt = first_sums(0)
        for e0 in range(0, pairs, group):
            sums = nxt
            if e0 + group < pairs:
                nxt = first_sums(e0 + group)
            first_keep(e0, sums)

    if True:
        m = k
        y0 = m * fine_step
        left = jnp.concatenate(
            [
                jnp.concatenate([fine[y0 + i + dy, 0:cols] for dy in range(3)], axis=1)
                for i in range(fine_step)
            ],
            axis=0,
        )
        second = dot(left, w2[...])
        for i in range(fine_step):
            up = ext[m * (fine_step // 2) + i // 2 + 1, 0:cols]
            for b in range(2):
                img_ref[i, pl.ds(b, cols, stride=2), :] = (
                    second[i * cols : (i + 1) * cols, b * ch : (b + 1) * ch] + up
                )
    taken(k).wait()
    given(k).start()

    @pl.when(k == pl.num_programs(0) - 1)
    def _():
        for i in range(in_sem.shape[0]):
            given(i).wait()


def back_call(block_out, coarse, halo, k1, k2):
    rows, cols, _ = block_out.shape
    ch = coarse.shape[1]
    ring = cols + 16
    fine_step = 16
    anywhere = pl.BlockSpec(memory_space=pl.ANY)
    return pl.pallas_call(
        back_kernel,
        grid=(2 * rows // fine_step,),
        in_specs=[anywhere] + [full(x.shape) for x in (coarse, halo, k1, k2)],
        out_specs=[anywhere, pl.BlockSpec((fine_step, 2 * cols, ch), lambda i: (i, 0, 0))],
        out_shape=[
            jax.ShapeDtypeStruct(block_out.shape, F32),
            jax.ShapeDtypeStruct((2 * rows, 2 * cols, ch), F32),
        ],
        scratch_shapes=[
            pltpu.VMEM((rows + 2, ring, ch), F32),
            pltpu.VMEM((6 * ch, 4 * ch), BF16),
            pltpu.VMEM((12 * ch, 2 * ch), BF16),
            pltpu.VMEM((rows + 2, ring, 3 * ch), BF16),
            pltpu.VMEM((2 * rows + 2, ring, 4 * ch), BF16),
            pltpu.VMEM(block_out.shape, F32),
            pltpu.SemaphoreType.DMA((2 * rows // fine_step,)),
            pltpu.SemaphoreType.DMA((2 * rows // fine_step,)),
        ],
        compiler_params=pltpu.CompilerParams(vmem_limit_bytes=VMEM_LIMIT),
        name="back",
    )(block_out, coarse, halo, k1, k2)


def per_device(
    codes, starts, embed, gain_one, row_qkv, row_out, gain_two, col_qkv, col_out,
    gain_three, mlp_in, mlp_out, project, conv_one, conv_two,
):
    block_out, coarse, halo = front_call(
        codes, starts[None], embed, gain_one[None], row_qkv, gain_two[None], col_qkv,
        gain_three[None], row_out, col_out, mlp_in, mlp_out, project,
    )
    return tuple(back_call(block_out, coarse, halo, conv_one, conv_two))


def solution(mesh):
    in_specs = (P("row", "col"),) + (P(),) * 14
    out_specs = (P("row", "col", None), P("row", "col", None))
    return jax.shard_map(
        per_device, mesh=mesh, in_specs=in_specs, out_specs=out_specs, check_vma=False
    )
```

```python
import functools
import math
import jax
import jax.numpy as jnp
from jax import lax
from jax.experimental import pallas as pl
from jax.experimental.pallas import tpu as pltpu
from jax.sharding import PartitionSpec as P

HEADS = 8
HD = 64
EPS = 1e-06
NEGATIVE = -1e30
LOG2E = math.log2(math.e)
F32 = jnp.float32
BF16 = jnp.bfloat16
MESH = pl.DeviceIdType.MESH
VMEM_LIMIT = 56 * 1024 * 1024


def dot(left, right):
    return jnp.dot(left, right, preferred_element_type=F32)


def dot_t(left, right):
    return lax.dot_general(left, right, (((1,), (1,)), ((), ())), preferred_element_type=F32)


def norm_round(values, norm_gain):
    scale = lax.rsqrt(jnp.mean(values * values, axis=-1, keepdims=True) + EPS)
    return (values * scale * norm_gain).astype(BF16)


def silu(v):
    h = 0.5 * v
    return h + h * jnp.tanh(h)


def lane_low(rows):
    return lax.broadcasted_iota(jnp.int32, (rows, 128), 1) < HD


PER = 8
AHEAD = 2


def row_setup(embed_ref, g1_ref, wqkv_ref, qtab, kz, vz, tri, rows):
    vocab, width = embed_ref.shape
    tile = tri.shape[0]
    scale = (HD ** -0.5) * LOG2E
    normed = norm_round(embed_ref[...].astype(F32), g1_ref[...])
    low = lane_low(vocab)
    qtab[...] = (dot(normed, wqkv_ref[:, :width]) * scale).astype(BF16)
    keys = dot(normed, wqkv_ref[:, width : 2 * width])
    values = dot(normed, wqkv_ref[:, 2 * width :])
    for h in range(HEADS):
        p = h // 2
        mine = low if h % 2 == 0 else jnp.logical_not(low)
        sl = slice(p * 128, p * 128 + 128)
        kz[h] = jnp.where(mine, keys[:, sl], 0.0).astype(BF16)
        vz[h] = jnp.where(mine, values[:, sl], 1.0).astype(BF16)
    out_t = lax.broadcasted_iota(jnp.int32, (tile, tile), 0)
    in_t = lax.broadcasted_iota(jnp.int32, (tile, tile), 1)
    tri[...] = jnp.where(
        (out_t % rows == in_t % rows) & (in_t // rows <= out_t // rows), 1.0, 0.0
    ).astype(BF16)


def row_tile(k, codes_ref, embed_ref, wro_ref, g2_ref, wcol_ref, qtab, kz, vz, seen, tri):
    vocab, width = embed_ref.shape
    rows = codes_ref.shape[0]
    tile = tri.shape[0]
    scale = (HD ** -0.5) * LOG2E
    codes = codes_ref[...]
    rolled = pltpu.roll(jnp.concatenate([codes, codes], axis=1), 128 - PER * k, 1)
    ids = lax.broadcasted_iota(jnp.int32, (rows, vocab), 1)
    one_hot = jnp.concatenate(
        [jnp.where(rolled[:, c : c + 1] == ids, 1.0, 0.0) for c in range(PER)], axis=0
    ).astype(BF16)
    counts = dot(tri[...], one_hot) + jnp.concatenate([seen[...]] * PER, axis=0)
    seen[...] = counts[tile - rows :]
    logn = jnp.where(counts > 0.5, jnp.log2(jnp.maximum(counts, 1.0)), NEGATIVE)
    emb = dot(one_hot, embed_ref[...])
    q = dot(one_hot, qtab[...]).astype(BF16)
    low = lane_low(tile)

    def scores(h):
        return dot_t(q[:, h // 2 * 128 : h // 2 * 128 + 128], kz[h]) + logn

    line = [scores(h) for h in range(AHEAD)]
    mixed, outs = [], []
    for h in range(HEADS):
        s = line.pop(0)
        if h + AHEAD < HEADS:
            line.append(scores(h + AHEAD))
        top = jnp.max(s, axis=-1, keepdims=True)
        e = jnp.exp2(s - top).astype(BF16)
        outs.append(dot(e, vz[h]))
        if h % 2:
            num = jnp.where(low, outs[0], outs[1])
            den = pltpu.roll(jnp.where(low, outs[1], outs[0]), HD, 1)
            mixed.append((num / den).astype(BF16))
            outs = []
    after = emb + dot(jnp.concatenate(mixed, axis=1), wro_ref[...])
    normed = norm_round(after, g2_ref[...])
    proj = dot(normed, wcol_ref[...])
    lane = lax.broadcasted_iota(jnp.int32, (tile, 128), 1)
    row = lax.broadcasted_iota(jnp.int32, (tile, 128), 0) % rows
    mark = jnp.where(lane == HD + row, 1.0, 0.0)
    q2 = []
    for p in range(HEADS // 2):
        pair = proj[:, p * 128 : p * 128 + 128] * scale
        q2.append(jnp.where(low, pair, mark).astype(BF16))
        q2.append(jnp.where(low, pltpu.roll(pair, HD, 1), mark).astype(BF16))
    return after, jnp.concatenate(q2, axis=1), proj[:, width:].astype(BF16)


def set_bias(bias, starts_ref, first, rows):
    lane = lax.broadcasted_iota(jnp.int32, bias.shape, 1)
    place = lax.broadcasted_iota(jnp.int32, bias.shape, 0)
    slot, line = place // rows, bias.shape[0] // rows // 2
    key_row = ((slot % line) * 2 + slot // line) * rows + place % rows
    query_row = first + lane - HD
    turn = lax.rem(HD - first + starts_ref.shape[1], starts_ref.shape[1])
    here = pltpu.roll(jnp.broadcast_to(starts_ref[...], (8, starts_ref.shape[1])), turn, 1)
    seen = (key_row <= query_row) & (key_row >= here[0:1, :128])
    bias[...] = jnp.where((lane < HD) | seen, 0.0, NEGATIVE).astype(BF16)


def col_tile(q_of, kv_of, bias, mixed, at, rows, keys, between):
    low_f = jnp.where(lane_low(keys), 1.0, 0.0)
    low_k = low_f.astype(BF16)
    high_k = (1.0 - low_f).astype(BF16)
    low = lane_low(rows)

    def scores(c):
        kv = kv_of(c)
        q = q_of(c)
        q = jnp.concatenate([q[:, h * 128 : h * 128 + 128] for h in range(HEADS)], axis=0)
        return dot_t(q, kv * low_k + bias[...]), kv * high_k + low_k

    line = [scores(c) for c in range(AHEAD)]
    for c in range(PER):
        s, va = line.pop(0)
        if c + AHEAD < PER:
            line.append(scores(c + AHEAD))
        top = jnp.max(s, axis=-1, keepdims=True)
        e = jnp.exp2(s - top).astype(BF16)
        o = dot(e, va)
        for p in range(HEADS // 2):
            even = o[(2 * p) * rows : (2 * p + 1) * rows]
            odd = o[(2 * p + 1) * rows : (2 * p + 2) * rows]
            keep = jnp.where(low, even, odd)
            other = pltpu.roll(jnp.where(low, odd, even), HD, 1)
            num = jnp.where(low, other, keep)
            den = jnp.where(low, keep, other)
            mixed[at, c * rows : (c + 1) * rows, p * 128 : p * 128 + 128] = (num / den).astype(BF16)
        next(between, None)


def feed_forward(mix, before, wco, g3_ref, win, wout, wp, keep):
    after = before + dot(mix, wco[...])
    normed = norm_round(after, g3_ref[...])
    yield
    inner, quarter = [], win.shape[1] // 4
    for i in range(4):
        inner.append(silu(dot(normed, win[:, i * quarter : (i + 1) * quarter])).astype(BF16))
        yield
    out = after + dot(jnp.concatenate(inner, axis=1), wout[...])
    yield
    keep(out, dot(out.astype(BF16), wp[...]).astype(BF16).astype(F32))
    yield


CORNERS = ((-1, -1), (-1, 1), (1, -1), (1, 1))


def front_kernel(
    row_count, col_count,
    codes_ref, starts_ref, g1_ref, g2_ref, g3_ref,
    embed_hbm, wqkv_hbm, wcol_hbm, wro_hbm, wco_hbm, win_hbm, wout_hbm, wp_hbm,
    bo_ref, co_ref, halo_ref,
    embed_ref, wqkv_ref, wcol_ref, wro_ref, wco_ref, win_ref, wout_ref, wp_ref,
    qtab, kz, vz, seen, tri, bias, mixed, kv_all, q2_all, held, coarse_all, hist, edge,
    late_sem, kv_send, kv_recv, hist_send, hist_recv, halo_send, halo_recv, out_sem, co_sem,
):
    rows = codes_ref.shape[0]
    vocab, width = embed_hbm.shape
    slots, cols = kv_all.shape[0], kv_all.shape[1]
    keys = slots * rows
    tile = PER * rows
    chunks = cols // PER
    my_row, my_col = lax.axis_index("row"), lax.axis_index("col")

    half = row_count // 4

    def sibling(r):
        return r + 1 - 2 * lax.rem(r, 2)

    def across(r):
        return r + 2 - 4 * lax.rem(lax.div(r, 2), 2)

    def turned(r, steps):
        return lax.rem(r + 4 * steps, row_count)

    sib, beyond = sibling(my_row), across(my_row)
    down, up = turned(my_row, 1), turned(my_row, half - 1)
    far = turned(my_row, 2)

    halo_ref[...] = jnp.zeros_like(halo_ref)
    hist[...] = jnp.zeros_like(hist)
    def row_by(dr):
        return lax.rem(my_row + dr + row_count, row_count)

    barrier = pltpu.get_barrier_semaphore()
    other = row_by(2 * lax.rem(my_row, 2) - 1)
    peers = [{"row": r, "col": my_col} for r in (sib, beyond, down, up, other)]
    for d in range(1, col_count):
        peers.append({"row": my_row, "col": lax.rem(my_col + d, col_count)})
    for dr, dc in CORNERS:
        peers.append({"row": row_by(dr), "col": lax.rem(my_col + dc + col_count, col_count)})
    for peer in peers:
        pl.semaphore_signal(barrier, 1, device_id=peer, device_id_type=MESH)

    def there(dr, dc):
        ok = None
        for at, step, count in ((my_row, dr, row_count), (my_col, dc, col_count)):
            if step:
                t = at + step >= 0 if step < 0 else at + step < count
                ok = t if ok is None else ok & t
        return ok

    late = [
        pltpu.make_async_copy(hbm, ref, late_sem.at[i])
        for i, (hbm, ref) in enumerate(
            (
                (embed_hbm, embed_ref), (wqkv_hbm, wqkv_ref), (wcol_hbm, wcol_ref),
                (wro_hbm, wro_ref), (wco_hbm, wco_ref), (win_hbm, win_ref),
                (wout_hbm, wout_ref), (wp_hbm, wp_ref),
            )
        )
    ]
    for copy in late:
        copy.start()

    ids = lax.broadcasted_iota(jnp.int32, (rows, vocab), 1)
    codes = codes_ref[...]
    own = jnp.zeros((rows, vocab), F32)
    for c in range(cols):
        own = own + jnp.where(codes[:, c : c + 1] == ids, 1.0, 0.0)
    hist[my_col] = own.astype(BF16)

    pl.semaphore_wait(barrier, len(peers))

    def hist_copy(d, slot):
        return pltpu.make_async_remote_copy(
            src_ref=hist.at[slot], dst_ref=hist.at[slot],
            send_sem=hist_send.at[d], recv_sem=hist_recv.at[slot],
            device_id={"col": lax.rem(my_col + d, col_count)}, device_id_type=MESH,
        )

    for d in range(1, col_count):
        @pl.when(my_col + d < col_count)
        def _():
            hist_copy(d, my_col).start()

    for copy in late[:2]:
        copy.wait()
    row_setup(embed_ref, g1_ref, wqkv_ref, qtab, kz, vz, tri, rows)

    for d in range(1, col_count):
        @pl.when(my_col >= d)
        def _():
            hist_copy(d, lax.rem(my_col - d + col_count, col_count)).wait_recv()
    base = jnp.zeros((rows, vocab), F32)
    for c in range(col_count):
        base = base + jnp.where(c < my_col, hist[c].astype(F32), 0.0)
    seen[...] = base

    def slot_of(r):
        return lax.rem(r, 2) * (slots // 2) + lax.div(r, 2)

    def kv_copy(k, slot, size, stage, dest):
        part = kv_all.at[pl.ds(slot, size), pl.ds(k * PER, PER)]
        return pltpu.make_async_remote_copy(
            src_ref=part, dst_ref=part,
            send_sem=kv_send.at[k], recv_sem=kv_recv.at[stage, k],
            device_id={"row": dest}, device_id_type=MESH,
        )

    def send(k, r, stage, dest):
        kv_copy(k, slot_of(r), 1, stage, dest).start()

    def arrived(k, stage, size):
        kv_copy(k, 0, size, stage, sib).wait_recv()

    def relay(s):
        k1 = jnp.where(s < 4, s - 2, s - 3)

        @pl.when((k1 >= 0) & (k1 < chunks) & (s != 4))
        def _():
            arrived(k1, 0, 3)
            send(k1, beyond, 1, down)
            send(k1, beyond, 1, up)
            even = lax.rem(k1, 2) == 0

            @pl.when(even)
            def _():
                send(k1, up, 1, down)

            @pl.when(jnp.logical_not(even))
            def _():
                send(k1, down, 1, up)

        k2 = s - 5

        @pl.when((k2 >= 0) & (k2 < chunks))
        def _():
            arrived(k2, 1, 3)
            send(k2, far, 2, beyond)

        k3 = s - 7

        @pl.when((k3 >= 0) & (k3 < chunks))
        def _():
            arrived(k3, 2, 1)
            line = lax.rem(my_row, 2) * (slots // 2)
            kv_copy(k3, line, slots // 2, 3, sib).start()

    for copy in late[2:4]:
        copy.wait()

    def row_step(k, carry):
        relay(k)
        after, q2, kv = row_tile(
            k, codes_ref, embed_ref, wro_ref, g2_ref, wcol_ref, qtab, kz, vz, seen, tri
        )
        kv_all[slot_of(my_row), pl.ds(k * PER, PER)] = kv.reshape(PER, rows, 2 * HD)
        send(k, my_row, 0, beyond)
        send(k, my_row, 0, down)
        send(k, my_row, 0, up)
        held[k] = after.reshape(rows, PER, width)
        q2_all[pl.ds(k * PER, PER)] = q2.reshape(PER, rows, 2 * width)
        return carry

    lax.fori_loop(0, chunks, row_step, 0)

    def halo_copy(sem, src, at, size, dr, dc):
        return pltpu.make_async_remote_copy(
            src_ref=src, dst_ref=halo_ref.at[pl.ds(at, size)],
            send_sem=halo_send.at[sem], recv_sem=halo_recv.at[sem],
            device_id={"row": my_row + dr, "col": my_col + dc}, device_id_type=MESH,
        )

    left_at, corner_at = 2 * cols, 2 * cols + 2 * rows
    side_sem = 2 * chunks

    def edge_copy(which, k, dr):
        at = cols if which == 0 else 0
        return halo_copy(
            which * chunks + k, edge.at[which, pl.ds(k * PER, PER)], at + k * PER, PER, dr, 0
        )

    def side_copy(which, dc):
        c = 0 if which == 0 else cols - 1
        at = left_at + rows if which == 0 else left_at
        return halo_copy(side_sem + which, coarse_all.at[pl.ds(c * rows, rows)], at, rows, 0, dc)

    def corner_copy(i, dr, dc):
        k = 0 if dc < 0 else chunks - 1
        at = corner_at + (len(CORNERS) - 1 - i) * PER
        return halo_copy(
            side_sem + 2 + i, edge.at[0 if dr < 0 else 1, pl.ds(k * PER, PER)], at, PER, dr, dc
        )

    def out_copies(k):
        part = pl.ds(k * tile, tile)
        return (
            pltpu.make_async_copy(
                held.at[k], bo_ref.at[pl.ds(0, rows), pl.ds(k * PER, PER)], out_sem.at[k]
            ),
            pltpu.make_async_copy(coarse_all.at[part], co_ref.at[part], co_sem.at[k]),
        )

    def chunk_of(j):
        return j

    def feed(j):
        k = chunk_of(j)

        def keep(out, coarse):
            held[k] = jnp.swapaxes(out.reshape(PER, rows, width), 0, 1)
            coarse_all[pl.ds(k * tile, tile)] = coarse
            grid = coarse.reshape(PER, rows, coarse.shape[1])
            edge[0, pl.ds(k * PER, PER)] = grid[:, 0]
            edge[1, pl.ds(k * PER, PER)] = grid[:, rows - 1]

        return feed_forward(
            mixed[lax.rem(j, 2)], held[k].reshape(tile, width), wco_ref, g3_ref, win_ref,
            wout_ref, wp_ref, keep,
        )

    def pass_on(j):
        k = chunk_of(j)
        for copy in out_copies(k):
            copy.start()

        @pl.when(there(-1, 0))
        def _():
            edge_copy(0, k, -1).start()

        @pl.when(there(1, 0))
        def _():
            edge_copy(1, k, 1).start()

        for which, dc in ((0, -1), (1, 1)):
            last = 0 if which == 0 else chunks - 1

            @pl.when(there(0, dc) & (k == last))
            def _():
                side_copy(which, dc).start()

        for i, (dr, dc) in enumerate(CORNERS):
            last = 0 if dc < 0 else chunks - 1

            @pl.when(there(dr, dc) & (k == last))
            def _():
                corner_copy(i, dr, dc).start()

    def attend(j, between):
        relay(chunks + j)
        k = chunk_of(j)
        arrived(k, 3, slots // 2)
        col_tile(
            lambda c: q2_all[k * PER + c],
            lambda c: kv_all[:, k * PER + c].reshape(keys, 2 * HD),
            bias, mixed, lax.rem(j, 2), rows, keys, between,
        )
        for _ in between:
            pass

    def col_step(j, carry):
        attend(j, feed(j - 1))
        pass_on(j - 1)
        return carry

    set_bias(bias, starts_ref, my_row * rows, rows)
    attend(0, iter(()))
    for copy in late[4:]:
        copy.wait()
    lax.fori_loop(1, chunks, col_step, 0)
    for _ in feed(chunks - 1):
        pass
    pass_on(chunks - 1)

    for d in range(1, col_count):
        @pl.when(my_col + d < col_count)
        def _():
            hist_copy(d, my_col).wait_send()

    def finish(k, carry):
        kv_copy(k, 0, 7 + slots // 2, 0, sib).wait_send()
        for copy in out_copies(k):
            copy.wait()

        @pl.when(there(-1, 0))
        def _():
            edge_copy(0, k, -1).wait_send()
            edge_copy(1, k, -1).wait_recv()

        @pl.when(there(1, 0))
        def _():
            edge_copy(1, k, 1).wait_send()
            edge_copy(0, k, 1).wait_recv()

        return carry

    lax.fori_loop(0, chunks, finish, 0)
    for which, dc in ((0, -1), (1, 1)):
        @pl.when(there(0, dc))
        def _():
            side_copy(which, dc).wait_send()
            side_copy(1 - which, dc).wait_recv()
    for i, (dr, dc) in enumerate(CORNERS):
        @pl.when(there(dr, dc))
        def _():
            corner_copy(i, dr, dc).wait_send()
            corner_copy(len(CORNERS) - 1 - i, dr, dc).wait_recv()


def full(shape):
    return pl.BlockSpec(shape, lambda *_: (0,) * len(shape))


def front_call(codes, starts, embed, g1, wqkv, g2, wcol, g3, wro, wco, win, wout, wp):
    vocab, width = embed.shape
    rows, cols = codes.shape
    ch = wp.shape[1]
    row_count, col_count = lax.axis_size("row"), lax.axis_size("col")
    tokens = rows * cols
    tile = rows * PER
    chunks = cols // PER
    halo = 2 * cols + 2 * rows + 4 * PER
    dma = pltpu.SemaphoreType.DMA
    early = (codes, starts, g1, g2, g3)
    late = (embed, wqkv, wcol, wro, wco, win, wout, wp)
    anywhere, vmem = pl.BlockSpec(memory_space=pl.ANY), pl.BlockSpec(memory_space=pltpu.VMEM)
    return pl.pallas_call(
        functools.partial(front_kernel, row_count, col_count),
        in_specs=[vmem] * len(early) + [anywhere] * len(late),
        out_specs=[anywhere, anywhere, vmem],
        out_shape=[
            jax.ShapeDtypeStruct((rows, cols, width), F32),
            jax.ShapeDtypeStruct((tokens, ch), F32),
            jax.ShapeDtypeStruct((halo, ch), F32),
        ],
        scratch_shapes=[pltpu.VMEM(x.shape, x.dtype) for x in late]
        + [
            pltpu.VMEM((vocab, width), BF16),
            pltpu.VMEM((HEADS, vocab, 128), BF16),
            pltpu.VMEM((HEADS, vocab, 128), BF16),
            pltpu.VMEM((rows, vocab), F32),
            pltpu.VMEM((tile, tile), BF16),
            pltpu.VMEM((row_count * rows, 128), BF16),
            pltpu.VMEM((2, tile, width), BF16),
            pltpu.VMEM((row_count, cols, rows, 2 * HD), BF16),
            pltpu.VMEM((cols, rows, 2 * width), BF16),
            pltpu.VMEM((chunks, rows, PER, width), F32),
            pltpu.VMEM((tokens, ch), F32),
            pltpu.VMEM((col_count, rows, vocab), BF16),
            pltpu.VMEM((2, cols, ch), F32),
            dma((len(late),)),
            dma((chunks,)),
            dma((4, chunks)),
            dma((col_count,)),
            dma((col_count,)),
            dma((2 * chunks + 6,)),
            dma((2 * chunks + 6,)),
            dma((chunks,)),
            dma((chunks,)),
        ],
        compiler_params=pltpu.CompilerParams(
            vmem_limit_bytes=VMEM_LIMIT, collective_id=0, has_side_effects=True
        ),
        name="front",
    )(*early, *late)


def back_kernel(bo_in, co_ref, halo_ref, k1_ref, k2_ref, bo_ref, img_ref, ext, w1, w2, cat, fine, hold, in_sem, out_sem):
    k = pl.program_id(0)
    erows, ring, ch = ext.shape
    rows = erows - 2
    pairs = erows - 1
    cols = img_ref.shape[1] // 2
    fine_step = img_ref.shape[0]
    my_row, my_col = lax.axis_index("row"), lax.axis_index("col")
    at_top, at_bottom = my_row == 0, my_row == lax.axis_size("row") - 1
    at_left, at_right = my_col == 0, my_col == lax.axis_size("col") - 1
    per = rows // in_sem.shape[0]

    def taken(i):
        part = pl.ds(i * per, per)
        return pltpu.make_async_copy(bo_in.at[part], hold.at[part], in_sem.at[i])

    def given(i):
        part = pl.ds(i * per, per)
        return pltpu.make_async_copy(hold.at[part], bo_ref.at[part], out_sem.at[i])

    @pl.when(k == 0)
    def _():
        for i in range(in_sem.shape[0]):
            taken(i).start()
        ext[...] = jnp.zeros_like(ext)
        for c in range(0, cols, PER):
            part = co_ref[c * rows : (c + PER) * rows].reshape(PER, rows, ch)
            ext[1 : rows + 1, c : c + PER, :] = jnp.swapaxes(part, 0, 1)
        coarse = halo_ref[...]
        zero = jnp.float32(0.0)
        ext[0, 0:cols] = jnp.where(at_top, zero, coarse[0:cols])
        ext[rows + 1, 0:cols] = jnp.where(at_bottom, zero, coarse[cols : 2 * cols])
        left = coarse[2 * cols : 2 * cols + rows]
        right = coarse[2 * cols + rows : 2 * cols + 2 * rows]
        ext[1 : rows + 1, ring - 1 : ring, :] = jnp.where(at_left, zero, left).reshape(rows, 1, ch)
        ext[1 : rows + 1, cols : cols + 1, :] = jnp.where(at_right, zero, right).reshape(rows, 1, ch)
        for i, (dr, dc) in enumerate(CORNERS):
            at = 2 * cols + 2 * rows + i * PER + (PER - 1 if dc < 0 else 0)
            outside = (at_top if dr < 0 else at_bottom) | (at_left if dc < 0 else at_right)
            to_row = 0 if dr < 0 else rows + 1
            to_col = ring - 1 if dc < 0 else cols
            ext[to_row, to_col : to_col + 1, :] = jnp.where(outside, zero, coarse[at : at + 1])
        taps = [[k1_ref[y, x].astype(F32) for x in range(3)] for y in range(3)]
        none = jnp.zeros((ch, ch), F32)
        by_half = (
            ([taps[0][x] + taps[1][x] for x in range(3)], taps[2]),
            (taps[0], [taps[1][x] + taps[2][x] for x in range(3)]),
        )
        for half in range(2):
            for dy in range(2):
                t = by_half[half][dy]
                for b in range(2):
                    three = (t[0], t[1] + t[2], none) if b == 0 else (none, t[0] + t[1], t[2])
                    for dx in range(3):
                        w1[
                            (dy * 3 + dx) * ch : (dy * 3 + dx + 1) * ch,
                            (half * 2 + b) * ch : (half * 2 + b + 1) * ch,
                        ] = three[dx].astype(BF16)
        for dy in range(3):
            for s in range(4):
                for b in range(2):
                    w2[(dy * 4 + s) * ch : (dy * 4 + s + 1) * ch, b * ch : (b + 1) * ch] = (
                        k2_ref[dy, s - b] if 0 <= s - b <= 2 else none.astype(BF16)
                    )

        def widen(e, carry):
            x = ext[e]
            cat[e] = jnp.concatenate(
                [pltpu.roll(x, 1, 0), x, pltpu.roll(x, ring - 1, 0)], axis=1
            ).astype(BF16)
            return carry

        lax.fori_loop(0, erows, widen, 0)
        place = lax.broadcasted_iota(jnp.int32, (ring, 128), 0)
        col_keep = jnp.where(
            ((place == ring - 1) & at_left) | ((place == cols) & at_right), 0.0, 1.0
        )
        group = 11

        def first_sums(e0):
            left = jnp.concatenate(
                [
                    jnp.concatenate([cat[e0 + i], cat[e0 + i + 1]], axis=1)
                    for i in range(group)
                ],
                axis=0,
            )
            return dot(left, w1[...])

        def first_keep(e0, sums):
            y = silu(sums)
            for i in range(group):
                for half in range(2):
                    f = 2 * (e0 + i) + half
                    outside = ((f == 0) & at_top) | ((f == 2 * pairs - 1) & at_bottom)
                    keep = jnp.where(outside, 0.0, 1.0) * col_keep
                    f0 = y[i * ring : (i + 1) * ring, (2 * half) * ch : (2 * half + 1) * ch] * keep
                    f1 = y[i * ring : (i + 1) * ring, (2 * half + 1) * ch : (2 * half + 2) * ch] * keep
                    fine[f] = jnp.concatenate(
                        [pltpu.roll(f1, 1, 0), f0, f1, pltpu.roll(f0, ring - 1, 0)], axis=1
                    ).astype(BF16)

        nxt = first_sums(0)
        for e0 in range(0, pairs, group):
            sums = nxt
            if e0 + group < pairs:
                nxt = first_sums(e0 + group)
            first_keep(e0, sums)

    if True:
        m = k
        y0 = m * fine_step
        left = jnp.concatenate(
            [
                jnp.concatenate([fine[y0 + i + dy, 0:cols] for dy in range(3)], axis=1)
                for i in range(fine_step)
            ],
            axis=0,
        )
        second = dot(left, w2[...])
        for i in range(fine_step):
            up = ext[m * (fine_step // 2) + i // 2 + 1, 0:cols]
            for b in range(2):
                img_ref[i, pl.ds(b, cols, stride=2), :] = (
                    second[i * cols : (i + 1) * cols, b * ch : (b + 1) * ch] + up
                )
    taken(k).wait()
    given(k).start()

    @pl.when(k == pl.num_programs(0) - 1)
    def _():
        for i in range(in_sem.shape[0]):
            given(i).wait()


def back_call(block_out, coarse, halo, k1, k2):
    rows, cols, _ = block_out.shape
    ch = coarse.shape[1]
    ring = cols + 16
    fine_step = 16
    anywhere = pl.BlockSpec(memory_space=pl.ANY)
    return pl.pallas_call(
        back_kernel,
        grid=(2 * rows // fine_step,),
        in_specs=[anywhere] + [full(x.shape) for x in (coarse, halo, k1, k2)],
        out_specs=[anywhere, pl.BlockSpec((fine_step, 2 * cols, ch), lambda i: (i, 0, 0))],
        out_shape=[
            jax.ShapeDtypeStruct(block_out.shape, F32),
            jax.ShapeDtypeStruct((2 * rows, 2 * cols, ch), F32),
        ],
        scratch_shapes=[
            pltpu.VMEM((rows + 2, ring, ch), F32),
            pltpu.VMEM((6 * ch, 4 * ch), BF16),
            pltpu.VMEM((12 * ch, 2 * ch), BF16),
            pltpu.VMEM((rows + 2, ring, 3 * ch), BF16),
            pltpu.VMEM((2 * rows + 2, ring, 4 * ch), BF16),
            pltpu.VMEM(block_out.shape, F32),
            pltpu.SemaphoreType.DMA((2 * rows // fine_step,)),
            pltpu.SemaphoreType.DMA((2 * rows // fine_step,)),
        ],
        compiler_params=pltpu.CompilerParams(vmem_limit_bytes=VMEM_LIMIT),
        name="back",
    )(block_out, coarse, halo, k1, k2)


def per_device(
    codes, starts, embed, gain_one, row_qkv, row_out, gain_two, col_qkv, col_out,
    gain_three, mlp_in, mlp_out, project, conv_one, conv_two,
):
    block_out, coarse, halo = front_call(
        codes, starts[None], embed, gain_one[None], row_qkv, gain_two[None], col_qkv,
        gain_three[None], row_out, col_out, mlp_in, mlp_out, project,
    )
    return tuple(back_call(block_out, coarse, halo, conv_one, conv_two))


def solution(mesh):
    in_specs = (P("row", "col"),) + (P(),) * 14
    out_specs = (P("row", "col", None), P("row", "col", None))
    return jax.shard_map(
        per_device, mesh=mesh, in_specs=in_specs, out_specs=out_specs, check_vma=False
    )
```
